32 devices in a mesh: band: 16 (over z, x, core), batch: 2 (over y).
Axes of the slice: x: 2, y: 2, z: 4, core: 2. Of those that a mesh axis runs over, the one named last changes fastest.
Arguments:
- incoming_rows: bfloat16 [2, 16384, 512], P('batch', 'band'), may hold values from -6 to 6
- picture_label: int32 [2, 16384], P('batch', 'band'), may hold values from -1 to 12, as said below
- triple_kernel: float32 [512, 1536], P(('band', 'batch')), may hold values from -0.25 to 0.25
- mixer_kernel: float32 [512, 512], P(('band', 'batch')), may hold values from -2 to 2
- widening_kernel: float32 [512, 2048], P(('band', 'batch')), may hold values from -0.25 to 0.25
- narrowing_kernel: float32 [2048, 512], P(('band', 'batch')), may hold values from -0.125 to 0.125
- asker_offset: float32 [512], P(('band', 'batch')), may hold values from -3 to 3
- content_offset: float32 [512], P(('band', 'batch')), may hold values from -3 to 3
- mixer_offset_vector: float32 [512], P(('band', 'batch')), may hold values from -3 to 3
- widening_offset: float32 [2048], P(('band', 'batch')), may hold values from -3 to 3
- narrowing_offset: float32 [512], P(('band', 'batch')), may hold values from -3 to 3
- leading_gain: float32 [512], P(('band', 'batch')), may hold values from 0.5 to 2
- leading_offset: float32 [512], P(('band', 'batch')), may hold values from -2 to 2
- second_gain: float32 [512], P(('band', 'batch')), may hold values from 0.5 to 2
- second_offset: float32 [512], P(('band', 'batch')), may hold values from -2 to 2
- loss_sensitivity: bfloat16 [2, 16384, 512], P('batch', 'band'), may hold values from -6 to 6
Outputs:
- layer_out: bfloat16 [2, 16384, 512], P('batch', 'band')
- input_grad: bfloat16 [2, 16384, 512], P('batch', 'band')
- qkv_grad: float32 [512, 1536], P(('band', 'batch'))
- proj_grad: float32 [512, 512], P(('band', 'batch'))
- expand_grad: float32 [512, 2048], P(('band', 'batch'))
- reduce_grad: float32 [2048, 512], P(('band', 'batch'))
- query_grad: float32 [512], P(('band', 'batch'))
- value_grad: float32 [512], P(('band', 'batch'))
- attn_grad: float32 [512], P(('band', 'batch'))
- hidden_grad: float32 [2048], P(('band', 'batch'))
- mlp_grad: float32 [512], P(('band', 'batch'))
- prescale_grad: float32 [512], P(('band', 'batch'))
- preshift_grad: float32 [512], P(('band', 'batch'))
- midscale_grad: float32 [512], P(('band', 'batch'))
- midshift_grad: float32 [512], P(('band', 'batch'))
The draws below stay inside these ranges and needn't reach their ends.
Inputs may be any that keep to these rules, and one draw needn't show every extreme that they name: `picture_label`: in every group the first 256 rows of each band of 1024 rows belong to image 0; the rest of a band holds its thumbnails numbered 1, 2, ... in order, 64 rows each, then padding rows marked -1. Thumbnail numbers count within a band only. Every group has a band filled with thumbnails and a band with a single thumbnail.
All inputs are finite; a program needn't handle non-finite values.
Results may differ from the reference program's by a relative error of at most 0.018.
Values may be sent and summed in bfloat16 or wider, within the bound.
No kernel may reach another device: no remote copies, remote signals or barrier semaphores. Data moves between devices by JAX's collectives and lax.ppermute only.
A program may use at most 256 MiB of HBM per device.

```python
import math
import jax
import jax.numpy as jnp
from jax import lax

EMBED_DIMENSION = 512
HEADS = 8
HEAD = 64
FF = 2048
TOK_DEV = 1024
THUMB = 64
LONG_DEV = 256
GROUPS = 2
TOKENS_G = 16384
N_BAND = 16


def draw_picture_label(key, part):
    key = jax.random.fold_in(key, 7)
    largest = (TOK_DEV - LONG_DEV) // THUMB
    count_key, band_key = jax.random.split(key)
    counts = jax.random.randint(count_key, (GROUPS, N_BAND), 1, largest + 1)
    full_band = jax.random.randint(band_key, (GROUPS, 1), 0, N_BAND)
    band_index = jnp.arange(N_BAND)[None, :]
    counts = jnp.where(band_index == full_band, largest, counts)
    counts = jnp.where(band_index == (full_band + 1) % N_BAND, 1, counts)
    row_index = jnp.arange(TOK_DEV)[None, None, :]
    slot_number = (row_index - LONG_DEV) // THUMB + 1
    thumbs = jnp.where(slot_number <= counts[:, :, None], slot_number, -1)
    segment_ids = jnp.where(row_index < LONG_DEV, 0, thumbs)
    return segment_ids.reshape(GROUPS, N_BAND * TOK_DEV).astype(jnp.int32)


def shard_levels(rng, dims, cuts, low, high):
    def one(dim, parts):
        draws = jax.random.uniform(jax.random.fold_in(jax.random.fold_in(rng, 6), dim), (parts,), jnp.float32, low / len(cuts), high / len(cuts))
        return jnp.repeat(jnp.exp(draws), dims[dim] // parts).reshape((-1,) + (1,) * (len(dims) - dim - 1))

    loudness = one(*cuts[0])
    for cut in cuts[1:]:
        loudness = loudness * one(*cut)
    return loudness


def bell_draw(own_key, dims, deviation, bound, cuts=(), kind=jnp.bfloat16):
    loudness = shard_levels(own_key, dims, cuts, -0.22, 0.18) if cuts else 1.0
    drawn = jax.random.normal(own_key, dims, jnp.float32) * deviation * loudness
    return jnp.minimum(jnp.maximum(drawn, -bound), bound).astype(kind)


def setup_inputs(seed: int = 0) -> dict:
    key_list = jax.random.split(jax.random.key(seed), 17)
    incoming_rows = bell_draw(key_list[0], (GROUPS, TOKENS_G, EMBED_DIMENSION), 1.0, 6.0, ((0, 2), (1, 16)))
    picture_label = draw_picture_label(jax.random.fold_in(key_list[16], 71), 0)
    triple_kernel = bell_draw(key_list[2], (EMBED_DIMENSION, 3 * EMBED_DIMENSION), EMBED_DIMENSION ** -0.5, 0.25, ((0, 32),), jnp.float32)
    mixer_kernel = bell_draw(key_list[3], (EMBED_DIMENSION, EMBED_DIMENSION), (EMBED_DIMENSION // 64) ** -0.5, 2.0, ((0, 32),), jnp.float32)
    widening_kernel = bell_draw(key_list[4], (EMBED_DIMENSION, FF), EMBED_DIMENSION ** -0.5, 0.25, ((0, 32),), jnp.float32)
    narrowing_kernel = bell_draw(key_list[5], (FF, EMBED_DIMENSION), FF ** -0.5, 0.125, ((0, 32),), jnp.float32)
    asker_offset = bell_draw(key_list[6], (EMBED_DIMENSION,), 0.5, 3.0, ((0, 32),), jnp.float32)
    content_offset = bell_draw(key_list[7], (EMBED_DIMENSION,), 0.5, 3.0, ((0, 32),), jnp.float32)
    mixer_offset_vector = bell_draw(key_list[8], (EMBED_DIMENSION,), 0.5, 3.0, ((0, 32),), jnp.float32)
    widening_offset = bell_draw(key_list[9], (FF,), 0.5, 3.0, ((0, 32),), jnp.float32)
    narrowing_offset = bell_draw(key_list[10], (EMBED_DIMENSION,), 0.5, 3.0, ((0, 32),), jnp.float32)
    leading_gain = jnp.clip(jnp.exp(math.log(2.0) - 1.3862944 * jax.random.uniform(key_list[11], (EMBED_DIMENSION,), jnp.float32) ** shard_levels(key_list[11], (EMBED_DIMENSION,), ((0, 32),), -0.2, 0.2)), 0.5, 2.0)
    leading_offset = bell_draw(key_list[12], (EMBED_DIMENSION,), 0.3, 2.0, ((0, 32),), jnp.float32)
    second_gain = jnp.clip(jnp.exp(math.log(2.0) - 1.3862944 * jax.random.uniform(key_list[13], (EMBED_DIMENSION,), jnp.float32) ** shard_levels(key_list[13], (EMBED_DIMENSION,), ((0, 32),), -0.2, 0.2)), 0.5, 2.0)
    second_offset = bell_draw(key_list[14], (EMBED_DIMENSION,), 0.3, 2.0, ((0, 32),), jnp.float32)
    loss_sensitivity = bell_draw(key_list[15], (GROUPS, TOKENS_G, EMBED_DIMENSION), 1.0, 6.0, ((0, 2), (1, 16)))
    return {"incoming_rows": incoming_rows, "picture_label": picture_label, "triple_kernel": triple_kernel, "mixer_kernel": mixer_kernel, "widening_kernel": widening_kernel, "narrowing_kernel": narrowing_kernel, "asker_offset": asker_offset, "content_offset": content_offset, "mixer_offset_vector": mixer_offset_vector, "widening_offset": widening_offset, "narrowing_offset": narrowing_offset, "leading_gain": leading_gain, "leading_offset": leading_offset, "second_gain": second_gain, "second_offset": second_offset, "loss_sensitivity": loss_sensitivity}


@jax.custom_vjp
def low(v):
    return lax.optimization_barrier(v.astype(jnp.bfloat16)).astype(jnp.float32)

@jax.custom_vjp
def low_back(v):
    return v

def low_keep(v):
    return (low(v), None)

def low_pass(kept, grad):
    return (grad,)

def back_keep(v):
    return (v, None)

def back_low(kept, grad):
    return (low(grad),)
low.defvjp(low_keep, low_pass)
low_back.defvjp(back_keep, back_low)
epsilon = 1e-06
gelu_scale = 0.7978845608028654

def matmul(left, right):
    return jnp.dot(left, right, precision=lax.Precision.HIGHEST, preferred_element_type=jnp.float32)

def gelu_tanh(value):
    inner = gelu_scale * (value + 0.044715 * value * value * value)
    return 0.5 * value * (1.0 + jnp.tanh(inner))

def normalize(matrix, scaling, offset):
    center = matrix - lax.optimization_barrier(jnp.mean(matrix, axis=1, keepdims=True))
    spread = lax.optimization_barrier(jnp.mean(center * center, axis=1, keepdims=True))
    return center * lax.rsqrt(spread + epsilon) * scaling + offset

def attend(queries, key_heads, value_heads, allowed):
    score_scale = 1.0 / math.sqrt(HEAD)
    scores = jnp.einsum('qhd,khd->hqk', queries, key_heads, precision=lax.Precision.HIGHEST) * score_scale
    scores = jnp.where(allowed, low_back(scores), -1e+30)
    weights = jnp.exp(scores - jax.nn.logsumexp(scores, axis=2, keepdims=True))
    return jnp.einsum('hqk,khd->qhd', low(weights), value_heads, precision=lax.Precision.HIGHEST)

def encoder_layer(token_rows, primary_replicas, live_mask, segment_ids):
    qkv_low, proj_low, expand_low, reduce_low, query_shift, value_shift, attn_shift, hidden_shift, mlp_shift, gain_one, offset_one, gain_two, offset_two = [low(master) for master in primary_replicas]
    normed = low(normalize(token_rows, gain_one, offset_one))
    projected = matmul(normed, qkv_low)
    queries = low_back(low(projected[:, :EMBED_DIMENSION] + query_shift))
    key_rows = low_back(low(projected[:, EMBED_DIMENSION:2 * EMBED_DIMENSION]))
    value_rows = low_back(low(projected[:, 2 * EMBED_DIMENSION:] + value_shift))
    query_bands = queries.reshape(N_BAND, TOK_DEV, HEADS, HEAD)
    key_bands = key_rows.reshape(N_BAND, TOK_DEV, HEADS, HEAD)
    value_bands = value_rows.reshape(N_BAND, TOK_DEV, HEADS, HEAD)
    long_keys = key_bands[:, :LONG_DEV].reshape(N_BAND * LONG_DEV, HEADS, HEAD)
    long_values = value_bands[:, :LONG_DEV].reshape(N_BAND * LONG_DEV, HEADS, HEAD)

    def long_block(query_block):
        return attend(query_block, long_keys, long_values, True)
    long_mixed = lax.map(jax.checkpoint(long_block), query_bands[:, :LONG_DEV])
    short_ids = segment_ids.reshape(N_BAND, TOK_DEV)[:, LONG_DEV:]

    def short_block(pieces):
        query_block, key_block, value_block, block_ids = pieces
        allowed = block_ids[:, None] == block_ids[None, :]
        return attend(query_block, key_block, value_block, allowed[None])
    short_mixed = lax.map(jax.checkpoint(short_block), (query_bands[:, LONG_DEV:], key_bands[:, LONG_DEV:], value_bands[:, LONG_DEV:], short_ids))
    attended = jnp.concatenate([long_mixed, short_mixed], axis=1).reshape(N_BAND * TOK_DEV, EMBED_DIMENSION)
    attended = low_back(low(attended))
    branch_one = low_back(matmul(attended, proj_low) + attn_shift)
    middle = token_rows + live_mask * branch_one
    normed_two = low(normalize(middle, gain_two, offset_two))
    hidden = low_back(matmul(normed_two, expand_low) + hidden_shift)
    active = low(gelu_tanh(hidden))
    branch_two = low_back(matmul(active, reduce_low) + mlp_shift)
    return middle + live_mask * branch_two

def reference(incoming_rows, picture_label, triple_kernel, mixer_kernel, widening_kernel, narrowing_kernel, asker_offset, content_offset, mixer_offset_vector, widening_offset, narrowing_offset, leading_gain, leading_offset, second_gain, second_offset, loss_sensitivity):
    primary_replicas = (triple_kernel, mixer_kernel, widening_kernel, narrowing_kernel, asker_offset, content_offset, mixer_offset_vector, widening_offset, narrowing_offset, leading_gain, leading_offset, second_gain, second_offset)

    def one_group(totals, group_data):
        group_rows, group_ids, group_cotangent = group_data
        live_mask = (group_ids >= 0).astype(jnp.float32)[:, None]

        def forward(rows_in, params_in):
            return encoder_layer(rows_in, params_in, live_mask, group_ids)
        result, pullback = jax.vjp(forward, group_rows.astype(jnp.float32), primary_replicas)
        row_grad, param_grads = pullback(group_cotangent.astype(jnp.float32))
        totals = tuple((running + fresh_grad for running, fresh_grad in zip(totals, param_grads)))
        return (totals, (result.astype(jnp.bfloat16), row_grad.astype(jnp.bfloat16)))
    initial = tuple((jnp.zeros(master.shape, jnp.float32) for master in primary_replicas))
    totals, outputs = lax.scan(one_group, initial, (incoming_rows, picture_label, loss_sensitivity))
    return (outputs[0], outputs[1], totals[0], totals[1], totals[2], totals[3], totals[4], totals[5], totals[6], totals[7], totals[8], totals[9], totals[10], totals[11], totals[12])
```

```python
import functools
import math

import jax
import jax.numpy as jnp
from jax import lax
from jax.experimental import pallas as pl
from jax.experimental.pallas import tpu as pltpu
from jax.sharding import PartitionSpec as P

HEADS = 8
HEAD = 64
LONG = 256
WIDTH = 512
FF = 2048
GROUP = 256
TILE = 512
epsilon = 1e-06
gelu_scale = 0.7978845608028654
f32 = jnp.float32
bf16 = jnp.bfloat16
PARAMS = dict(vmem_limit_bytes=58 << 20)


def dot(left, right, cl=1, cr=0):
    return lax.dot_general(left, right, (((cl,), (cr,)), ((), ())), preferred_element_type=f32)


def standardize(rows):
    center = rows - jnp.mean(rows, axis=1, keepdims=True)
    inverse = lax.rsqrt(jnp.mean(center * center, axis=1, keepdims=True) + epsilon)
    return center * inverse, inverse


def norm_backward(incoming, standard, inverse, scaling):
    scaled = incoming * scaling
    return inverse * (
        scaled
        - jnp.mean(scaled, axis=1, keepdims=True)
        - standard * jnp.mean(scaled * standard, axis=1, keepdims=True)
    )


def column_sum(rows):
    return jnp.sum(rows, axis=0, keepdims=True)


def head_lanes(block, head):
    lane = lax.broadcasted_iota(jnp.int32, block.shape, 1) // HEAD
    return jnp.where(lane == head, block.astype(f32), 0.0).astype(bf16)


V_ASK, V_CONTENT, V_MIXER, V_NARROW, V_G1, V_O1, V_G2, V_O2 = range(8)


def row_of(table_ref, index):
    return table_ref[index : index + 1, :]


def whole(shape):
    return pl.BlockSpec(shape, lambda *_: (0,) * len(shape))


def once(shape):
    return pl.BlockSpec(shape, lambda *_: (0,) * len(shape), pipeline_mode=pl.Buffered(1))


def short_qkv_kernel(x_ref, w_ref, vec_ref, n1_ref, q_ref, k_ref, v_ref, kt_ref, vt_ref):
    standard, _ = standardize(x_ref[...].astype(f32))
    normed = (standard * row_of(vec_ref, V_G1) + row_of(vec_ref, V_O1)).astype(bf16)
    n1_ref[...] = normed
    projected = dot(normed, w_ref[...])
    q = (projected[:, :WIDTH] + row_of(vec_ref, V_ASK)).astype(bf16)
    q_ref[...] = (q.astype(f32) * (1.0 / math.sqrt(HEAD))).astype(bf16)
    k = projected[:, WIDTH : 2 * WIDTH]
    v = projected[:, 2 * WIDTH :] + row_of(vec_ref, V_CONTENT)
    k_ref[...] = k.astype(bf16)
    v_ref[...] = v.astype(bf16)
    kt_ref[...] = k.T.astype(bf16)
    vt_ref[...] = v.T.astype(bf16)


def short_qkv(rows, weights, vectors):
    count = rows.shape[0] - LONG
    block = 256
    row_spec = pl.BlockSpec((block, WIDTH), lambda i: (i, 0))
    col_spec = pl.BlockSpec((WIDTH, block), lambda i: (0, i))
    flat = jax.ShapeDtypeStruct((count, WIDTH), bf16)
    tall = jax.ShapeDtypeStruct((WIDTH, count), bf16)
    return pl.pallas_call(
        short_qkv_kernel,
        grid=(count // block,),
        in_specs=[
            pl.BlockSpec((block, WIDTH), lambda i: (i + LONG // block, 0)),
            whole((WIDTH, 3 * WIDTH)),
            whole(vectors.shape),
        ],
        out_specs=[row_spec, row_spec, row_spec, row_spec, col_spec, col_spec],
        out_shape=[flat, flat, flat, flat, tall, tall],
        compiler_params=pltpu.CompilerParams(**PARAMS),
        cost_estimate=pl.CostEstimate(
            flops=2 * count * WIDTH * 3 * WIDTH, bytes_accessed=6 << 20, transcendentals=0
        ),
        name="short_qkv",
    )(rows, weights, vectors)


def short_forward_kernel(
    q_ref, k_ref, vt_ref, idc_ref, idr_ref, e_ref, o_ref, linv_ref, att_ref, s_ref, bias_ref, top_ref
):
    step = pl.program_id(0)
    count = k_ref.shape[0]
    tile = 256

    @pl.when(step == 0)
    def _():
        same = idc_ref[...] == idr_ref[...]
        bias_ref[...] = jnp.where(same, 0.0, -1e30)

    def first(slot):
        masked = head_lanes(q_ref[...], lax.rem(step, 4))
        top = None
        for low in range(0, count, tile):
            s = dot(k_ref[low : low + tile, :], masked, 1, 1) + bias_ref[low : low + tile, :]
            s_ref[slot, low : low + tile, :] = s
            part = jnp.max(s, axis=0, keepdims=True)
            top = part if top is None else jnp.maximum(top, part)
        top_ref[slot] = jnp.broadcast_to(top, (8, count))

    def second(slot):
        head = step - 1
        top = top_ref[slot, 0:1, :]
        mixed = jnp.zeros((HEAD, count), f32)
        total = jnp.zeros((1, count), f32)
        for low in range(0, count, tile):
            e = jnp.exp(s_ref[slot, low : low + tile, :] - top)
            total += column_sum(e)
            low_e = e.astype(bf16)
            e_ref[low : low + tile, :] = low_e
            mixed += dot(vt_ref[pl.ds(pl.multiple_of(head * HEAD, HEAD), HEAD), low : low + tile], low_e)
        linv = 1.0 / total
        linv_ref[...] = jnp.broadcast_to(linv, (8, count))
        o_ref[pl.ds(pl.multiple_of(head * HEAD, HEAD), HEAD), :] = mixed * linv

    last = pl.num_programs(0) - 1

    @pl.when(step == 0)
    def _():
        first(0)

    for parity in (0, 1):
        @pl.when((step > 0) & (step < last) & (lax.rem(step, 2) == parity))
        def _():
            first(parity)
            second(1 - parity)

    @pl.when(step == last)
    def _():
        second((HEADS - 1) % 2)
        for low in range(0, WIDTH, 128):
            att_ref[:, low : low + 128] = o_ref[low : low + 128, :].T.astype(bf16)


def short_forward(q, k, vt, ids):
    count = q.shape[0]
    now = lambda s: (0, jnp.minimum(s, HEADS - 1) // 4)
    before = lambda s: (0, jnp.maximum(s - 1, 0))
    return pl.pallas_call(
        short_forward_kernel,
        grid=(HEADS + 1,),
        in_specs=[
            pl.BlockSpec((count, GROUP), now),
            pl.BlockSpec((count, GROUP), now),
            whole((WIDTH, count)),
            whole((count, 1)),
            whole((1, count)),
        ],
        out_specs=[
            pl.BlockSpec((count, count), before),
            whole((WIDTH, count)),
            pl.BlockSpec((8, count), lambda s: (jnp.maximum(s - 1, 0), 0)),
            whole((count, WIDTH)),
        ],
        out_shape=[
            jax.ShapeDtypeStruct((count, HEADS * count), bf16),
            jax.ShapeDtypeStruct((WIDTH, count), f32),
            jax.ShapeDtypeStruct((HEADS * 8, count), f32),
            jax.ShapeDtypeStruct((count, WIDTH), bf16),
        ],
        scratch_shapes=[
            pltpu.VMEM((2, count, count), f32),
            pltpu.VMEM((count, count), f32),
            pltpu.VMEM((2, 8, count), f32),
        ],
        compiler_params=pltpu.CompilerParams(**PARAMS),
        cost_estimate=pl.CostEstimate(
            flops=12 * count * count * WIDTH, bytes_accessed=12 << 20, transcendentals=HEADS * count * count
        ),
        name="short_forward",
    )(q, k, vt, ids[:, None], ids[None, :])


def long_prepare_kernel(place_ref, x_ref, w_ref, vec_ref, q_ref, k_ref, v_ref, kt_ref, vt_ref):
    step = pl.program_id(0)
    core = place_ref[1]
    lanes = lambda base: pl.ds(pl.multiple_of(base + core * GROUP, GROUP), GROUP)
    standard, _ = standardize(x_ref[...].astype(f32))
    normed = (standard * row_of(vec_ref, V_G1) + row_of(vec_ref, V_O1)).astype(bf16)
    k = dot(normed, w_ref[:, lanes(WIDTH)])
    v = dot(normed, w_ref[:, lanes(2 * WIDTH)]) + vec_ref[V_CONTENT : V_CONTENT + 1, lanes(0)]
    k_ref[...] = k.astype(bf16)
    v_ref[...] = v.astype(bf16)
    kt_ref[...] = k.T.astype(bf16)
    vt_ref[...] = v.T.astype(bf16)

    @pl.when(step == place_ref[0])
    def _():
        q = (dot(normed, w_ref[:, lanes(0)]) + vec_ref[V_ASK : V_ASK + 1, lanes(0)]).astype(bf16)
        q_ref[...] = (q.astype(f32) * (1.0 / math.sqrt(HEAD))).astype(bf16)


def long_prepare(place, rows, weights, vectors):
    total = rows.shape[0]
    row_spec = pl.BlockSpec((TILE, GROUP), lambda i, _: (i, 0))
    col_spec = pl.BlockSpec((GROUP, TILE), lambda i, _: (0, i))
    flat = jax.ShapeDtypeStruct((total, GROUP), bf16)
    tall = jax.ShapeDtypeStruct((GROUP, total), bf16)
    return pl.pallas_call(
        long_prepare_kernel,
        grid_spec=pltpu.PrefetchScalarGridSpec(
            num_scalar_prefetch=1,
            grid=(total // TILE,),
            in_specs=[
                pl.BlockSpec((TILE, WIDTH), lambda i, _: (i, 0)),
                whole((WIDTH, 3 * WIDTH)),
                whole(vectors.shape),
            ],
            out_specs=[whole((TILE, GROUP)), row_spec, row_spec, col_spec, col_spec],
        ),
        out_shape=[jax.ShapeDtypeStruct((TILE, GROUP), bf16), flat, flat, tall, tall],
        compiler_params=pltpu.CompilerParams(**PARAMS),
        cost_estimate=pl.CostEstimate(
            flops=4 * total * WIDTH * GROUP, bytes_accessed=14 << 20, transcendentals=0
        ),
        name="long_prepare",
    )(place, rows, weights, vectors)


CHUNK = 256
PARTS = TILE // CHUNK
LOCAL_HEADS = GROUP // HEAD
STEPS = LOCAL_HEADS * PARTS


def long_forward_kernel(q_ref, k_ref, vt_ref, e_ref, o_ref, linv_ref, att_ref, s_ref, top_ref):
    step = pl.program_id(0)
    total = k_ref.shape[0]
    tile = 512
    last = pl.num_programs(0) - 1

    def masked_queries():
        rows = pl.ds(pl.multiple_of(lax.rem(step, PARTS) * CHUNK, CHUNK), CHUNK)
        return head_lanes(q_ref[rows, :], step // PARTS)

    def first_tile(slot, low, masked, top):
        s = dot(k_ref[pl.ds(low, tile), :], masked, 1, 1)
        s_ref[slot, pl.ds(low, tile), :] = s
        return jnp.maximum(top, jnp.max(s.reshape(tile // 8, 8, CHUNK), axis=0))

    def second_tile(slot, low, top, head, carry):
        summed, mixed = carry
        e = jnp.exp(s_ref[slot, pl.ds(low, tile), :] - top)
        summed = summed + jnp.sum(e.reshape(tile // 8, 8, CHUNK), axis=0)
        low_e = e.astype(bf16)
        e_ref[pl.ds(low, tile), :] = low_e
        values = vt_ref[pl.ds(pl.multiple_of(head * HEAD, HEAD), HEAD), pl.ds(low, tile)]
        return summed, mixed + dot(values, low_e)

    start_top = jnp.full((8, CHUNK), -1e30, f32)
    start_sum = (jnp.zeros((8, CHUNK), f32), jnp.zeros((HEAD, CHUNK), f32))

    def finish(head, part, carry):
        summed, mixed = carry
        linv = 1.0 / column_sum(summed)
        linv_ref[...] = jnp.broadcast_to(linv, (8, CHUNK))
        o_ref[part, pl.ds(pl.multiple_of(head * HEAD, HEAD), HEAD), :] = mixed * linv

    def place(turn):
        return pl.multiple_of(turn * tile, tile)

    @pl.when(step == 0)
    def _():
        masked = masked_queries()
        top_ref[0] = lax.fori_loop(
            0, total // tile, lambda t, top: first_tile(0, place(t), masked, top), start_top
        )

    for parity in (0, 1):
        @pl.when((step > 0) & (step < last) & (lax.rem(step, 2) == parity))
        def _():
            masked = masked_queries()
            before = step - 1
            head = before // PARTS
            top_row = jnp.max(top_ref[1 - parity], axis=0, keepdims=True)

            def body(turn, carry):
                top, kept = carry
                low = place(turn)
                top = first_tile(parity, low, masked, top)
                kept = second_tile(1 - parity, low, top_row, head, kept)
                return top, kept

            top, kept = lax.fori_loop(0, total // tile, body, (start_top, start_sum))
            top_ref[parity] = top
            finish(head, lax.rem(before, PARTS), kept)

    @pl.when(step == last)
    def _():
        slot = (STEPS - 1) % 2
        top_row = jnp.max(top_ref[slot], axis=0, keepdims=True)
        head = LOCAL_HEADS - 1
        kept = lax.fori_loop(
            0,
            total // tile,
            lambda t, carry: second_tile(slot, place(t), top_row, head, carry),
            start_sum,
        )
        finish(head, PARTS - 1, kept)
        for part in range(PARTS):
            att_ref[part * CHUNK : (part + 1) * CHUNK, :] = o_ref[part].T.astype(bf16)


def long_forward(q, k, vt):
    total = k.shape[0]
    before = lambda s: jnp.maximum(s - 1, 0)
    return pl.pallas_call(
        long_forward_kernel,
        grid=(STEPS + 1,),
        in_specs=[once((TILE, GROUP)), once((total, GROUP)), once((GROUP, total))],
        out_specs=[
            pl.BlockSpec((total, CHUNK), lambda s: (0, before(s))),
            whole((PARTS, GROUP, CHUNK)),
            pl.BlockSpec((8, CHUNK), lambda s: (before(s), 0)),
            whole((TILE, GROUP)),
        ],
        out_shape=[
            jax.ShapeDtypeStruct((total, STEPS * CHUNK), bf16),
            jax.ShapeDtypeStruct((PARTS, GROUP, CHUNK), f32),
            jax.ShapeDtypeStruct((STEPS * 8, CHUNK), f32),
            jax.ShapeDtypeStruct((TILE, GROUP), bf16),
        ],
        scratch_shapes=[pltpu.VMEM((2, total, CHUNK), f32), pltpu.VMEM((2, 8, CHUNK), f32)],
        compiler_params=pltpu.CompilerParams(**PARAMS),
        cost_estimate=pl.CostEstimate(
            flops=16 * TILE * total * GROUP, bytes_accessed=24 << 20, transcendentals=4 * TILE * total
        ),
        name="long_forward",
    )(q, k, vt)


def feed_kernel(
    x_ref, ids_ref, g_ref, att_long_ref, att_short_ref, wp_ref, we_ref, wr_ref, vec_ref, hid_ref,
    out_ref, mid_ref, da_ref, gp_ref, ge_ref, gr_ref, row_ref, hsum_ref, accp, acce, accr,
):
    step = pl.program_id(0)

    @pl.when(step == 0)
    def _():
        accp[...] = jnp.zeros_like(accp)
        acce[...] = jnp.zeros_like(acce)
        accr[...] = jnp.zeros_like(accr)
        row_ref[...] = jnp.zeros_like(row_ref)
        hsum_ref[...] = jnp.zeros_like(hsum_ref)

    x = x_ref[...].astype(f32)
    live = (ids_ref[...] >= 0).astype(f32)
    upstream = g_ref[...].astype(f32)
    attended = jnp.where(step == 0, att_long_ref[...], att_short_ref[...])
    branch = dot(attended, wp_ref[...]) + row_of(vec_ref, V_MIXER)
    middle = x + live * branch
    standard, inverse = standardize(middle)
    gain = row_of(vec_ref, V_G2)
    normed = (standard * gain + row_of(vec_ref, V_O2)).astype(bf16)
    hidden = dot(normed, we_ref[...]) + hid_ref[...]
    square = hidden * hidden
    tangent = jnp.tanh(hidden * (gelu_scale + (gelu_scale * 0.044715) * square))
    half = 0.5 * (1.0 + tangent)
    active = (hidden * half).astype(bf16)
    slope = half + (0.5 * hidden) * (1.0 - tangent * tangent) * (
        gelu_scale + (gelu_scale * 3.0 * 0.044715) * square
    )
    branch_two = dot(active, wr_ref[...]) + row_of(vec_ref, V_NARROW)
    out_ref[...] = (middle + live * branch_two).astype(bf16)
    branch_grad = live * upstream
    branch_low = branch_grad.astype(bf16)
    accr[...] += dot(active, branch_low, 0, 0)
    hidden_grad = dot(branch_low, wr_ref[...], 1, 1) * slope
    hidden_low = hidden_grad.astype(bf16)
    hsum_ref[...] += column_sum(hidden_low.astype(f32))
    acce[...] += dot(normed, hidden_low, 0, 0)
    normed_grad = dot(hidden_low, we_ref[...], 1, 1)
    middle_grad = upstream + norm_backward(normed_grad, standard, inverse, gain)
    mid_ref[...] = middle_grad
    attn_low = (live * middle_grad).astype(bf16)
    accp[...] += dot(attended, attn_low, 0, 0)
    da_ref[...] = dot(attn_low, wp_ref[...], 1, 1).astype(bf16)
    row_ref[0:1, :] += column_sum(attn_low.astype(f32))
    row_ref[1:2, :] += column_sum(branch_low.astype(f32))
    row_ref[2:3, :] += column_sum(normed_grad * standard)
    row_ref[3:4, :] += column_sum(normed_grad)

    @pl.when(step == pl.num_programs(0) - 1)
    def _():
        gp_ref[...] = accp[...].astype(bf16)
        ge_ref[...] = acce[...].astype(bf16)
        gr_ref[...] = accr[...].astype(bf16)


def feed(rows, ids, upstream, att_long, att_short, wp, we, wr, vectors, hidden_shift):
    count = rows.shape[0]
    block = LONG
    row_spec = pl.BlockSpec((block, WIDTH), lambda i: (i, 0))
    return pl.pallas_call(
        feed_kernel,
        grid=(count // block,),
        in_specs=[
            row_spec,
            pl.BlockSpec((block, 1), lambda i: (i, 0)),
            row_spec,
            whole((block, WIDTH)),
            pl.BlockSpec((block, WIDTH), lambda i: (jnp.maximum(i - 1, 0), 0)),
            once((WIDTH, WIDTH)),
            once((WIDTH, FF)),
            once((FF, WIDTH)),
            whole(vectors.shape),
            whole((1, FF)),
        ],
        out_specs=[
            row_spec,
            row_spec,
            row_spec,
            once((WIDTH, WIDTH)),
            once((WIDTH, FF)),
            once((FF, WIDTH)),
            whole((8, WIDTH)),
            whole((1, FF)),
        ],
        out_shape=[
            jax.ShapeDtypeStruct((count, WIDTH), bf16),
            jax.ShapeDtypeStruct((count, WIDTH), f32),
            jax.ShapeDtypeStruct((count, WIDTH), bf16),
            jax.ShapeDtypeStruct((WIDTH, WIDTH), bf16),
            jax.ShapeDtypeStruct((WIDTH, FF), bf16),
            jax.ShapeDtypeStruct((FF, WIDTH), bf16),
            jax.ShapeDtypeStruct((8, WIDTH), f32),
            jax.ShapeDtypeStruct((1, FF), f32),
        ],
        scratch_shapes=[
            pltpu.VMEM((WIDTH, WIDTH), f32),
            pltpu.VMEM((WIDTH, FF), f32),
            pltpu.VMEM((FF, WIDTH), f32),
        ],
        compiler_params=pltpu.CompilerParams(**PARAMS),
        cost_estimate=pl.CostEstimate(
            flops=6 * count * WIDTH * (WIDTH + 2 * FF), bytes_accessed=18 << 20, transcendentals=count * FF
        ),
        name="feed",
    )(rows, ids[:, None], upstream, att_long, att_short, wp, we, wr, vectors, hidden_shift)


def long_backward_kernel(
    place_ref, e_ref, k_ref, v_ref, kt_ref, x_ref, q_ref, da_ref, o_ref, linv_ref, w_ref, vec_ref,
    dx_ref, gq_ref, gkv_ref, row_ref, side_ref,
    qblk, dblk, delta, ds_ref, dq_acc, wq, wkv,
):
    step = pl.program_id(0)
    last = pl.num_programs(0) - 1
    core = place_ref[1]

    @pl.when(step == 0)
    def _():
        lanes = lambda base: pl.ds(pl.multiple_of(base + core * GROUP, GROUP), GROUP)
        wq[...] = w_ref[:, lanes(0)]
        wkv[:, :GROUP] = w_ref[:, lanes(WIDTH)]
        wkv[:, GROUP:] = w_ref[:, lanes(2 * WIDTH)]
        dq_acc[...] = jnp.zeros_like(dq_acc)
        gkv_ref[...] = jnp.zeros_like(gkv_ref)
        row_ref[...] = jnp.zeros_like(row_ref)
        side_ref[...] = jnp.zeros_like(side_ref)
        for part in range(PARTS):
            rows = slice(part * CHUNK, (part + 1) * CHUNK)
            turned = da_ref[rows, :].astype(f32).T
            product = turned * o_ref[part]
            pieces = []
            for head in range(LOCAL_HEADS):
                index = head * PARTS + part
                span = slice(head * HEAD, (head + 1) * HEAD)
                linv = linv_ref[8 * index : 8 * index + 1, :]
                delta[8 * index : 8 * index + 8, :] = jnp.broadcast_to(
                    column_sum(product[span, :]) * linv, (8, CHUNK)
                )
                pieces.append(turned[span, :] * linv)
            scaled = jnp.concatenate(pieces, axis=0).T
            for head in range(LOCAL_HEADS):
                index = head * PARTS + part
                span = slice(index * CHUNK, (index + 1) * CHUNK)
                dblk[span, :] = head_lanes(scaled, head)
                qblk[span, :] = head_lanes(q_ref[rows, :], head)

    for head in range(LOCAL_HEADS):
        for part in range(PARTS):
            index = head * PARTS + part
            span = slice(index * CHUNK, (index + 1) * CHUNK)
            slopes = dot(v_ref[...], dblk[span, :], 1, 1)
            ds = (
                e_ref[:, span].astype(f32) * (slopes - delta[8 * index : 8 * index + 1, :])
            ).astype(bf16)
            ds_ref[:, span] = ds
            own = slice(head * HEAD, (head + 1) * HEAD)
            dq_acc[part, own, :] += dot(kt_ref[own, :], ds)

    value_grad = dot(e_ref[...], dblk[...]).astype(bf16)
    key_grad = dot(ds_ref[...], qblk[...]).astype(bf16)
    both = jnp.concatenate([key_grad, value_grad], axis=1)
    standard, _ = standardize(x_ref[...].astype(f32))
    normed = (standard * row_of(vec_ref, V_G1) + row_of(vec_ref, V_O1)).astype(bf16)
    through = dot(both, wkv[...], 1, 1)
    gkv_ref[...] += dot(normed, both, 0, 0)
    side_ref[1:2, :] += column_sum(value_grad.astype(f32))

    @pl.when(step < last)
    def _():
        dx_ref[...] = through.astype(bf16)
        row_ref[0:1, :] += column_sum(through * standard)
        row_ref[1:2, :] += column_sum(through)

    @pl.when(step == last)
    def _():
        query_grad = jnp.concatenate(
            [dq_acc[part].T for part in range(PARTS)], axis=0
        ) * (1.0 / math.sqrt(HEAD))
        low = query_grad.astype(bf16)
        entire = through + dot(low, wq[...], 1, 1)
        dx_ref[...] = entire.astype(bf16)
        row_ref[0:1, :] += column_sum(entire * standard)
        row_ref[1:2, :] += column_sum(entire)
        gq_ref[...] = dot(normed, low, 0, 0)
        side_ref[0:1, :] = column_sum(low.astype(f32))


def long_backward(place, e, k, v, kt, rows, q, da, o, linv, weights, vectors):
    total = k.shape[0]
    tiles = total // TILE
    turn = lambda i, place: lax.rem(place[0] + 1 + i, tiles)
    return pl.pallas_call(
        long_backward_kernel,
        grid_spec=pltpu.PrefetchScalarGridSpec(
            num_scalar_prefetch=1,
            grid=(tiles,),
            in_specs=[
                pl.BlockSpec((TILE, STEPS * CHUNK), lambda i, p: (turn(i, p), 0)),
                pl.BlockSpec((TILE, GROUP), lambda i, p: (turn(i, p), 0)),
                pl.BlockSpec((TILE, GROUP), lambda i, p: (turn(i, p), 0)),
                pl.BlockSpec((GROUP, TILE), lambda i, p: (0, turn(i, p))),
                pl.BlockSpec((TILE, WIDTH), lambda i, p: (turn(i, p), 0)),
                whole((TILE, GROUP)),
                whole((TILE, GROUP)),
                whole((PARTS, GROUP, CHUNK)),
                whole((STEPS * 8, CHUNK)),
                whole((WIDTH, 3 * WIDTH)),
                whole(vectors.shape),
            ],
            out_specs=[
                pl.BlockSpec((TILE, WIDTH), lambda i, p: (turn(i, p), 0)),
                whole((WIDTH, GROUP)),
                whole((WIDTH, 2 * GROUP)),
                whole((8, WIDTH)),
                whole((8, GROUP)),
            ],
            scratch_shapes=[
                pltpu.VMEM((STEPS * CHUNK, GROUP), bf16),
                pltpu.VMEM((STEPS * CHUNK, GROUP), bf16),
                pltpu.VMEM((STEPS * 8, CHUNK), f32),
                pltpu.VMEM((TILE, STEPS * CHUNK), bf16),
                pltpu.VMEM((PARTS, GROUP, CHUNK), f32),
                pltpu.VMEM((WIDTH, GROUP), bf16),
                pltpu.VMEM((WIDTH, 2 * GROUP), bf16),
            ],
        ),
        out_shape=[
            jax.ShapeDtypeStruct((total, WIDTH), bf16),
            jax.ShapeDtypeStruct((WIDTH, GROUP), f32),
            jax.ShapeDtypeStruct((WIDTH, 2 * GROUP), f32),
            jax.ShapeDtypeStruct((8, WIDTH), f32),
            jax.ShapeDtypeStruct((8, GROUP), f32),
        ],
        compiler_params=pltpu.CompilerParams(**PARAMS),
        cost_estimate=pl.CostEstimate(
            flops=40 * TILE * total * GROUP, bytes_accessed=32 << 20, transcendentals=0
        ),
        name="long_backward",
    )(place, e, k, v, kt, rows, q, da, o, linv, weights, vectors)


def short_backward_kernel(
    place_ref, e_ref, k_ref, v_ref, q_ref, kt_ref, da_ref, o_ref, linv_ref, n1_ref, x_ref, mid_ref, w_ref,
    vec_ref, gq_ref, gkv_ref,
    dx_ref, g_ref, row_ref, qv_ref,
    scaled, delta, dblk, qblk, ds_ref, dqt, dqkv,
):
    step = pl.program_id(0)
    count = k_ref.shape[0]

    @pl.when(step == 0)
    def _():
        for low in range(0, WIDTH, GROUP):
            turned = da_ref[:, low : low + GROUP].astype(f32).T
            product = turned * o_ref[low : low + GROUP, :]
            pieces = []
            for head in range(4):
                span = slice(head * HEAD, (head + 1) * HEAD)
                index = low // HEAD + head
                linv = linv_ref[8 * index : 8 * index + 1, :]
                delta[8 * index : 8 * index + 8, :] = jnp.broadcast_to(
                    column_sum(product[span, :]) * linv, (8, count)
                )
                pieces.append(turned[span, :] * linv)
            scaled[:, low : low + GROUP] = jnp.concatenate(pieces, axis=0).T.astype(bf16)

    def group(side):
        low = side * GROUP
        for head in range(4):
            index = side * 4 + head
            span = slice(head * count, (head + 1) * count)
            own = slice(head * HEAD, (head + 1) * HEAD)
            dblk[span, :] = head_lanes(scaled[:, low : low + GROUP], head)
            qblk[span, :] = head_lanes(q_ref[...], head)
            slopes = dot(v_ref[...], dblk[span, :], 1, 1)
            ds = (
                e_ref[:, span].astype(f32) * (slopes - delta[8 * index : 8 * index + 1, :])
            ).astype(bf16)
            ds_ref[:, span] = ds
            dqt[own, :] = dot(kt_ref[low + head * HEAD : low + (head + 1) * HEAD, :], ds)
        value_grad = dot(e_ref[...], dblk[...])
        key_grad = dot(ds_ref[...], qblk[...])
        query_grad = dqt[...].T * (1.0 / math.sqrt(HEAD))
        dqkv[:, low : low + GROUP] = query_grad.astype(bf16)
        dqkv[:, WIDTH + low : WIDTH + low + GROUP] = key_grad.astype(bf16)
        dqkv[:, 2 * WIDTH + low : 2 * WIDTH + low + GROUP] = value_grad.astype(bf16)

    for side in (0, 1):
        pl.when(step == side)(functools.partial(group, side))

    @pl.when(step == 1)
    def _():
        rows_grad = dot(dqkv[...], w_ref[...], 1, 1)
        standard, inverse = standardize(x_ref[...].astype(f32))
        through = norm_backward(rows_grad, standard, inverse, row_of(vec_ref, V_G1))
        dx_ref[...] = (mid_ref[...] + through).astype(bf16)
        row_ref[...] = jnp.zeros_like(row_ref)
        row_ref[0:1, :] = column_sum(rows_grad * standard)
        row_ref[1:2, :] = column_sum(rows_grad)
        qv_ref[...] = jnp.broadcast_to(column_sum(dqkv[...].astype(f32)), qv_ref.shape)
        total = dot(n1_ref[...], dqkv[...], 0, 0)
        g_ref[...] = total.astype(bf16)
        core = place_ref[1]
        for other in (0, 1):
            @pl.when(core == other)
            def _():
                for third in range(3):
                    low = third * WIDTH + other * GROUP
                    extra = gq_ref[...] if third == 0 else gkv_ref[:, (third - 1) * GROUP : third * GROUP]
                    g_ref[:, low : low + GROUP] = (total[:, low : low + GROUP] + extra).astype(bf16)


def short_backward(place, e, k, v, q, kt, da, o, linv, n1, rows, mid, weights, vectors, gq, gkv):
    count = k.shape[0]
    half = pl.BlockSpec((count, GROUP), lambda i, _: (0, i))
    return pl.pallas_call(
        short_backward_kernel,
        grid_spec=pltpu.PrefetchScalarGridSpec(
            num_scalar_prefetch=1,
            grid=(2,),
            in_specs=[
                pl.BlockSpec((count, 4 * count), lambda i, _: (0, i)),
                half,
                half,
                half,
                once((WIDTH, count)),
                once((count, WIDTH)),
                once((WIDTH, count)),
                once((HEADS * 8, count)),
                once((count, WIDTH)),
                once((count, WIDTH)),
                once((count, WIDTH)),
                once((WIDTH, 3 * WIDTH)),
                whole(vectors.shape),
                once((WIDTH, GROUP)),
                once((WIDTH, 2 * GROUP)),
            ],
            out_specs=[
                once((count, WIDTH)),
                once((WIDTH, 3 * WIDTH)),
                whole((8, WIDTH)),
                whole((8, 3 * WIDTH)),
            ],
            scratch_shapes=[
                pltpu.VMEM((count, WIDTH), bf16),
                pltpu.VMEM((HEADS * 8, count), f32),
                pltpu.VMEM((4 * count, GROUP), bf16),
                pltpu.VMEM((4 * count, GROUP), bf16),
                pltpu.VMEM((count, 4 * count), bf16),
                pltpu.VMEM((GROUP, count), f32),
                pltpu.VMEM((count, 3 * WIDTH), bf16),
            ],
        ),
        out_shape=[
            jax.ShapeDtypeStruct((count, WIDTH), bf16),
            jax.ShapeDtypeStruct((WIDTH, 3 * WIDTH), bf16),
            jax.ShapeDtypeStruct((8, WIDTH), f32),
            jax.ShapeDtypeStruct((8, 3 * WIDTH), f32),
        ],
        compiler_params=pltpu.CompilerParams(**PARAMS),
        cost_estimate=pl.CostEstimate(
            flops=24 * count * count * WIDTH, bytes_accessed=18 << 20, transcendentals=0
        ),
        name="short_backward",
    )(place, e, k, v, q, kt, da, o, linv, n1, rows, mid, weights, vectors, gq, gkv)


def per_device(
    incoming_rows,
    picture_label,
    triple_kernel,
    mixer_kernel,
    widening_kernel,
    narrowing_kernel,
    asker_offset,
    content_offset,
    mixer_offset_vector,
    widening_offset,
    narrowing_offset,
    leading_gain,
    leading_offset,
    second_gain,
    second_offset,
    loss_sensitivity,
):
    axes = ("band", "batch")
    band = lax.axis_index("band")
    bands = lax.axis_size("band")
    rows = incoming_rows[0]
    ids = picture_label[0]
    upstream = loss_sensitivity[0]
    shard = triple_kernel.shape[0]
    place = jnp.stack([band // 2, band % 2]).astype(jnp.int32)

    vector_shards = [
        v.astype(bf16)[:, None]
        for v in (
            asker_offset,
            content_offset,
            mixer_offset_vector,
            narrowing_offset,
            leading_gain,
            leading_offset,
            second_gain,
            second_offset,
        )
    ] + [widening_offset.astype(bf16).reshape(shard, 4)]
    vector_shard = jnp.concatenate(vector_shards + [jnp.zeros((shard, 116), bf16)], axis=1)
    first = lax.all_gather(
        jnp.concatenate([triple_kernel.astype(bf16), vector_shard], axis=1), axes, axis=0, tiled=True
    )
    all_rows = lax.all_gather(rows[:LONG], "band", axis=0, tiled=True)
    second = lax.all_gather(
        jnp.concatenate(
            [
                mixer_kernel.astype(bf16),
                widening_kernel.astype(bf16),
                narrowing_kernel.astype(bf16).reshape(4, shard, WIDTH).transpose(1, 0, 2).reshape(shard, FF),
            ],
            axis=1,
        ),
        axes,
        axis=0,
        tiled=True,
    )
    wqkv = first[:, : 3 * WIDTH]
    vectors = first[:, 3 * WIDTH : 3 * WIDTH + 16].T.astype(f32)
    hidden_shift = first[:, 3 * WIDTH + 8 : 3 * WIDTH + 12].reshape(1, FF).astype(f32)
    wp = second[:, :WIDTH]
    we = second[:, WIDTH : WIDTH + FF]
    wr = (
        second[:, WIDTH + FF :]
        .reshape(WIDTH // shard, shard, 4, WIDTH)
        .transpose(0, 2, 1, 3)
        .reshape(FF, WIDTH)
    )

    n1, q_s, k_s, v_s, kt_s, vt_s = short_qkv(rows, wqkv, vectors)
    e_s, o_s, linv_s, att_s = short_forward(q_s, k_s, vt_s, ids[LONG:])
    q_l, k_l, v_l, kt_l, vt_l = long_prepare(place, all_rows, wqkv, vectors)
    e_l, o_l, linv_l, att_l = long_forward(q_l, k_l, vt_l)

    pairs = [(i, i ^ 1) for i in range(bands)]
    even = place[1] == 0
    mine = jnp.where(even, att_l[:LONG], att_l[LONG:])
    other = lax.ppermute(jnp.where(even, att_l[LONG:], att_l[:LONG]), "band", pairs)
    att_long = jnp.concatenate([jnp.where(even, mine, other), jnp.where(even, other, mine)], axis=1)

    layer_out, mid, da, gp, ge, gr, feed_rows, hidden_sum = feed(
        rows, ids, upstream, att_long, att_s, wp, we, wr, vectors, hidden_shift
    )
    da_mine = jnp.where(even, da[:LONG, :GROUP], da[:LONG, GROUP:])
    da_other = lax.ppermute(jnp.where(even, da[:LONG, GROUP:], da[:LONG, :GROUP]), "band", pairs)
    da_l = jnp.concatenate([jnp.where(even, da_mine, da_other), jnp.where(even, da_other, da_mine)], axis=0)

    shards = WIDTH // shard
    second_grad = lax.psum_scatter(
        jnp.concatenate(
            [gp, ge, gr.reshape(shards, 4, shard, WIDTH).transpose(0, 2, 1, 3).reshape(WIDTH, FF)], axis=1
        ),
        axes,
        scatter_dimension=0,
        tiled=True,
    )

    dx, gq, gkv, long_rows, long_side = long_backward(
        place, e_l, k_l, v_l, kt_l, all_rows, q_l, da_l, o_l, linv_l, wqkv, vectors
    )
    dx_long = lax.psum_scatter(dx, "band", scatter_dimension=0, tiled=True)
    dx_s, g_qkv, short_rows, short_side = short_backward(
        place, e_s, k_s, v_s, q_s, kt_s, da[LONG:], o_s, linv_s, n1, rows[LONG:], mid[LONG:], wqkv, vectors, gq, gkv
    )

    spread = lambda row: jnp.where(
        even, jnp.concatenate([row, jnp.zeros_like(row)]), jnp.concatenate([jnp.zeros_like(row), row])
    )
    vector_rows = [
        short_side[0, :WIDTH] + spread(long_side[0]),
        short_side[0, 2 * WIDTH :] + spread(long_side[1]),
        feed_rows[0],
        feed_rows[1],
        short_rows[0] + long_rows[0],
        short_rows[1] + long_rows[1],
        feed_rows[2],
        feed_rows[3],
    ]
    vector_grad = jnp.concatenate(
        [jnp.stack(vector_rows, axis=1), hidden_sum.reshape(WIDTH, 4), jnp.zeros((WIDTH, 116), f32)], axis=1
    ).astype(bf16)
    first_grad = lax.psum_scatter(
        jnp.concatenate([g_qkv, vector_grad], axis=1), axes, scatter_dimension=0, tiled=True
    )

    standard, inverse = standardize(rows[:LONG].astype(f32))
    dx_l = (
        mid[:LONG] + norm_backward(dx_long.astype(f32), standard, inverse, vectors[V_G1][None, :])
    ).astype(bf16)
    input_grad = jnp.concatenate([dx_l, dx_s], axis=0)

    first_grad = first_grad.astype(f32)
    second_grad = second_grad.astype(f32)
    small = first_grad[:, 3 * WIDTH :]
    return (
        layer_out[None],
        input_grad[None],
        first_grad[:, : 3 * WIDTH],
        second_grad[:, :WIDTH],
        second_grad[:, WIDTH : WIDTH + FF],
        second_grad[:, WIDTH + FF :].reshape(shard, 4, WIDTH).transpose(1, 0, 2).reshape(4 * shard, WIDTH),
        small[:, 0],
        small[:, 1],
        small[:, 2],
        small[:, 8:12].reshape(4 * shard),
        small[:, 3],
        small[:, 4],
        small[:, 5],
        small[:, 6],
        small[:, 7],
    )


def solution(mesh):
    shards = P(("band", "batch"))
    tokens = P("batch", "band", None)
    kernels = P(("band", "batch"), None)
    in_specs = (
        (tokens, P("batch", "band")) + (kernels,) * 4 + (shards,) * 9 + (tokens,)
    )
    out_specs = (tokens, tokens) + (kernels,) * 4 + (shards,) * 9
    return jax.shard_map(
        per_device, mesh=mesh, in_specs=in_specs, out_specs=out_specs, check_vma=False
    )
```

```python
import functools
import math

import jax
import jax.numpy as jnp
from jax import lax
from jax.experimental import pallas as pl
from jax.experimental.pallas import tpu as pltpu
from jax.sharding import PartitionSpec as P

HEADS = 8
HEAD = 64
LONG = 256
WIDTH = 512
FF = 2048
GROUP = 256
TILE = 512
epsilon = 1e-06
gelu_scale = 0.7978845608028654
f32 = jnp.float32
bf16 = jnp.bfloat16
PARAMS = dict(vmem_limit_bytes=58 << 20)


def dot(left, right, cl=1, cr=0):
    return lax.dot_general(left, right, (((cl,), (cr,)), ((), ())), preferred_element_type=f32)


def standardize(rows):
    center = rows - jnp.mean(rows, axis=1, keepdims=True)
    inverse = lax.rsqrt(jnp.mean(center * center, axis=1, keepdims=True) + epsilon)
    return center * inverse, inverse


def norm_backward(incoming, standard, inverse, scaling):
    scaled = incoming * scaling
    return inverse * (
        scaled
        - jnp.mean(scaled, axis=1, keepdims=True)
        - standard * jnp.mean(scaled * standard, axis=1, keepdims=True)
    )


def column_sum(rows):
    return jnp.sum(rows, axis=0, keepdims=True)


def head_lanes(block, head):
    lane = lax.broadcasted_iota(jnp.int32, block.shape, 1) // HEAD
    return jnp.where(lane == head, block.astype(f32), 0.0).astype(bf16)


V_ASK, V_CONTENT, V_MIXER, V_NARROW, V_G1, V_O1, V_G2, V_O2 = range(8)


def row_of(table_ref, index):
    return table_ref[index : index + 1, :]


def whole(shape):
    return pl.BlockSpec(shape, lambda *_: (0,) * len(shape))


def once(shape):
    return pl.BlockSpec(shape, lambda *_: (0,) * len(shape), pipeline_mode=pl.Buffered(1))


ANYWHERE = pl.BlockSpec(memory_space=pl.ANY)


def behind(kernel, count, prefetch=True):
    skip = 1 if prefetch else 0
    return lambda *refs: kernel(*refs[:skip], *refs[skip + count :])


SIDE = 128
FIRST = 3 * WIDTH + SIDE
SECOND = WIDTH + 2 * FF


class Layout:
    def __init__(self, bands, batches):
        self.bands, self.batches = bands, batches
        self.depth = bands // 4
        self.shards = bands * batches
        self.rows = WIDTH // self.shards
        self.pieces = self.rows % 16 == 0
        self.plane = [(kx, ky) for kx in (0, 1) for ky in range(batches)]

    def shard(self, place, kc, kx, ky, kz, sign):
        z = lax.rem(place[2] + (self.depth + sign * kz), self.depth)
        x = lax.rem(place[3] + kx, 2)
        y = lax.rem(place[4] + (self.batches + sign * ky), self.batches)
        core = lax.rem(place[1] + kc, 2)
        return ((z * 2 + x) * 2 + core) * self.batches + y

    def chip(self, place, kx, kz):
        return lax.rem(place[2] + kz, self.depth) * 2 + lax.rem(place[3] + kx, 2)

    def shift_depth(self, block, k):
        pairs = [(i, ((i // 4 + k) % self.depth) * 4 + i % 4) for i in range(self.bands)]
        return lax.ppermute(block, "band", pairs)

    def flip(self, block, bit):
        return lax.ppermute(block, "band", [(i, i ^ bit) for i in range(self.bands)])

    def shift_plane(self, block, kx, ky):
        n = self.batches
        pairs = [
            (b * n + y, (b ^ (2 * kx)) * n + (y + ky) % n) for b in range(self.bands) for y in range(n)
        ]
        return lax.ppermute(block, ("band", "batch"), pairs)

    def gather_depth(self, block, deps=()):
        return stack_blocks([block] + [self.shift_depth(block, k) for k in range(1, self.depth)], deps)

    def gather_plane(self, stack):
        return [stack if k == (0, 0) else self.shift_plane(stack, *k) for k in self.plane]

    def gather_core(self, plane):
        return plane + [self.flip(part, 1) for part in plane]

    def gather_whole(self, block):
        return [lax.all_gather(block, ("band", "batch"), axis=0, tiled=True)]

    def gathered_specs(self, columns):
        if not self.pieces:
            return [once((WIDTH, columns))]
        return [once((self.depth, self.rows, columns))] * (2 * len(self.plane))

    def each_gathered(self, place, refs, visit):
        if not self.pieces:
            for low in range(0, WIDTH, 16):
                visit(low // 16, refs[0][low : low + 16, :])
            return
        index = 0
        for kc in (0, 1):
            for kx, ky in self.plane:
                for kz in range(self.depth):
                    visit(self.shard(place, kc, kx, ky, kz, -1), refs[index][kz])
                index += 1

    def scattered_shapes(self, columns):
        if not self.pieces:
            return [jax.ShapeDtypeStruct((WIDTH, columns), bf16)]
        shape = (len(self.plane), self.depth, self.rows, columns)
        return [jax.ShapeDtypeStruct(shape, bf16)] * 2

    def store_scattered(self, place, refs, take):
        if not self.pieces:
            for low in range(0, WIDTH, 16):
                refs[0][low : low + 16, :] = take(low // 16)
            return
        for kc in (0, 1):
            for n, (kx, ky) in enumerate(self.plane):
                for kz in range(self.depth):
                    refs[kc][n, kz] = take(self.shard(place, kc, kx, ky, kz, 1))

    def scatter_core(self, parts):
        keep, send = parts
        arrived = self.flip(send, 1)
        return [(keep[n].astype(f32) + arrived[n].astype(f32)).astype(bf16) for n in range(len(self.plane))]

    def scatter_plane(self, pairs):
        arrived = [self.shift_plane(pairs[n], *k) for n, k in enumerate(self.plane) if n]
        return self.add_depth(pairs[:1] + arrived)

    def add_depth(self, stacks):
        totals = []
        for k in range(self.depth):
            total = stacks[0][k].astype(f32)
            for stack in stacks[1:]:
                total = total + stack[k].astype(f32)
            totals.append(total if k == 0 else total.astype(bf16))
        return totals

    def scatter_depth(self, totals, sign=1):
        final = totals[0]
        for k in range(1, self.depth):
            final = final + self.shift_depth(totals[k], (sign * k) % self.depth).astype(f32)
        return final

    def scatter_whole(self, part):
        return lax.psum_scatter(part, ("band", "batch"), scatter_dimension=0, tiled=True).astype(f32)


def tie(values, deps):
    count = len(values)
    return pl.pallas_call(
        lambda *refs: None,
        in_specs=[ANYWHERE] * (count + len(deps)),
        out_specs=[ANYWHERE] * count,
        out_shape=[jax.ShapeDtypeStruct(v.shape, v.dtype) for v in values],
        input_output_aliases={i: i for i in range(count)},
        name="tie",
    )(*values, *deps)


def stack_kernel(*refs):
    for index, ref in enumerate(refs[:-1]):
        refs[-1][index] = ref[...]


def stack_blocks(blocks, deps):
    shape = blocks[0].shape
    return pl.pallas_call(
        behind(stack_kernel, len(deps), False),
        in_specs=[ANYWHERE] * len(deps) + [pl.BlockSpec(memory_space=pltpu.VMEM)] * len(blocks),
        out_shape=jax.ShapeDtypeStruct((len(blocks), *shape), blocks[0].dtype),
        name="stack_blocks",
    )(*deps, *blocks)


def pack_first_kernel(triple_ref, *refs):
    vectors, wide, out_ref, table = refs[:8], *refs[8:]
    shard = triple_ref.shape[0]
    table[...] = jnp.zeros_like(table)
    for index, ref in enumerate(vectors):
        table[index : index + 1, :shard] = ref[...]
    out_ref[:, : 3 * WIDTH] = triple_ref[...].astype(bf16)
    turned = table[...].T[:shard, :]
    across = jnp.pad(wide[...], ((0, shard - 1), (SIDE - 4 * shard, 0)))
    out_ref[:, 3 * WIDTH :] = (turned + across).astype(bf16)


def pack_first(triple, vectors, wide):
    shard = triple.shape[0]
    return pl.pallas_call(
        pack_first_kernel,
        out_shape=jax.ShapeDtypeStruct((shard, FIRST), bf16),
        scratch_shapes=[pltpu.VMEM((SIDE, SIDE), f32)],
        compiler_params=pltpu.CompilerParams(**PARAMS),
        name="pack_first",
    )(triple, *[v[None, :] for v in vectors], wide[None, :])


def pack_rows_kernel(rows_ref, out_ref):
    out_ref[...] = rows_ref[...]


def pack_rows(rows, deps):
    block = pl.BlockSpec((LONG, WIDTH), lambda i: (0, 0))
    return pl.pallas_call(
        behind(pack_rows_kernel, len(deps), False),
        grid=(1,),
        in_specs=[ANYWHERE] * len(deps) + [block],
        out_specs=block,
        out_shape=jax.ShapeDtypeStruct((LONG, WIDTH), bf16),
        name="pack_rows",
    )(*deps, rows)


def pack_second_kernel(mixer_ref, widening_ref, narrowing_ref, out_ref):
    shard = mixer_ref.shape[0]
    out_ref[:, :WIDTH] = mixer_ref[...].astype(bf16)
    out_ref[:, WIDTH : WIDTH + FF] = widening_ref[...].astype(bf16)
    for k in range(4):
        low = WIDTH + FF + k * WIDTH
        out_ref[:, low : low + WIDTH] = narrowing_ref[k * shard : (k + 1) * shard, :].astype(bf16)


def pack_second(mixer, widening, narrowing, deps):
    blocks = [pl.BlockSpec(memory_space=pltpu.VMEM)] * 3
    return pl.pallas_call(
        behind(pack_second_kernel, len(deps), False),
        out_shape=jax.ShapeDtypeStruct((mixer.shape[0], SECOND), bf16),
        in_specs=[ANYWHERE] * len(deps) + blocks,
        compiler_params=pltpu.CompilerParams(**PARAMS),
        name="pack_second",
    )(*deps, mixer, widening, narrowing)


def short_qkv_kernel(layout, place_ref, x_ref, *refs):
    count = len(layout.gathered_specs(FIRST))
    pieces = refs[:count]
    n1_ref, q_ref, k_ref, v_ref, kt_ref, vt_ref, w_ref, vec_ref, hid_ref, side, spread = refs[count:]

    @pl.when(pl.program_id(0) == 0)
    def _():
        def visit(block, rows):
            span = pl.ds(pl.multiple_of(block * 16, 16), 16)
            w_ref[span, :] = rows[:, : 3 * WIDTH]
            side[span, :] = rows[:, 3 * WIDTH :].astype(f32)
            if layout.pieces:
                spread[pl.ds(block, 1), :] = rows[0:1, 3 * WIDTH :].astype(f32)

        layout.each_gathered(place_ref, pieces, visit)
        vec_ref[...] = side[...].T[:16, :]
        if layout.pieces:
            shard = 4 * layout.rows
            for index in range(layout.shards):
                hid_ref[:, index * shard : (index + 1) * shard] = spread[index : index + 1, SIDE - shard :]

    standard, _ = standardize(x_ref[...].astype(f32))
    normed = (standard * row_of(vec_ref, V_G1) + row_of(vec_ref, V_O1)).astype(bf16)
    n1_ref[...] = normed
    projected = dot(normed, w_ref[...])
    q = (projected[:, :WIDTH] + row_of(vec_ref, V_ASK)).astype(bf16)
    q_ref[...] = (q.astype(f32) * (1.0 / math.sqrt(HEAD))).astype(bf16)
    k = projected[:, WIDTH : 2 * WIDTH]
    v = projected[:, 2 * WIDTH :] + row_of(vec_ref, V_CONTENT)
    k_ref[...] = k.astype(bf16)
    v_ref[...] = v.astype(bf16)
    kt_ref[...] = k.T.astype(bf16)
    vt_ref[...] = v.T.astype(bf16)


def short_qkv(layout, place, rows, pieces):
    count = rows.shape[0] - LONG
    block = 256
    row_spec = pl.BlockSpec((block, WIDTH), lambda i, _: (i, 0))
    col_spec = pl.BlockSpec((WIDTH, block), lambda i, _: (0, i))
    flat = jax.ShapeDtypeStruct((count, WIDTH), bf16)
    tall = jax.ShapeDtypeStruct((WIDTH, count), bf16)
    return pl.pallas_call(
        functools.partial(short_qkv_kernel, layout),
        grid_spec=pltpu.PrefetchScalarGridSpec(
            num_scalar_prefetch=1,
            grid=(count // block,),
            in_specs=[pl.BlockSpec((block, WIDTH), lambda i, _: (i + LONG // block, 0))]
            + layout.gathered_specs(FIRST),
            out_specs=[row_spec, row_spec, row_spec, row_spec, col_spec, col_spec]
            + [once((WIDTH, 3 * WIDTH)), whole((16, WIDTH)), whole((1, FF))],
            scratch_shapes=[pltpu.VMEM((WIDTH, SIDE), f32), pltpu.VMEM((max(8, layout.shards), SIDE), f32)],
        ),
        out_shape=[flat, flat, flat, flat, tall, tall]
        + [
            jax.ShapeDtypeStruct((WIDTH, 3 * WIDTH), bf16),
            jax.ShapeDtypeStruct((16, WIDTH), f32),
            jax.ShapeDtypeStruct((1, FF), f32),
        ],
        compiler_params=pltpu.CompilerParams(**PARAMS),
        cost_estimate=pl.CostEstimate(
            flops=2 * count * WIDTH * 3 * WIDTH, bytes_accessed=10 << 20, transcendentals=0
        ),
        name="short_qkv",
    )(place, rows, *pieces)


def short_forward_kernel(
    q_ref, k_ref, vt_ref, idc_ref, idr_ref, e_ref, o_ref, linv_ref, att_ref, s_ref, bias_ref, top_ref
):
    step = pl.program_id(0)
    count = k_ref.shape[0]
    tile = 256

    @pl.when(step == 0)
    def _():
        same = idc_ref[...] == idr_ref[...]
        bias_ref[...] = jnp.where(same, 0.0, -1e30)

    def first(slot):
        masked = head_lanes(q_ref[...], lax.rem(step, 4))
        top = None
        for low in range(0, count, tile):
            s = dot(k_ref[low : low + tile, :], masked, 1, 1) + bias_ref[low : low + tile, :]
            s_ref[slot, low : low + tile, :] = s
            part = jnp.max(s, axis=0, keepdims=True)
            top = part if top is None else jnp.maximum(top, part)
        top_ref[slot] = jnp.broadcast_to(top, (8, count))

    def second(slot):
        head = step - 1
        top = top_ref[slot, 0:1, :]
        mixed = jnp.zeros((HEAD, count), f32)
        total = jnp.zeros((1, count), f32)
        for low in range(0, count, tile):
            e = jnp.exp(s_ref[slot, low : low + tile, :] - top)
            total += column_sum(e)
            low_e = e.astype(bf16)
            e_ref[low : low + tile, :] = low_e
            mixed += dot(vt_ref[pl.ds(pl.multiple_of(head * HEAD, HEAD), HEAD), low : low + tile], low_e)
        linv = 1.0 / total
        linv_ref[...] = jnp.broadcast_to(linv, (8, count))
        o_ref[pl.ds(pl.multiple_of(head * HEAD, HEAD), HEAD), :] = mixed * linv

    last = pl.num_programs(0) - 1

    @pl.when(step == 0)
    def _():
        first(0)

    for parity in (0, 1):
        @pl.when((step > 0) & (step < last) & (lax.rem(step, 2) == parity))
        def _():
            first(parity)
            second(1 - parity)

    @pl.when(step == last)
    def _():
        second((HEADS - 1) % 2)
        for low in range(0, WIDTH, 128):
            att_ref[:, low : low + 128] = o_ref[low : low + 128, :].T.astype(bf16)


def short_forward(q, k, vt, ids, deps):
    count = q.shape[0]
    now = lambda s: (0, jnp.minimum(s, HEADS - 1) // 4)
    before = lambda s: (0, jnp.maximum(s - 1, 0))
    return pl.pallas_call(
        behind(short_forward_kernel, len(deps), False),
        grid=(HEADS + 1,),
        in_specs=[ANYWHERE] * len(deps)
        + [
            pl.BlockSpec((count, GROUP), now),
            pl.BlockSpec((count, GROUP), now),
            whole((WIDTH, count)),
            whole((count, 1)),
            whole((1, count)),
        ],
        out_specs=[
            pl.BlockSpec((count, count), before),
            whole((WIDTH, count)),
            pl.BlockSpec((8, count), lambda s: (jnp.maximum(s - 1, 0), 0)),
            whole((count, WIDTH)),
        ],
        out_shape=[
            jax.ShapeDtypeStruct((count, HEADS * count), bf16),
            jax.ShapeDtypeStruct((WIDTH, count), f32),
            jax.ShapeDtypeStruct((HEADS * 8, count), f32),
            jax.ShapeDtypeStruct((count, WIDTH), bf16),
        ],
        scratch_shapes=[
            pltpu.VMEM((2, count, count), f32),
            pltpu.VMEM((count, count), f32),
            pltpu.VMEM((2, 8, count), f32),
        ],
        compiler_params=pltpu.CompilerParams(**PARAMS),
        cost_estimate=pl.CostEstimate(
            flops=12 * count * count * WIDTH, bytes_accessed=12 << 20, transcendentals=HEADS * count * count
        ),
        name="short_forward",
    )(*deps, q, k, vt, ids[:, None], ids[None, :])


def long_prepare_kernel(
    depth, place_ref, own0, other0, own1, other1, w_ref, vec_ref, n1_ref, q_ref, k_ref, v_ref, kt_ref, vt_ref
):
    step = pl.program_id(0)
    core = place_ref[1]
    near = step < depth
    lanes = lambda base: pl.ds(pl.multiple_of(base + core * GROUP, GROUP), GROUP)
    rows = jnp.concatenate(
        [jnp.where(near, own0[0], own1[0]), jnp.where(near, other0[0], other1[0])], axis=0
    )
    standard, _ = standardize(rows.astype(f32))
    normed = (standard * row_of(vec_ref, V_G1) + row_of(vec_ref, V_O1)).astype(bf16)
    n1_ref[...] = normed
    k = dot(normed, w_ref[:, lanes(WIDTH)])
    v = dot(normed, w_ref[:, lanes(2 * WIDTH)]) + vec_ref[V_CONTENT : V_CONTENT + 1, lanes(0)]
    k_ref[...] = k.astype(bf16)
    v_ref[...] = v.astype(bf16)
    kt_ref[...] = k.T.astype(bf16)
    vt_ref[...] = v.T.astype(bf16)

    @pl.when(step == 0)
    def _():
        q = (dot(normed, w_ref[:, lanes(0)]) + vec_ref[V_ASK : V_ASK + 1, lanes(0)]).astype(bf16)
        q_ref[...] = (q.astype(f32) * (1.0 / math.sqrt(HEAD))).astype(bf16)


def long_prepare(layout, place, stacks, weights, vectors, deps):
    depth = layout.depth
    total = 2 * depth * TILE
    row_spec = pl.BlockSpec((TILE, GROUP), lambda i, _: (i, 0))
    col_spec = pl.BlockSpec((GROUP, TILE), lambda i, _: (0, i))
    near = pl.BlockSpec((1, LONG, WIDTH), lambda i, _: (jnp.minimum(i, depth - 1), 0, 0))
    far = pl.BlockSpec((1, LONG, WIDTH), lambda i, _: (jnp.maximum(i - depth, 0), 0, 0))
    flat = jax.ShapeDtypeStruct((total, GROUP), bf16)
    tall = jax.ShapeDtypeStruct((GROUP, total), bf16)
    return pl.pallas_call(
        behind(functools.partial(long_prepare_kernel, depth), len(deps)),
        grid_spec=pltpu.PrefetchScalarGridSpec(
            num_scalar_prefetch=1,
            grid=(2 * depth,),
            in_specs=[ANYWHERE] * len(deps)
            + [near, near, far, far, whole((WIDTH, 3 * WIDTH)), whole(vectors.shape)],
            out_specs=[
                pl.BlockSpec((TILE, WIDTH), lambda i, _: (i, 0)),
                whole((TILE, GROUP)),
                row_spec,
                row_spec,
                col_spec,
                col_spec,
            ],
        ),
        out_shape=[
            jax.ShapeDtypeStruct((total, WIDTH), bf16),
            jax.ShapeDtypeStruct((TILE, GROUP), bf16),
            flat,
            flat,
            tall,
            tall,
        ],
        compiler_params=pltpu.CompilerParams(**PARAMS),
        cost_estimate=pl.CostEstimate(
            flops=4 * total * WIDTH * GROUP, bytes_accessed=18 << 20, transcendentals=0
        ),
        name="long_prepare",
    )(place, *deps, *stacks, weights, vectors)


CHUNK = 256
PARTS = TILE // CHUNK
LOCAL_HEADS = GROUP // HEAD
STEPS = LOCAL_HEADS * PARTS


def long_forward_kernel(
    q_ref, k_ref, vt_ref, e_ref, o_ref, linv_ref, keep_ref, send_ref, s_ref, top_ref
):
    step = pl.program_id(0)
    total = k_ref.shape[0]
    tile = 512
    last = pl.num_programs(0) - 1

    def masked_queries():
        rows = pl.ds(pl.multiple_of(lax.rem(step, PARTS) * CHUNK, CHUNK), CHUNK)
        return head_lanes(q_ref[rows, :], step // PARTS)

    def first_tile(slot, low, masked, top):
        s = dot(k_ref[pl.ds(low, tile), :], masked, 1, 1)
        s_ref[slot, pl.ds(low, tile), :] = s
        return jnp.maximum(top, jnp.max(s.reshape(tile // 8, 8, CHUNK), axis=0))

    def second_tile(slot, low, top, head, carry):
        summed, mixed = carry
        e = jnp.exp(s_ref[slot, pl.ds(low, tile), :] - top)
        summed = summed + jnp.sum(e.reshape(tile // 8, 8, CHUNK), axis=0)
        low_e = e.astype(bf16)
        e_ref[pl.ds(low, tile), :] = low_e
        values = vt_ref[pl.ds(pl.multiple_of(head * HEAD, HEAD), HEAD), pl.ds(low, tile)]
        return summed, mixed + dot(values, low_e)

    start_top = jnp.full((8, CHUNK), -1e30, f32)
    start_sum = (jnp.zeros((8, CHUNK), f32), jnp.zeros((HEAD, CHUNK), f32))

    def finish(head, part, carry):
        summed, mixed = carry
        linv = 1.0 / column_sum(summed)
        linv_ref[...] = jnp.broadcast_to(linv, (8, CHUNK))
        o_ref[part, pl.ds(pl.multiple_of(head * HEAD, HEAD), HEAD), :] = mixed * linv

    def place(turn):
        return pl.multiple_of(turn * tile, tile)

    @pl.when(step == 0)
    def _():
        masked = masked_queries()
        top_ref[0] = lax.fori_loop(
            0, total // tile, lambda t, top: first_tile(0, place(t), masked, top), start_top
        )

    for parity in (0, 1):
        @pl.when((step > 0) & (step < last) & (lax.rem(step, 2) == parity))
        def _():
            masked = masked_queries()
            before = step - 1
            head = before // PARTS
            top_row = jnp.max(top_ref[1 - parity], axis=0, keepdims=True)

            def body(turn, carry):
                top, kept = carry
                low = place(turn)
                top = first_tile(parity, low, masked, top)
                kept = second_tile(1 - parity, low, top_row, head, kept)
                return top, kept

            top, kept = lax.fori_loop(0, total // tile, body, (start_top, start_sum))
            top_ref[parity] = top
            finish(head, lax.rem(before, PARTS), kept)

    @pl.when(step == last)
    def _():
        slot = (STEPS - 1) % 2
        top_row = jnp.max(top_ref[slot], axis=0, keepdims=True)
        head = LOCAL_HEADS - 1
        kept = lax.fori_loop(
            0,
            total // tile,
            lambda t, carry: second_tile(slot, place(t), top_row, head, carry),
            start_sum,
        )
        finish(head, PARTS - 1, kept)
        keep_ref[...] = o_ref[0].T.astype(bf16)
        send_ref[...] = o_ref[1].T.astype(bf16)


def long_forward(q, k, vt):
    total = k.shape[0]
    before = lambda s: jnp.maximum(s - 1, 0)
    half = jax.ShapeDtypeStruct((CHUNK, GROUP), bf16)
    return pl.pallas_call(
        long_forward_kernel,
        grid=(STEPS + 1,),
        in_specs=[once((TILE, GROUP)), once((total, GROUP)), once((GROUP, total))],
        out_specs=[
            pl.BlockSpec((total, CHUNK), lambda s: (0, before(s))),
            whole((PARTS, GROUP, CHUNK)),
            pl.BlockSpec((8, CHUNK), lambda s: (before(s), 0)),
            whole((CHUNK, GROUP)),
            whole((CHUNK, GROUP)),
        ],
        scratch_shapes=[pltpu.VMEM((2, total, CHUNK), f32), pltpu.VMEM((2, 8, CHUNK), f32)],
        out_shape=[
            jax.ShapeDtypeStruct((total, STEPS * CHUNK), bf16),
            jax.ShapeDtypeStruct((PARTS, GROUP, CHUNK), f32),
            jax.ShapeDtypeStruct((STEPS * 8, CHUNK), f32),
            half,
            half,
        ],
        compiler_params=pltpu.CompilerParams(**PARAMS),
        cost_estimate=pl.CostEstimate(
            flops=16 * TILE * total * GROUP, bytes_accessed=24 << 20, transcendentals=4 * TILE * total
        ),
        name="long_forward",
    )(q, k, vt)


def feed_kernel(layout, place_ref, x_ref, ids_ref, g_ref, mine_ref, other_ref, short_ref, vec_ref, hid_ref, *refs):
    count = len(layout.gathered_specs(SECOND))
    pieces, refs = refs[:count], refs[count:]
    out_ref, midl_ref, mids_ref, keep_ref, send_ref, das_ref, row_ref, hsum_ref = refs[:8]
    grads = refs[8:-6]
    wp_ref, we_ref, wr_ref, accp, acce, accr = refs[-6:]
    step = pl.program_id(0)
    core = place_ref[1]

    @pl.when(step == 0)
    def _():
        accp[...] = jnp.zeros_like(accp)
        acce[...] = jnp.zeros_like(acce)
        accr[...] = jnp.zeros_like(accr)
        row_ref[...] = jnp.zeros_like(row_ref)
        hsum_ref[...] = jnp.zeros_like(hsum_ref)

        def visit(block, rows):
            span = pl.ds(pl.multiple_of(block * 16, 16), 16)
            wp_ref[span, :] = rows[:, :WIDTH]
            we_ref[span, :] = rows[:, WIDTH : WIDTH + FF]
            for k in range(4):
                low = WIDTH + FF + k * WIDTH
                wr_ref[pl.ds(pl.multiple_of(block * 64 + 16 * k, 16), 16), :] = rows[:, low : low + WIDTH]

        layout.each_gathered(place_ref, pieces, visit)

    x = x_ref[...].astype(f32)
    live = (ids_ref[...] >= 0).astype(f32)
    upstream = g_ref[...].astype(f32)
    mine, other = mine_ref[...], other_ref[...]
    swapped = core == 1
    long = jnp.concatenate([jnp.where(swapped, other, mine), jnp.where(swapped, mine, other)], axis=1)
    attended = jnp.where(step == 0, long, short_ref[...])
    branch = dot(attended, wp_ref[...]) + row_of(vec_ref, V_MIXER)
    middle = x + live * branch
    standard, inverse = standardize(middle)
    gain = row_of(vec_ref, V_G2)
    normed = (standard * gain + row_of(vec_ref, V_O2)).astype(bf16)
    hidden = dot(normed, we_ref[...]) + hid_ref[...]
    square = hidden * hidden
    tangent = jnp.tanh(hidden * (gelu_scale + (gelu_scale * 0.044715) * square))
    half = 0.5 * (1.0 + tangent)
    active = (hidden * half).astype(bf16)
    slope = half + (0.5 * hidden) * (1.0 - tangent * tangent) * (
        gelu_scale + (gelu_scale * 3.0 * 0.044715) * square
    )
    branch_two = dot(active, wr_ref[...]) + row_of(vec_ref, V_NARROW)
    out_ref[...] = (middle + live * branch_two).astype(bf16)
    branch_grad = live * upstream
    branch_low = branch_grad.astype(bf16)
    accr[...] += dot(active, branch_low, 0, 0)
    hidden_grad = dot(branch_low, wr_ref[...], 1, 1) * slope
    hidden_low = hidden_grad.astype(bf16)
    hsum_ref[...] += column_sum(hidden_low.astype(f32))
    acce[...] += dot(normed, hidden_low, 0, 0)
    normed_grad = dot(hidden_low, we_ref[...], 1, 1)
    middle_grad = upstream + norm_backward(normed_grad, standard, inverse, gain)
    attn_low = (live * middle_grad).astype(bf16)
    accp[...] += dot(attended, attn_low, 0, 0)
    attended_grad = dot(attn_low, wp_ref[...], 1, 1).astype(bf16)
    mids_ref[...] = middle_grad
    das_ref[...] = attended_grad

    @pl.when(step == 0)
    def _():
        midl_ref[...] = middle_grad
        left, right = attended_grad[:, :GROUP], attended_grad[:, GROUP:]
        keep_ref[...] = jnp.where(swapped, right, left)
        send_ref[...] = jnp.where(swapped, left, right)

    row_ref[0:1, :] += column_sum(attn_low.astype(f32))
    row_ref[1:2, :] += column_sum(branch_low.astype(f32))
    row_ref[2:3, :] += column_sum(normed_grad * standard)
    row_ref[3:4, :] += column_sum(normed_grad)

    @pl.when(step == pl.num_programs(0) - 1)
    def _():
        def take(block):
            span = pl.ds(pl.multiple_of(block * 16, 16), 16)
            parts = [accp[span, :], acce[span, :]] + [
                accr[pl.ds(pl.multiple_of(block * 64 + 16 * k, 16), 16), :] for k in range(4)
            ]
            return jnp.concatenate(parts, axis=1).astype(bf16)

        layout.store_scattered(place_ref, grads, take)


def feed(layout, place, rows, ids, upstream, mine, other, short, vectors, hidden_shift, pieces):
    count = rows.shape[0]
    block = LONG
    row_spec = pl.BlockSpec((block, WIDTH), lambda i, _: (i, 0))
    late_spec = pl.BlockSpec((block, WIDTH), lambda i, _: (jnp.maximum(i - 1, 0), 0))
    grads = layout.scattered_shapes(SECOND)
    return pl.pallas_call(
        functools.partial(feed_kernel, layout),
        grid_spec=pltpu.PrefetchScalarGridSpec(
            num_scalar_prefetch=1,
            grid=(count // block,),
            in_specs=[
                row_spec,
                pl.BlockSpec((block, 1), lambda i, _: (i, 0)),
                row_spec,
                once((block, GROUP)),
                once((block, GROUP)),
                late_spec,
                whole(vectors.shape),
                whole((1, FF)),
            ]
            + layout.gathered_specs(SECOND),
            out_specs=[
                row_spec,
                once((block, WIDTH)),
                late_spec,
                once((block, GROUP)),
                once((block, GROUP)),
                late_spec,
                whole((8, WIDTH)),
                whole((1, FF)),
            ]
            + [once(g.shape) for g in grads],
            scratch_shapes=[
                pltpu.VMEM((WIDTH, WIDTH), bf16),
                pltpu.VMEM((WIDTH, FF), bf16),
                pltpu.VMEM((FF, WIDTH), bf16),
                pltpu.VMEM((WIDTH, WIDTH), f32),
                pltpu.VMEM((WIDTH, FF), f32),
                pltpu.VMEM((FF, WIDTH), f32),
            ],
        ),
        out_shape=[
            jax.ShapeDtypeStruct((count, WIDTH), bf16),
            jax.ShapeDtypeStruct((block, WIDTH), f32),
            jax.ShapeDtypeStruct((count - block, WIDTH), f32),
            jax.ShapeDtypeStruct((block, GROUP), bf16),
            jax.ShapeDtypeStruct((block, GROUP), bf16),
            jax.ShapeDtypeStruct((count - block, WIDTH), bf16),
            jax.ShapeDtypeStruct((8, WIDTH), f32),
            jax.ShapeDtypeStruct((1, FF), f32),
        ]
        + grads,
        compiler_params=pltpu.CompilerParams(**PARAMS),
        cost_estimate=pl.CostEstimate(
            flops=6 * count * WIDTH * (WIDTH + 2 * FF), bytes_accessed=18 << 20, transcendentals=count * FF
        ),
        name="feed",
    )(place, rows, ids[:, None], upstream, mine, other, short, vectors, hidden_shift, *pieces)


def long_backward_kernel(
    final, place_ref, e_ref, k_ref, v_ref, kt_ref, n1_ref, q_ref, mine_ref, other_ref, o_ref, linv_ref, w_ref, vec_ref,
    *refs,
):
    if final:
        dq_in, gkv_in, row_in, side_in, *refs = refs
    (
    keep_ref, send_ref, gq_ref, dq_acc, gkv_ref, row_ref, side_ref,
    qblk, dblk, delta, ds_ref, wq, wkv,
    ) = refs
    step = pl.program_id(0)
    core = place_ref[1]

    @pl.when(step == 0)
    def _():
        lanes = lambda base: pl.ds(pl.multiple_of(base + core * GROUP, GROUP), GROUP)
        wq[...] = w_ref[:, lanes(0)]
        wkv[:, :GROUP] = w_ref[:, lanes(WIDTH)]
        wkv[:, GROUP:] = w_ref[:, lanes(2 * WIDTH)]
        if final:
            dq_acc[...] = dq_in[...]
            gkv_ref[...] = gkv_in[...]
            row_ref[...] = row_in[...]
            side_ref[...] = side_in[...]
        else:
            for ref in (dq_acc, gkv_ref, row_ref, side_ref):
                ref[...] = jnp.zeros_like(ref)
        for part in range(PARTS):
            rows = slice(part * CHUNK, (part + 1) * CHUNK)
            turned = (mine_ref, other_ref)[part][...].astype(f32).T
            product = turned * o_ref[part]
            pieces = []
            for head in range(LOCAL_HEADS):
                index = head * PARTS + part
                span = slice(head * HEAD, (head + 1) * HEAD)
                linv = linv_ref[8 * index : 8 * index + 1, :]
                delta[8 * index : 8 * index + 8, :] = jnp.broadcast_to(
                    column_sum(product[span, :]) * linv, (8, CHUNK)
                )
                pieces.append(turned[span, :] * linv)
            scaled = jnp.concatenate(pieces, axis=0).T
            for head in range(LOCAL_HEADS):
                index = head * PARTS + part
                span = slice(index * CHUNK, (index + 1) * CHUNK)
                dblk[span, :] = head_lanes(scaled, head)
                qblk[span, :] = head_lanes(q_ref[rows, :], head)

    for head in range(LOCAL_HEADS):
        for part in range(PARTS):
            index = head * PARTS + part
            span = slice(index * CHUNK, (index + 1) * CHUNK)
            slopes = dot(v_ref[...], dblk[span, :], 1, 1)
            ds = (
                e_ref[:, span].astype(f32) * (slopes - delta[8 * index : 8 * index + 1, :])
            ).astype(bf16)
            ds_ref[:, span] = ds
            own = slice(head * HEAD, (head + 1) * HEAD)
            dq_acc[part, own, :] += dot(kt_ref[own, :], ds)

    value_grad = dot(e_ref[...], dblk[...]).astype(bf16)
    key_grad = dot(ds_ref[...], qblk[...]).astype(bf16)
    both = jnp.concatenate([key_grad, value_grad], axis=1)
    normed = n1_ref[...]
    through = dot(both, wkv[...], 1, 1)
    gkv_ref[...] += dot(normed, both, 0, 0)
    side_ref[1:2, :] += column_sum(value_grad.astype(f32))

    def put(entire):
        low = entire.astype(bf16)
        keep_ref[0] = low[:LONG, :]
        send_ref[0] = low[LONG:, :]
        shifts = column_sum(entire)
        scales = column_sum(entire * normed.astype(f32)) - shifts * row_of(vec_ref, V_O1)
        row_ref[0:1, :] += scales / row_of(vec_ref, V_G1)
        row_ref[1:2, :] += shifts

    if not final:
        put(through)
        return
    last = pl.num_programs(0) - 1

    @pl.when(step < last)
    def _():
        put(through)

    @pl.when(step == last)
    def _():
        query_grad = jnp.concatenate(
            [dq_acc[part].T for part in range(PARTS)], axis=0
        ) * (1.0 / math.sqrt(HEAD))
        low = query_grad.astype(bf16)
        put(through + dot(low, wq[...], 1, 1))
        gq_ref[...] = dot(normed, low, 0, 0)
        side_ref[0:1, :] += column_sum(low.astype(f32))


def long_backward(layout, final, place, e, k, v, kt, normed, q, mine, other, o, linv, weights, vectors, sums, deps):
    tiles = layout.depth
    away = (lambda i: i) if not final else (lambda i: lax.rem(i + 1, tiles))
    turn = lambda i: away(i) if final else tiles + i
    out = jax.ShapeDtypeStruct((tiles, LONG, WIDTH), bf16)
    out_spec = pl.BlockSpec((1, LONG, WIDTH), lambda i, p: (away(i), 0, 0))
    sum_shapes = [
        jax.ShapeDtypeStruct((PARTS, GROUP, CHUNK), f32),
        jax.ShapeDtypeStruct((WIDTH, 2 * GROUP), f32),
        jax.ShapeDtypeStruct((8, WIDTH), f32),
        jax.ShapeDtypeStruct((8, GROUP), f32),
    ]
    sum_specs = [whole(x.shape) for x in sum_shapes]
    return pl.pallas_call(
        behind(functools.partial(long_backward_kernel, final), len(deps)),
        grid_spec=pltpu.PrefetchScalarGridSpec(
            num_scalar_prefetch=1,
            grid=(tiles,),
            in_specs=[ANYWHERE] * len(deps)
            + [
                pl.BlockSpec((TILE, STEPS * CHUNK), lambda i, p: (turn(i), 0)),
                pl.BlockSpec((TILE, GROUP), lambda i, p: (turn(i), 0)),
                pl.BlockSpec((TILE, GROUP), lambda i, p: (turn(i), 0)),
                pl.BlockSpec((GROUP, TILE), lambda i, p: (0, turn(i))),
                pl.BlockSpec((TILE, WIDTH), lambda i, p: (turn(i), 0)),
                whole((TILE, GROUP)),
                whole((CHUNK, GROUP)),
                whole((CHUNK, GROUP)),
                whole((PARTS, GROUP, CHUNK)),
                whole((STEPS * 8, CHUNK)),
                once((WIDTH, 3 * WIDTH)),
                whole(vectors.shape),
            ]
            + sum_specs[: len(sums)],
            out_specs=[out_spec, out_spec, whole((WIDTH, GROUP))] + sum_specs,
            scratch_shapes=[
                pltpu.VMEM((STEPS * CHUNK, GROUP), bf16),
                pltpu.VMEM((STEPS * CHUNK, GROUP), bf16),
                pltpu.VMEM((STEPS * 8, CHUNK), f32),
                pltpu.VMEM((TILE, STEPS * CHUNK), bf16),
                pltpu.VMEM((WIDTH, GROUP), bf16),
                pltpu.VMEM((WIDTH, 2 * GROUP), bf16),
            ],
        ),
        out_shape=[out, out, jax.ShapeDtypeStruct((WIDTH, GROUP), f32)] + sum_shapes,
        compiler_params=pltpu.CompilerParams(**PARAMS),
        cost_estimate=pl.CostEstimate(
            flops=20 * TILE * k.shape[0] * GROUP, bytes_accessed=16 << 20, transcendentals=0
        ),
        name="long_backward_final" if final else "long_backward",
    )(place, *deps, e, k, v, kt, normed, q, mine, other, o, linv, weights, vectors, *sums)


def short_backward_kernel(
    layout, place_ref, e_ref, k_ref, v_ref, q_ref, kt_ref, da_ref, o_ref, linv_ref, n1_ref, x_ref, mid_ref, w_ref,
    vec_ref, gq_ref, gkv_ref, lrow_ref, lside_ref, frow_ref, hsum_ref,
    dx_ref, *refs,
):
    grads = refs[:-9]
    scaled, delta, dblk, qblk, ds_ref, dqt, dqkv, packed, column = refs[-9:]
    step = pl.program_id(0)
    count = k_ref.shape[0]

    @pl.when(step == 0)
    def _():
        for low in range(0, WIDTH, GROUP):
            turned = da_ref[:, low : low + GROUP].astype(f32).T
            product = turned * o_ref[low : low + GROUP, :]
            pieces = []
            for head in range(4):
                span = slice(head * HEAD, (head + 1) * HEAD)
                index = low // HEAD + head
                linv = linv_ref[8 * index : 8 * index + 1, :]
                delta[8 * index : 8 * index + 8, :] = jnp.broadcast_to(
                    column_sum(product[span, :]) * linv, (8, count)
                )
                pieces.append(turned[span, :] * linv)
            scaled[:, low : low + GROUP] = jnp.concatenate(pieces, axis=0).T.astype(bf16)

    def group(side):
        low = side * GROUP
        for head in range(4):
            index = side * 4 + head
            span = slice(head * count, (head + 1) * count)
            own = slice(head * HEAD, (head + 1) * HEAD)
            dblk[span, :] = head_lanes(scaled[:, low : low + GROUP], head)
            qblk[span, :] = head_lanes(q_ref[...], head)
            slopes = dot(v_ref[...], dblk[span, :], 1, 1)
            ds = (
                e_ref[:, span].astype(f32) * (slopes - delta[8 * index : 8 * index + 1, :])
            ).astype(bf16)
            ds_ref[:, span] = ds
            dqt[own, :] = dot(kt_ref[low + head * HEAD : low + (head + 1) * HEAD, :], ds)
        value_grad = dot(e_ref[...], dblk[...])
        key_grad = dot(ds_ref[...], qblk[...])
        query_grad = dqt[...].T * (1.0 / math.sqrt(HEAD))
        dqkv[:, low : low + GROUP] = query_grad.astype(bf16)
        dqkv[:, WIDTH + low : WIDTH + low + GROUP] = key_grad.astype(bf16)
        dqkv[:, 2 * WIDTH + low : 2 * WIDTH + low + GROUP] = value_grad.astype(bf16)

    for side in (0, 1):
        pl.when(step == side)(functools.partial(group, side))

    @pl.when(step == 1)
    def _():
        rows_grad = dot(dqkv[...], w_ref[...], 1, 1)
        standard, inverse = standardize(x_ref[LONG:, :].astype(f32))
        through = norm_backward(rows_grad, standard, inverse, row_of(vec_ref, V_G1))
        dx_ref[...] = (mid_ref[...] + through).astype(bf16)
        core = place_ref[1]
        column[...] = jnp.zeros_like(column)
        column[0:1, :] = column_sum(dqkv[:, :WIDTH].astype(f32))
        column[1:2, :] = column_sum(dqkv[:, 2 * WIDTH :].astype(f32))
        for other in (0, 1):
            @pl.when(core == other)
            def _():
                span = slice(other * GROUP, (other + 1) * GROUP)
                column[0:2, span] += lside_ref[0:2, :]
        column[2:4, :] = frow_ref[0:2, :]
        column[4:5, :] = lrow_ref[0:1, :] + column_sum(rows_grad * standard)
        column[5:6, :] = lrow_ref[1:2, :] + column_sum(rows_grad)
        column[6:8, :] = frow_ref[2:4, :]
        packed[:, 3 * WIDTH :] = column[...].T
        if layout.pieces:
            shard = 4 * layout.rows
            for index in range(layout.shards):
                low = index * layout.rows
                packed[low : low + 1, FIRST - shard :] = hsum_ref[:, index * shard : (index + 1) * shard]
        packed[:, : 3 * WIDTH] = dot(n1_ref[...], dqkv[...], 0, 0)
        for other in (0, 1):
            @pl.when(core == other)
            def _():
                for third in range(3):
                    low = third * WIDTH + other * GROUP
                    extra = gq_ref[...] if third == 0 else gkv_ref[:, (third - 1) * GROUP : third * GROUP]
                    packed[:, low : low + GROUP] += extra

        layout.store_scattered(
            place_ref, grads, lambda block: packed[pl.ds(pl.multiple_of(block * 16, 16), 16), :].astype(bf16)
        )


def short_backward(
    layout, place, e, k, v, q, kt, da, o, linv, n1, rows, mid, weights, vectors, gq, gkv, lrow, lside, frow, hsum, deps
):
    count = k.shape[0]
    half = pl.BlockSpec((count, GROUP), lambda i, _: (0, i))
    grads = layout.scattered_shapes(FIRST)
    return pl.pallas_call(
        behind(functools.partial(short_backward_kernel, layout), len(deps)),
        grid_spec=pltpu.PrefetchScalarGridSpec(
            num_scalar_prefetch=1,
            grid=(2,),
            in_specs=[ANYWHERE] * len(deps)
            + [
                pl.BlockSpec((count, 4 * count), lambda i, _: (0, i)),
                half,
                half,
                half,
                once((WIDTH, count)),
                once((count, WIDTH)),
                once((WIDTH, count)),
                once((HEADS * 8, count)),
                once((count, WIDTH)),
                once(rows.shape),
                once((count, WIDTH)),
                once((WIDTH, 3 * WIDTH)),
                whole(vectors.shape),
                once((WIDTH, GROUP)),
                once((WIDTH, 2 * GROUP)),
                whole((8, WIDTH)),
                whole((8, GROUP)),
                whole((8, WIDTH)),
                whole((1, FF)),
            ],
            out_specs=[once((count, WIDTH))] + [once(g.shape) for g in grads],
            scratch_shapes=[
                pltpu.VMEM((count, WIDTH), bf16),
                pltpu.VMEM((HEADS * 8, count), f32),
                pltpu.VMEM((4 * count, GROUP), bf16),
                pltpu.VMEM((4 * count, GROUP), bf16),
                pltpu.VMEM((count, 4 * count), bf16),
                pltpu.VMEM((GROUP, count), f32),
                pltpu.VMEM((count, 3 * WIDTH), bf16),
                pltpu.VMEM((WIDTH, FIRST), f32),
                pltpu.VMEM((SIDE, WIDTH), f32),
            ],
        ),
        out_shape=[jax.ShapeDtypeStruct((count, WIDTH), bf16)] + grads,
        compiler_params=pltpu.CompilerParams(**PARAMS),
        cost_estimate=pl.CostEstimate(
            flops=24 * count * count * WIDTH, bytes_accessed=18 << 20, transcendentals=0
        ),
        name="short_backward",
    )(place, *deps, e, k, v, q, kt, da, o, linv, n1, rows, mid, weights, vectors, gq, gkv, lrow, lside, frow, hsum)


def per_device(
    incoming_rows,
    picture_label,
    triple_kernel,
    mixer_kernel,
    widening_kernel,
    narrowing_kernel,
    asker_offset,
    content_offset,
    mixer_offset_vector,
    widening_offset,
    narrowing_offset,
    leading_gain,
    leading_offset,
    second_gain,
    second_offset,
    loss_sensitivity,
):
    layout = Layout(lax.axis_size("band"), lax.axis_size("batch"))
    band = lax.axis_index("band")
    rows = incoming_rows[0]
    ids = picture_label[0]
    upstream = loss_sensitivity[0]
    shard = layout.rows
    place = jnp.stack([band // 2, band % 2, band // 4, (band // 2) % 2, lax.axis_index("batch")]).astype(jnp.int32)

    small = (
        asker_offset,
        content_offset,
        mixer_offset_vector,
        narrowing_offset,
        leading_gain,
        leading_offset,
        second_gain,
        second_offset,
    )
    if layout.pieces:
        first_stack = layout.gather_depth(pack_first(triple_kernel, small, widening_offset))
        first_plane = layout.gather_plane(first_stack)
        near = layout.gather_depth(pack_rows(rows, (first_stack,)), tuple(first_plane[1:]))
        first = layout.gather_core(first_plane)
    else:
        near = layout.gather_depth(rows[:LONG])
        columns = [v.astype(bf16)[:, None] for v in small]
        columns += [jnp.zeros((shard, SIDE - 12), bf16), widening_offset.astype(bf16).reshape(shard, 4)]
        first = layout.gather_whole(jnp.concatenate([triple_kernel.astype(bf16)] + columns, axis=1))
        second_stack = layout.gather_whole(
            jnp.concatenate([mixer_kernel.astype(bf16), widening_kernel.astype(bf16)], axis=1)
        )[0]
        narrow = layout.gather_whole(narrowing_kernel.astype(bf16))[0]
        narrow = narrow.reshape(WIDTH // 16, 4, 16, WIDTH).transpose(0, 2, 1, 3).reshape(WIDTH, FF)
        second = [jnp.concatenate([second_stack, narrow], axis=1)]
    far = layout.flip(near, 2)

    n1, q_s, k_s, v_s, kt_s, vt_s, wqkv, vectors, hidden_shift = short_qkv(layout, place, rows, first)
    if layout.pieces:
        packed = pack_second(mixer_kernel, widening_kernel, narrowing_kernel, (n1,))
    else:
        hidden_shift = first[0][:, FIRST - 4 :].reshape(1, FF).astype(f32)
        packed = second[0]
    e_s, o_s, linv_s, att_s = short_forward(q_s, k_s, vt_s, ids[LONG:], (near, packed))
    if layout.pieces:
        second_stack = layout.gather_depth(packed, (linv_s,))
        second_plane = layout.gather_plane(second_stack)
    (far,) = tie([far], (second_stack,))
    stacks = (near, layout.flip(near, 1), far, layout.flip(far, 1))
    n1_l, q_l, k_l, v_l, kt_l, vt_l = long_prepare(layout, place, stacks, wqkv, vectors, (second_stack,))

    e_l, o_l, linv_l, att_keep, att_send = long_forward(q_l, k_l, vt_l)
    if layout.pieces:
        second = layout.gather_core(second_plane[:1] + list(tie(second_plane[1:], (att_keep,))))
    layer_out, mid_l, mid_s, da_keep, da_send, da_s, feed_rows, hidden_sum, *second_grads = feed(
        layout, place, rows, ids, upstream, att_keep, layout.flip(att_send, 1), att_s, vectors, hidden_shift, second
    )
    da_other = layout.flip(da_send, 1)
    inputs = (place, e_l, k_l, v_l, kt_l, n1_l, q_l, da_keep, da_other, o_l, linv_l, wqkv, vectors)

    pairs = layout.scatter_core(second_grads) if layout.pieces else []
    keep_x, send_x, _, *sums = long_backward(layout, False, *inputs, (), tuple(pairs[1:]))
    moved = (keep_x.astype(f32) + layout.flip(send_x, 1).astype(f32)).astype(bf16)
    totals = layout.scatter_plane(pairs) if layout.pieces else []
    keep, send, gq, _, gkv, long_sums, long_side = long_backward(
        layout, True, *inputs, sums, (moved, *totals[1:])
    )
    dx_totals = layout.add_depth([keep, layout.flip(send, 1), layout.flip(moved, 2)])
    dx_s, *first_grads = short_backward(
        layout, place, e_s, k_s, v_s, q_s, kt_s, da_s, o_s, linv_s, n1, rows, mid_s, wqkv, vectors,
        gq, gkv, long_sums, long_side, feed_rows, hidden_sum, tuple(dx_totals[1:]),
    )
    dx_long = layout.scatter_depth(dx_totals, -1)
    if layout.pieces:
        second_grad = layout.scatter_depth(totals)
        narrow_grad = second_grad[:, WIDTH + FF :].reshape(shard, 4, WIDTH).transpose(1, 0, 2)
        narrow_grad = narrow_grad.reshape(4 * shard, WIDTH)
        first_grad = layout.scatter_depth(layout.scatter_plane(layout.scatter_core(first_grads)))
        hidden_grad = first_grad[0, FIRST - 4 * shard :]
    else:
        packed = second_grads[0][:, WIDTH + FF :].reshape(WIDTH // 16, 16, 4, WIDTH).transpose(0, 2, 1, 3)
        narrow_grad = layout.scatter_whole(packed.reshape(FF, WIDTH))
        second_grad = layout.scatter_whole(second_grads[0][:, : WIDTH + FF])
        first_grad = layout.scatter_whole(first_grads[0])
        hidden_grad = layout.scatter_whole(hidden_sum[0])
    small = first_grad[:, 3 * WIDTH :]

    standard, inverse = standardize(rows[:LONG].astype(f32))
    dx_l = (mid_l + norm_backward(dx_long, standard, inverse, vectors[V_G1][None, :])).astype(bf16)
    input_grad = jnp.concatenate([dx_l, dx_s], axis=0)
    return (
        layer_out[None],
        input_grad[None],
        first_grad[:, : 3 * WIDTH],
        second_grad[:, :WIDTH],
        second_grad[:, WIDTH : WIDTH + FF],
        narrow_grad,
        small[:, 0],
        small[:, 1],
        small[:, 2],
        hidden_grad,
        small[:, 3],
        small[:, 4],
        small[:, 5],
        small[:, 6],
        small[:, 7],
    )


def solution(mesh):
    shards = P(("band", "batch"))
    tokens = P("batch", "band", None)
    kernels = P(("band", "batch"), None)
    in_specs = (
        (tokens, P("batch", "band")) + (kernels,) * 4 + (shards,) * 9 + (tokens,)
    )
    out_specs = (tokens, tokens) + (kernels,) * 4 + (shards,) * 9
    return jax.shard_map(
        per_device, mesh=mesh, in_specs=in_specs, out_specs=out_specs, check_vma=False
    )
```

```python
import functools
import math

import jax
import jax.numpy as jnp
from jax import lax
from jax.experimental import pallas as pl
from jax.experimental.pallas import tpu as pltpu
from jax.sharding import PartitionSpec as P

HEADS = 8
HEAD = 64
LONG = 256
WIDTH = 512
FF = 2048
GROUP = 256
TILE = 512
epsilon = 1e-06
gelu_scale = 0.7978845608028654
f32 = jnp.float32
bf16 = jnp.bfloat16
PARAMS = dict(vmem_limit_bytes=58 << 20)


def dot(left, right, cl=1, cr=0):
    return lax.dot_general(left, right, (((cl,), (cr,)), ((), ())), preferred_element_type=f32)


def standardize(rows):
    center = rows - jnp.mean(rows, axis=1, keepdims=True)
    inverse = lax.rsqrt(jnp.mean(center * center, axis=1, keepdims=True) + epsilon)
    return center * inverse, inverse


def norm_backward(incoming, standard, inverse, scaling):
    scaled = incoming * scaling
    return inverse * (
        scaled
        - jnp.mean(scaled, axis=1, keepdims=True)
        - standard * jnp.mean(scaled * standard, axis=1, keepdims=True)
    )


def column_sum(rows):
    return jnp.sum(rows, axis=0, keepdims=True)


def head_lanes(block, head):
    lane = lax.broadcasted_iota(jnp.int32, block.shape, 1) // HEAD
    return jnp.where(lane == head, block.astype(f32), 0.0).astype(bf16)


V_ASK, V_CONTENT, V_MIXER, V_NARROW, V_G1, V_O1, V_G2, V_O2 = range(8)


def row_of(table_ref, index):
    return table_ref[index : index + 1, :]


def whole(shape):
    return pl.BlockSpec(shape, lambda *_: (0,) * len(shape))


def once(shape):
    return pl.BlockSpec(shape, lambda *_: (0,) * len(shape), pipeline_mode=pl.Buffered(1))


ANYWHERE = pl.BlockSpec(memory_space=pl.ANY)


def behind(kernel, count, prefetch=True):
    skip = 1 if prefetch else 0
    return lambda *refs: kernel(*refs[:skip], *refs[skip + count :])


SIDE = 128
FIRST = 3 * WIDTH + SIDE
SECOND = WIDTH + 2 * FF


class Layout:
    def __init__(self, bands, batches):
        self.bands, self.batches = bands, batches
        self.depth = bands // 4
        self.shards = bands * batches
        self.rows = WIDTH // self.shards
        self.pieces = self.rows % 16 == 0
        self.plane = [(kx, ky) for kx in (0, 1) for ky in range(batches)]

    def shard(self, place, kc, kx, ky, kz, sign):
        z = lax.rem(place[2] + (self.depth + sign * kz), self.depth)
        x = lax.rem(place[3] + kx, 2)
        y = lax.rem(place[4] + (self.batches + sign * ky), self.batches)
        core = lax.rem(place[1] + kc, 2)
        return ((z * 2 + x) * 2 + core) * self.batches + y

    def chip(self, place, kx, kz):
        return lax.rem(place[2] + kz, self.depth) * 2 + lax.rem(place[3] + kx, 2)

    def shift_depth(self, block, k):
        pairs = [(i, ((i // 4 + k) % self.depth) * 4 + i % 4) for i in range(self.bands)]
        return lax.ppermute(block, "band", pairs)

    def flip(self, block, bit):
        return lax.ppermute(block, "band", [(i, i ^ bit) for i in range(self.bands)])

    def shift_plane(self, block, kx, ky):
        n = self.batches
        pairs = [
            (b * n + y, (b ^ (2 * kx)) * n + (y + ky) % n) for b in range(self.bands) for y in range(n)
        ]
        return lax.ppermute(block, ("band", "batch"), pairs)

    def gather_depth(self, block, deps=()):
        return stack_blocks([block] + [self.shift_depth(block, k) for k in range(1, self.depth)], deps)

    def gather_plane(self, stack):
        return [stack if k == (0, 0) else self.shift_plane(stack, *k) for k in self.plane]

    def gather_core(self, plane):
        return plane + [self.flip(part, 1) for part in plane]

    def gather_whole(self, block):
        return [lax.all_gather(block, ("band", "batch"), axis=0, tiled=True)]

    def gathered_specs(self, columns):
        if not self.pieces:
            return [once((WIDTH, columns))]
        return [once((self.depth, self.rows, columns))] * (2 * len(self.plane))

    def each_gathered(self, place, refs, visit):
        if not self.pieces:
            for low in range(0, WIDTH, 16):
                visit(low // 16, refs[0][low : low + 16, :])
            return
        index = 0
        for kc in (0, 1):
            for kx, ky in self.plane:
                for kz in range(self.depth):
                    visit(self.shard(place, kc, kx, ky, kz, -1), refs[index][kz])
                index += 1

    def scattered_shapes(self, columns):
        if not self.pieces:
            return [jax.ShapeDtypeStruct((WIDTH, columns), bf16)]
        shape = (len(self.plane), self.depth, self.rows, columns)
        return [jax.ShapeDtypeStruct(shape, bf16)] * 2

    def store_scattered(self, place, refs, take):
        if not self.pieces:
            for low in range(0, WIDTH, 16):
                refs[0][low : low + 16, :] = take(low // 16)
            return
        for kc in (0, 1):
            for n, (kx, ky) in enumerate(self.plane):
                for kz in range(self.depth):
                    refs[kc][n, kz] = take(self.shard(place, kc, kx, ky, kz, 1))

    def scatter_core(self, parts):
        keep, send = parts
        arrived = self.flip(send, 1)
        return [(keep[n].astype(f32) + arrived[n].astype(f32)).astype(bf16) for n in range(len(self.plane))]

    def scatter_plane(self, pairs):
        arrived = [self.shift_plane(pairs[n], *k) for n, k in enumerate(self.plane) if n]
        return self.add_depth(pairs[:1] + arrived)

    def add_depth(self, stacks):
        totals = []
        for k in range(self.depth):
            total = stacks[0][k].astype(f32)
            for stack in stacks[1:]:
                total = total + stack[k].astype(f32)
            totals.append(total if k == 0 else total.astype(bf16))
        return totals

    def scatter_depth(self, totals, sign=1):
        final = totals[0]
        for k in range(1, self.depth):
            final = final + self.shift_depth(totals[k], (sign * k) % self.depth).astype(f32)
        return final

    def scatter_whole(self, part):
        return lax.psum_scatter(part, ("band", "batch"), scatter_dimension=0, tiled=True).astype(f32)


def tie(values, deps):
    count = len(values)
    return pl.pallas_call(
        lambda *refs: None,
        in_specs=[ANYWHERE] * (count + len(deps)),
        out_specs=[ANYWHERE] * count,
        out_shape=[jax.ShapeDtypeStruct(v.shape, v.dtype) for v in values],
        input_output_aliases={i: i for i in range(count)},
        name="tie",
    )(*values, *deps)


def stack_kernel(*refs):
    for index, ref in enumerate(refs[:-1]):
        refs[-1][index] = ref[...]


def stack_blocks(blocks, deps):
    shape = blocks[0].shape
    return pl.pallas_call(
        behind(stack_kernel, len(deps), False),
        in_specs=[ANYWHERE] * len(deps) + [pl.BlockSpec(memory_space=pltpu.VMEM)] * len(blocks),
        out_shape=jax.ShapeDtypeStruct((len(blocks), *shape), blocks[0].dtype),
        name="stack_blocks",
    )(*deps, *blocks)


def pack_first_kernel(triple_ref, *refs):
    vectors, wide, out_ref, table = refs[:8], *refs[8:]
    shard = triple_ref.shape[0]
    table[...] = jnp.zeros_like(table)
    for index, ref in enumerate(vectors):
        table[index : index + 1, :shard] = ref[...]
    out_ref[:, : 3 * WIDTH] = triple_ref[...].astype(bf16)
    turned = table[...].T[:shard, :]
    across = jnp.pad(wide[...], ((0, shard - 1), (SIDE - 4 * shard, 0)))
    out_ref[:, 3 * WIDTH :] = (turned + across).astype(bf16)


def pack_first(triple, vectors, wide):
    shard = triple.shape[0]
    return pl.pallas_call(
        pack_first_kernel,
        out_shape=jax.ShapeDtypeStruct((shard, FIRST), bf16),
        scratch_shapes=[pltpu.VMEM((SIDE, SIDE), f32)],
        compiler_params=pltpu.CompilerParams(**PARAMS),
        name="pack_first",
    )(triple, *[v[None, :] for v in vectors], wide[None, :])


def pack_rows_kernel(rows_ref, out_ref):
    out_ref[...] = rows_ref[...]


def pack_rows(rows, deps):
    block = pl.BlockSpec((LONG, WIDTH), lambda i: (0, 0))
    return pl.pallas_call(
        behind(pack_rows_kernel, len(deps), False),
        grid=(1,),
        in_specs=[ANYWHERE] * len(deps) + [block],
        out_specs=block,
        out_shape=jax.ShapeDtypeStruct((LONG, WIDTH), bf16),
        name="pack_rows",
    )(*deps, rows)


def pack_second_kernel(mixer_ref, widening_ref, narrowing_ref, out_ref):
    shard = mixer_ref.shape[0]
    out_ref[:, :WIDTH] = mixer_ref[...].astype(bf16)
    out_ref[:, WIDTH : WIDTH + FF] = widening_ref[...].astype(bf16)
    for k in range(4):
        low = WIDTH + FF + k * WIDTH
        out_ref[:, low : low + WIDTH] = narrowing_ref[k * shard : (k + 1) * shard, :].astype(bf16)


def pack_second(mixer, widening, narrowing, deps):
    blocks = [pl.BlockSpec(memory_space=pltpu.VMEM)] * 3
    return pl.pallas_call(
        behind(pack_second_kernel, len(deps), False),
        out_shape=jax.ShapeDtypeStruct((mixer.shape[0], SECOND), bf16),
        in_specs=[ANYWHERE] * len(deps) + blocks,
        compiler_params=pltpu.CompilerParams(**PARAMS),
        name="pack_second",
    )(*deps, mixer, widening, narrowing)


def short_qkv_kernel(layout, place_ref, x_ref, *refs):
    count = len(layout.gathered_specs(FIRST))
    pieces = refs[:count]
    n1_ref, q_ref, k_ref, v_ref, kt_ref, vt_ref, w_ref, vec_ref, hid_ref, side, spread = refs[count:]

    @pl.when(pl.program_id(0) == 0)
    def _():
        def visit(block, rows):
            span = pl.ds(pl.multiple_of(block * 16, 16), 16)
            w_ref[span, :] = rows[:, : 3 * WIDTH]
            side[span, :] = rows[:, 3 * WIDTH :].astype(f32)
            if layout.pieces:
                spread[pl.ds(block, 1), :] = rows[0:1, 3 * WIDTH :].astype(f32)

        layout.each_gathered(place_ref, pieces, visit)
        vec_ref[...] = side[...].T[:16, :]
        if layout.pieces:
            shard = 4 * layout.rows
            for index in range(layout.shards):
                hid_ref[:, index * shard : (index + 1) * shard] = spread[index : index + 1, SIDE - shard :]

    standard, _ = standardize(x_ref[...].astype(f32))
    normed = (standard * row_of(vec_ref, V_G1) + row_of(vec_ref, V_O1)).astype(bf16)
    n1_ref[...] = normed
    projected = dot(normed, w_ref[...])
    q = (projected[:, :WIDTH] + row_of(vec_ref, V_ASK)).astype(bf16)
    q_ref[...] = (q.astype(f32) * (1.0 / math.sqrt(HEAD))).astype(bf16)
    k = projected[:, WIDTH : 2 * WIDTH]
    v = projected[:, 2 * WIDTH :] + row_of(vec_ref, V_CONTENT)
    k_ref[...] = k.astype(bf16)
    v_ref[...] = v.astype(bf16)
    kt_ref[...] = k.T.astype(bf16)
    vt_ref[...] = v.T.astype(bf16)


def short_qkv(layout, place, rows, pieces):
    count = rows.shape[0] - LONG
    block = 256
    row_spec = pl.BlockSpec((block, WIDTH), lambda i, _: (i, 0))
    col_spec = pl.BlockSpec((WIDTH, block), lambda i, _: (0, i))
    flat = jax.ShapeDtypeStruct((count, WIDTH), bf16)
    tall = jax.ShapeDtypeStruct((WIDTH, count), bf16)
    return pl.pallas_call(
        functools.partial(short_qkv_kernel, layout),
        grid_spec=pltpu.PrefetchScalarGridSpec(
            num_scalar_prefetch=1,
            grid=(count // block,),
            in_specs=[pl.BlockSpec((block, WIDTH), lambda i, _: (i + LONG // block, 0))]
            + layout.gathered_specs(FIRST),
            out_specs=[row_spec, row_spec, row_spec, row_spec, col_spec, col_spec]
            + [once((WIDTH, 3 * WIDTH)), whole((16, WIDTH)), whole((1, FF))],
            scratch_shapes=[pltpu.VMEM((WIDTH, SIDE), f32), pltpu.VMEM((max(8, layout.shards), SIDE), f32)],
        ),
        out_shape=[flat, flat, flat, flat, tall, tall]
        + [
            jax.ShapeDtypeStruct((WIDTH, 3 * WIDTH), bf16),
            jax.ShapeDtypeStruct((16, WIDTH), f32),
            jax.ShapeDtypeStruct((1, FF), f32),
        ],
        compiler_params=pltpu.CompilerParams(**PARAMS),
        cost_estimate=pl.CostEstimate(
            flops=2 * count * WIDTH * 3 * WIDTH, bytes_accessed=10 << 20, transcendentals=0
        ),
        name="short_qkv",
    )(place, rows, *pieces)


def short_forward_kernel(
    q_ref, k_ref, vt_ref, idc_ref, idr_ref, e_ref, o_ref, linv_ref, att_ref, s_ref, bias_ref, top_ref
):
    step = pl.program_id(0)
    count = k_ref.shape[0]
    tile = count

    @pl.when(step == 0)
    def _():
        same = idc_ref[...] == idr_ref[...]
        bias_ref[...] = jnp.where(same, 0.0, -1e30)

    def first(slot):
        masked = head_lanes(q_ref[...], lax.rem(step, 4))
        top = None
        for low in range(0, count, tile):
            s = dot(k_ref[low : low + tile, :], masked, 1, 1) + bias_ref[low : low + tile, :]
            s_ref[slot, low : low + tile, :] = s
            part = jnp.max(s, axis=0, keepdims=True)
            top = part if top is None else jnp.maximum(top, part)
        top_ref[slot] = jnp.broadcast_to(top, (8, count))

    def second(slot):
        head = step - 1
        top = top_ref[slot, 0:1, :]
        mixed = jnp.zeros((HEAD, count), f32)
        total = jnp.zeros((1, count), f32)
        for low in range(0, count, tile):
            e = jnp.exp(s_ref[slot, low : low + tile, :] - top)
            total += column_sum(e)
            low_e = e.astype(bf16)
            e_ref[low : low + tile, :] = low_e
            mixed += dot(vt_ref[pl.ds(pl.multiple_of(head * HEAD, HEAD), HEAD), low : low + tile], low_e)
        linv = 1.0 / total
        linv_ref[...] = jnp.broadcast_to(linv, (8, count))
        o_ref[pl.ds(pl.multiple_of(head * HEAD, HEAD), HEAD), :] = mixed * linv

    last = pl.num_programs(0) - 1

    @pl.when(step == 0)
    def _():
        first(0)

    for parity in (0, 1):
        @pl.when((step > 0) & (step < last) & (lax.rem(step, 2) == parity))
        def _():
            first(parity)
            second(1 - parity)

    @pl.when(step == last)
    def _():
        second((HEADS - 1) % 2)
        for low in range(0, WIDTH, 128):
            att_ref[:, low : low + 128] = o_ref[low : low + 128, :].T.astype(bf16)


def short_forward(q, k, vt, ids, deps):
    count = q.shape[0]
    now = lambda s: (0, jnp.minimum(s, HEADS - 1) // 4)
    before = lambda s: (0, jnp.maximum(s - 1, 0))
    return pl.pallas_call(
        behind(short_forward_kernel, len(deps), False),
        grid=(HEADS + 1,),
        in_specs=[ANYWHERE] * len(deps)
        + [
            pl.BlockSpec((count, GROUP), now),
            pl.BlockSpec((count, GROUP), now),
            whole((WIDTH, count)),
            whole((count, 1)),
            whole((1, count)),
        ],
        out_specs=[
            pl.BlockSpec((count, count), before),
            whole((WIDTH, count)),
            pl.BlockSpec((8, count), lambda s: (jnp.maximum(s - 1, 0), 0)),
            whole((count, WIDTH)),
        ],
        out_shape=[
            jax.ShapeDtypeStruct((count, HEADS * count), bf16),
            jax.ShapeDtypeStruct((WIDTH, count), f32),
            jax.ShapeDtypeStruct((HEADS * 8, count), f32),
            jax.ShapeDtypeStruct((count, WIDTH), bf16),
        ],
        scratch_shapes=[
            pltpu.VMEM((2, count, count), f32),
            pltpu.VMEM((count, count), f32),
            pltpu.VMEM((2, 8, count), f32),
        ],
        compiler_params=pltpu.CompilerParams(**PARAMS),
        cost_estimate=pl.CostEstimate(
            flops=12 * count * count * WIDTH, bytes_accessed=12 << 20, transcendentals=HEADS * count * count
        ),
        name="short_forward",
    )(*deps, q, k, vt, ids[:, None], ids[None, :])


CHIPS = 2


def long_prepare_kernel(
    depth, place_ref, own0, other0, own1, other1, w_ref, vec_ref, n1_ref, q_ref, k_ref, vt_ref,
    wk, wv,
):
    step = pl.program_id(0)
    core = place_ref[1]
    near = step < depth
    lanes = lambda base: pl.ds(pl.multiple_of(base + core * GROUP, GROUP), GROUP)

    @pl.when(step == 0)
    def _():
        for other in (0, 1):
            @pl.when(core == other)
            def _():
                wk[...] = w_ref[:, WIDTH + other * GROUP : WIDTH + (other + 1) * GROUP]
                wv[...] = w_ref[:, 2 * WIDTH + other * GROUP : 2 * WIDTH + (other + 1) * GROUP]

    chips = own0.shape[0]
    rows = jnp.concatenate(
        [jnp.where(near, a[chip], b[chip]) for chip in range(chips) for a, b in ((own0, own1), (other0, other1))],
        axis=0,
    )
    standard, _ = standardize(rows.astype(f32))
    normed = (standard * row_of(vec_ref, V_G1) + row_of(vec_ref, V_O1)).astype(bf16)
    n1_ref[...] = normed
    k = dot(normed, wk[...])
    v = dot(normed, wv[...]) + vec_ref[V_CONTENT : V_CONTENT + 1, lanes(0)]
    k_ref[...] = k.astype(bf16)
    vt_ref[...] = v.astype(bf16).T

    @pl.when(step == 0)
    def _():
        q = (dot(normed[:TILE, :], w_ref[:, lanes(0)]) + vec_ref[V_ASK : V_ASK + 1, lanes(0)]).astype(bf16)
        q_ref[...] = (q.astype(f32) * (1.0 / math.sqrt(HEAD))).astype(bf16)


def long_prepare(layout, place, stacks, weights, vectors, deps):
    depth = layout.depth
    total = 2 * depth * TILE
    steps = depth // CHIPS
    tile = CHIPS * TILE
    row_spec = pl.BlockSpec((tile, GROUP), lambda i, _: (i, 0))
    col_spec = pl.BlockSpec((GROUP, tile), lambda i, _: (0, i))
    near = pl.BlockSpec((CHIPS, LONG, WIDTH), lambda i, _: (jnp.minimum(i, steps - 1), 0, 0))
    far = pl.BlockSpec((CHIPS, LONG, WIDTH), lambda i, _: (jnp.maximum(i - steps, 0), 0, 0))
    flat = jax.ShapeDtypeStruct((total, GROUP), bf16)
    tall = jax.ShapeDtypeStruct((GROUP, total), bf16)
    return pl.pallas_call(
        behind(functools.partial(long_prepare_kernel, depth // CHIPS), len(deps)),
        grid_spec=pltpu.PrefetchScalarGridSpec(
            num_scalar_prefetch=1,
            grid=(2 * steps,),
            in_specs=[ANYWHERE] * len(deps)
            + [near, near, far, far, whole((WIDTH, 3 * WIDTH)), whole(vectors.shape)],
            out_specs=[
                pl.BlockSpec((tile, WIDTH), lambda i, _: (i, 0)),
                whole((TILE, GROUP)),
                row_spec,
                col_spec,
            ],
            scratch_shapes=[pltpu.VMEM((WIDTH, GROUP), bf16)] * 2,
        ),
        out_shape=[
            jax.ShapeDtypeStruct((total, WIDTH), bf16),
            jax.ShapeDtypeStruct((TILE, GROUP), bf16),
            flat,
            tall,
        ],
        compiler_params=pltpu.CompilerParams(**PARAMS),
        cost_estimate=pl.CostEstimate(
            flops=4 * total * WIDTH * GROUP, bytes_accessed=18 << 20, transcendentals=0
        ),
        name="long_prepare",
    )(place, *deps, *stacks, weights, vectors)


CHUNK = 256
BACK = 2 * TILE
PARTS = TILE // CHUNK
LOCAL_HEADS = GROUP // HEAD
STEPS = LOCAL_HEADS * PARTS


def long_forward_kernel(
    q_ref, k_ref, vt_ref, e_ref, o_ref, linv_ref, keep_ref, send_ref, s_ref, top_ref
):
    step = pl.program_id(0)
    total = k_ref.shape[0]
    tile = min(total, 4096)
    last = pl.num_programs(0) - 1

    def masked_queries():
        rows = pl.ds(pl.multiple_of(lax.rem(step, PARTS) * CHUNK, CHUNK), CHUNK)
        return head_lanes(q_ref[rows, :], step // PARTS)

    def first_tile(slot, low, masked, top):
        s = dot(k_ref[pl.ds(low, tile), :], masked, 1, 1)
        s_ref[slot, pl.ds(low, tile), :] = s
        return jnp.maximum(top, jnp.max(s.reshape(tile // 8, 8, CHUNK), axis=0))

    def second_tile(slot, low, top, head, carry):
        summed, mixed = carry
        e = jnp.exp(s_ref[slot, pl.ds(low, tile), :] - top)
        summed = summed + jnp.sum(e.reshape(tile // 8, 8, CHUNK), axis=0)
        low_e = e.astype(bf16)
        e_ref[pl.ds(low, tile), :] = low_e
        values = vt_ref[pl.ds(pl.multiple_of(head * HEAD, HEAD), HEAD), pl.ds(low, tile)]
        return summed, mixed + dot(values, low_e)

    start_top = jnp.full((8, CHUNK), -1e30, f32)
    start_sum = (jnp.zeros((8, CHUNK), f32), jnp.zeros((HEAD, CHUNK), f32))

    def finish(head, part, carry):
        summed, mixed = carry
        linv = 1.0 / column_sum(summed)
        linv_ref[...] = jnp.broadcast_to(linv, (8, CHUNK))
        o_ref[part, pl.ds(pl.multiple_of(head * HEAD, HEAD), HEAD), :] = mixed * linv

    def place(turn):
        return pl.multiple_of(turn * tile, tile)

    @pl.when(step == 0)
    def _():
        masked = masked_queries()
        top_ref[0] = lax.fori_loop(
            0, total // tile, lambda t, top: first_tile(0, place(t), masked, top), start_top
        )

    for parity in (0, 1):
        @pl.when((step > 0) & (step < last) & (lax.rem(step, 2) == parity))
        def _():
            masked = masked_queries()
            before = step - 1
            head = before // PARTS
            top_row = jnp.max(top_ref[1 - parity], axis=0, keepdims=True)

            def body(turn, carry):
                top, kept = carry
                low = place(turn)
                top = first_tile(parity, low, masked, top)
                kept = second_tile(1 - parity, low, top_row, head, kept)
                return top, kept

            top, kept = lax.fori_loop(0, total // tile, body, (start_top, start_sum))
            top_ref[parity] = top
            finish(head, lax.rem(before, PARTS), kept)

    @pl.when(step == last)
    def _():
        slot = (STEPS - 1) % 2
        top_row = jnp.max(top_ref[slot], axis=0, keepdims=True)
        head = LOCAL_HEADS - 1
        kept = lax.fori_loop(
            0,
            total // tile,
            lambda t, carry: second_tile(slot, place(t), top_row, head, carry),
            start_sum,
        )
        finish(head, PARTS - 1, kept)
        keep_ref[...] = o_ref[0].T.astype(bf16)
        send_ref[...] = o_ref[1].T.astype(bf16)


def long_forward(q, k, vt):
    total = k.shape[0]
    before = lambda s: jnp.maximum(s - 1, 0)
    half = jax.ShapeDtypeStruct((CHUNK, GROUP), bf16)
    return pl.pallas_call(
        long_forward_kernel,
        grid=(STEPS + 1,),
        in_specs=[once((TILE, GROUP)), once((total, GROUP)), once((GROUP, total))],
        out_specs=[
            pl.BlockSpec((total, CHUNK), lambda s: (0, before(s))),
            whole((PARTS, GROUP, CHUNK)),
            pl.BlockSpec((8, CHUNK), lambda s: (before(s), 0)),
            whole((CHUNK, GROUP)),
            whole((CHUNK, GROUP)),
        ],
        scratch_shapes=[pltpu.VMEM((2, total, CHUNK), f32), pltpu.VMEM((2, 8, CHUNK), f32)],
        out_shape=[
            jax.ShapeDtypeStruct((total, STEPS * CHUNK), bf16),
            jax.ShapeDtypeStruct((PARTS, GROUP, CHUNK), f32),
            jax.ShapeDtypeStruct((STEPS * 8, CHUNK), f32),
            half,
            half,
        ],
        compiler_params=pltpu.CompilerParams(**PARAMS),
        cost_estimate=pl.CostEstimate(
            flops=16 * TILE * total * GROUP, bytes_accessed=24 << 20, transcendentals=4 * TILE * total
        ),
        name="long_forward",
    )(q, k, vt)


def feed_kernel(layout, place_ref, x_ref, ids_ref, g_ref, mine_ref, other_ref, short_ref, vec_ref, hid_ref, *refs):
    count = len(layout.gathered_specs(SECOND))
    pieces, refs = refs[:count], refs[count:]
    out_ref, midl_ref, mids_ref, keep_ref, send_ref, das_ref, row_ref, hsum_ref = refs[:8]
    grads = refs[8:-8]
    wp_ref, we_ref, wr_ref, gp_ref, ge_ref, gr_ref, act_ref, dh_ref = refs[-8:]
    swapped = place_ref[1] == 1

    def visit(block, rows):
        span = pl.ds(pl.multiple_of(block * 16, 16), 16)
        wp_ref[span, :] = rows[:, :WIDTH]
        we_ref[span, :] = rows[:, WIDTH : WIDTH + FF]
        for k in range(4):
            low = WIDTH + FF + k * WIDTH
            wr_ref[pl.ds(pl.multiple_of(block * 64 + 16 * k, 16), 16), :] = rows[:, low : low + WIDTH]

    layout.each_gathered(place_ref, pieces, visit)

    x = x_ref[...].astype(f32)
    live = (ids_ref[...] >= 0).astype(f32)
    upstream = g_ref[...].astype(f32)
    mine, other = mine_ref[...], other_ref[...]
    long = jnp.concatenate([jnp.where(swapped, other, mine), jnp.where(swapped, mine, other)], axis=1)
    attended = jnp.concatenate([long, short_ref[...]], axis=0)
    branch = dot(attended, wp_ref[...]) + row_of(vec_ref, V_MIXER)
    middle = x + live * branch
    standard, inverse = standardize(middle)
    gain = row_of(vec_ref, V_G2)
    normed = (standard * gain + row_of(vec_ref, V_O2)).astype(bf16)
    branch_low = (live * upstream).astype(bf16)

    part = 256

    def products(low):
        return (
            dot(normed, we_ref[:, low : low + part]) + hid_ref[:, low : low + part],
            dot(branch_low, wr_ref[low : low + part, :], 1, 1),
        )

    following = products(0)
    for low in range(0, FF, part):
        hidden, into = following
        if low + part < FF:
            following = products(low + part)
        square = hidden * hidden
        tangent = jnp.tanh(hidden * (gelu_scale + (gelu_scale * 0.044715) * square))
        half = 0.5 + 0.5 * tangent
        active = (hidden * half).astype(bf16)
        slope = half + (0.5 * hidden) * (1.0 - tangent * tangent) * (
            gelu_scale + (gelu_scale * 3.0 * 0.044715) * square
        )
        hidden_low = (into * slope).astype(bf16)
        hsum_ref[:, low : low + part] = column_sum(hidden_low.astype(f32))
        act_ref[:, low : low + part] = active
        dh_ref[:, low : low + part] = hidden_low
        gr_ref[low : low + part, :] = dot(active, branch_low, 0, 0).astype(bf16)
        ge_ref[:, low : low + part] = dot(normed, hidden_low, 0, 0).astype(bf16)

    branch_two = dot(act_ref[...], wr_ref[...]) + row_of(vec_ref, V_NARROW)
    out_ref[...] = (middle + live * branch_two).astype(bf16)
    normed_grad = dot(dh_ref[...], we_ref[...], 1, 1)
    middle_grad = upstream + norm_backward(normed_grad, standard, inverse, gain)
    midl_ref[...] = middle_grad[:LONG, :]
    mids_ref[...] = middle_grad[LONG:, :]
    attn_low = (live * middle_grad).astype(bf16)
    attended_grad = dot(attn_low, wp_ref[...], 1, 1).astype(bf16)
    das_ref[...] = attended_grad[LONG:, :]
    left, right = attended_grad[:LONG, :GROUP], attended_grad[:LONG, GROUP:]
    keep_ref[...] = jnp.where(swapped, right, left)
    send_ref[...] = jnp.where(swapped, left, right)
    gp_ref[...] = dot(attended, attn_low, 0, 0).astype(bf16)
    row_ref[...] = jnp.zeros_like(row_ref)
    row_ref[0:1, :] = column_sum(attn_low.astype(f32))
    row_ref[1:2, :] = column_sum(branch_low.astype(f32))
    row_ref[2:3, :] = column_sum(normed_grad * standard)
    row_ref[3:4, :] = column_sum(normed_grad)

    def take(block):
        span = pl.ds(pl.multiple_of(block * 16, 16), 16)
        parts = [gp_ref[span, :], ge_ref[span, :]] + [
            gr_ref[pl.ds(pl.multiple_of(block * 64 + 16 * k, 16), 16), :] for k in range(4)
        ]
        return jnp.concatenate(parts, axis=1)

    layout.store_scattered(place_ref, grads, take)


def feed(layout, place, rows, ids, upstream, mine, other, short, vectors, hidden_shift, pieces):
    count = rows.shape[0]
    grads = layout.scattered_shapes(SECOND)
    operands = [rows, ids[:, None], upstream, mine, other, short, vectors, hidden_shift]
    shapes = [
        jax.ShapeDtypeStruct((count, WIDTH), bf16),
        jax.ShapeDtypeStruct((LONG, WIDTH), f32),
        jax.ShapeDtypeStruct((count - LONG, WIDTH), f32),
        jax.ShapeDtypeStruct((LONG, GROUP), bf16),
        jax.ShapeDtypeStruct((LONG, GROUP), bf16),
        jax.ShapeDtypeStruct((count - LONG, WIDTH), bf16),
        jax.ShapeDtypeStruct((8, WIDTH), f32),
        jax.ShapeDtypeStruct((1, FF), f32),
    ] + grads
    return pl.pallas_call(
        functools.partial(feed_kernel, layout),
        grid_spec=pltpu.PrefetchScalarGridSpec(
            num_scalar_prefetch=1,
            grid=(1,),
            in_specs=[once(x.shape) for x in operands] + layout.gathered_specs(SECOND),
            out_specs=[once(x.shape) for x in shapes],
            scratch_shapes=[
                pltpu.VMEM((WIDTH, WIDTH), bf16),
                pltpu.VMEM((WIDTH, FF), bf16),
                pltpu.VMEM((FF, WIDTH), bf16),
                pltpu.VMEM((WIDTH, WIDTH), bf16),
                pltpu.VMEM((WIDTH, FF), bf16),
                pltpu.VMEM((FF, WIDTH), bf16),
                pltpu.VMEM((count, FF), bf16),
                pltpu.VMEM((count, FF), bf16),
            ],
        ),
        out_shape=shapes,
        compiler_params=pltpu.CompilerParams(**PARAMS),
        cost_estimate=pl.CostEstimate(
            flops=6 * count * WIDTH * (WIDTH + 2 * FF), bytes_accessed=18 << 20, transcendentals=count * FF
        ),
        name="feed",
    )(place, *operands, *pieces)


def long_backward_kernel(
    final, place_ref, e_ref, k_ref, vt_ref, n1_ref, q_ref, mine_ref, other_ref, o_ref, linv_ref, w_ref, vec_ref,
    *refs,
):
    if final:
        dq_in, gkv_in, row_in, side_in, *refs = refs
    (
    keep_ref, send_ref, gq_ref, dq_acc, gkv_ref, row_ref, side_ref,
    qblk, dblk, delta, ds_ref, wq, wkv,
    ) = refs
    step = pl.program_id(0)
    core = place_ref[1]

    @pl.when(step == 0)
    def _():
        lanes = lambda base: pl.ds(pl.multiple_of(base + core * GROUP, GROUP), GROUP)
        wq[...] = w_ref[:, lanes(0)]
        wkv[:, :GROUP] = w_ref[:, lanes(WIDTH)]
        wkv[:, GROUP:] = w_ref[:, lanes(2 * WIDTH)]
        if final:
            dq_acc[...] = dq_in[...]
            gkv_ref[...] = gkv_in[...]
            row_ref[...] = row_in[...]
            side_ref[...] = side_in[...]
        else:
            for ref in (dq_acc, gkv_ref, row_ref, side_ref):
                ref[...] = jnp.zeros_like(ref)
        for part in range(PARTS):
            rows = slice(part * CHUNK, (part + 1) * CHUNK)
            turned = (mine_ref, other_ref)[part][...].astype(f32).T
            product = turned * o_ref[part]
            pieces = []
            for head in range(LOCAL_HEADS):
                index = head * PARTS + part
                span = slice(head * HEAD, (head + 1) * HEAD)
                linv = linv_ref[8 * index : 8 * index + 1, :]
                delta[8 * index : 8 * index + 8, :] = jnp.broadcast_to(
                    column_sum(product[span, :]) * linv, (8, CHUNK)
                )
                pieces.append(turned[span, :] * linv)
            scaled = jnp.concatenate(pieces, axis=0).T
            for head in range(LOCAL_HEADS):
                index = head * PARTS + part
                span = slice(index * CHUNK, (index + 1) * CHUNK)
                dblk[span, :] = head_lanes(scaled, head)
                qblk[span, :] = head_lanes(q_ref[rows, :], head)

    def span_of(index):
        return slice(index * CHUNK, (index + 1) * CHUNK)

    v = vt_ref[...].T
    kt = k_ref[...].T
    slopes = dot(v, dblk[span_of(0), :], 1, 1)
    for index in range(STEPS):
        head, part = index // PARTS, index % PARTS
        span = span_of(index)
        following = dot(v, dblk[span_of(index + 1), :], 1, 1) if index + 1 < STEPS else None
        ds = (
            e_ref[:, span].astype(f32) * (slopes - delta[8 * index : 8 * index + 1, :])
        ).astype(bf16)
        ds_ref[:, span] = ds
        own = slice(head * HEAD, (head + 1) * HEAD)
        dq_acc[part, own, :] += dot(kt[own, :], ds)
        slopes = following

    value_grad = dot(e_ref[...], dblk[...]).astype(bf16)
    key_grad = dot(ds_ref[...], qblk[...]).astype(bf16)
    both = jnp.concatenate([key_grad, value_grad], axis=1)
    normed = n1_ref[...]
    through = dot(both, wkv[...], 1, 1)
    gkv_ref[...] += dot(normed, both, 0, 0)
    side_ref[1:2, :] += column_sum(value_grad.astype(f32))

    def put(entire):
        low = entire.astype(bf16)
        for chip in range(BACK // TILE):
            base = chip * TILE
            keep_ref[chip] = low[base : base + LONG, :]
            send_ref[chip] = low[base + LONG : base + TILE, :]
        shifts = column_sum(entire)
        scales = column_sum(entire * normed.astype(f32)) - shifts * row_of(vec_ref, V_O1)
        row_ref[0:1, :] += scales / row_of(vec_ref, V_G1)
        row_ref[1:2, :] += shifts

    if not final:
        put(through)
        return
    last = pl.num_programs(0) - 1

    @pl.when(step < last)
    def _():
        put(through)

    @pl.when(step == last)
    def _():
        query_grad = jnp.concatenate(
            [dq_acc[part].T for part in range(PARTS)], axis=0
        ) * (1.0 / math.sqrt(HEAD))
        low = query_grad.astype(bf16)
        put(jnp.concatenate([through[:TILE, :] + dot(low, wq[...], 1, 1), through[TILE:, :]], axis=0))
        gq_ref[...] = dot(normed[:TILE, :], low, 0, 0)
        side_ref[0:1, :] += column_sum(low.astype(f32))


def long_backward(layout, final, place, e, k, vt, normed, q, mine, other, o, linv, weights, vectors, sums, deps):
    tiles = layout.depth * TILE // BACK
    away = (lambda i: i) if not final else (lambda i: lax.rem(i + 1, tiles))
    turn = lambda i: away(i) if final else tiles + i
    out = jax.ShapeDtypeStruct((layout.depth, LONG, WIDTH), bf16)
    out_spec = pl.BlockSpec((BACK // TILE, LONG, WIDTH), lambda i, p: (away(i), 0, 0))
    sum_shapes = [
        jax.ShapeDtypeStruct((PARTS, GROUP, CHUNK), f32),
        jax.ShapeDtypeStruct((WIDTH, 2 * GROUP), f32),
        jax.ShapeDtypeStruct((8, WIDTH), f32),
        jax.ShapeDtypeStruct((8, GROUP), f32),
    ]
    sum_specs = [whole(x.shape) for x in sum_shapes]
    return pl.pallas_call(
        behind(functools.partial(long_backward_kernel, final), len(deps)),
        grid_spec=pltpu.PrefetchScalarGridSpec(
            num_scalar_prefetch=1,
            grid=(tiles,),
            in_specs=[ANYWHERE] * len(deps)
            + [
                pl.BlockSpec((BACK, STEPS * CHUNK), lambda i, p: (turn(i), 0)),
                pl.BlockSpec((BACK, GROUP), lambda i, p: (turn(i), 0)),
                pl.BlockSpec((GROUP, BACK), lambda i, p: (0, turn(i))),
                pl.BlockSpec((BACK, WIDTH), lambda i, p: (turn(i), 0)),
                whole((TILE, GROUP)),
                whole((CHUNK, GROUP)),
                whole((CHUNK, GROUP)),
                whole((PARTS, GROUP, CHUNK)),
                whole((STEPS * 8, CHUNK)),
                once((WIDTH, 3 * WIDTH)),
                whole(vectors.shape),
            ]
            + sum_specs[: len(sums)],
            out_specs=[out_spec, out_spec, whole((WIDTH, GROUP))] + sum_specs,
            scratch_shapes=[
                pltpu.VMEM((STEPS * CHUNK, GROUP), bf16),
                pltpu.VMEM((STEPS * CHUNK, GROUP), bf16),
                pltpu.VMEM((STEPS * 8, CHUNK), f32),
                pltpu.VMEM((BACK, STEPS * CHUNK), bf16),
                pltpu.VMEM((WIDTH, GROUP), bf16),
                pltpu.VMEM((WIDTH, 2 * GROUP), bf16),
            ],
        ),
        out_shape=[out, out, jax.ShapeDtypeStruct((WIDTH, GROUP), f32)] + sum_shapes,
        compiler_params=pltpu.CompilerParams(**PARAMS),
        cost_estimate=pl.CostEstimate(
            flops=20 * TILE * k.shape[0] * GROUP, bytes_accessed=16 << 20, transcendentals=0
        ),
        name="long_backward_final" if final else "long_backward",
    )(place, *deps, e, k, vt, normed, q, mine, other, o, linv, weights, vectors, *sums)


def short_backward_kernel(
    layout, place_ref, e_ref, k_ref, v_ref, q_ref, kt_ref, da_ref, o_ref, linv_ref, n1_ref, x_ref, mid_ref, w_ref,
    vec_ref, gq_ref, gkv_ref, lrow_ref, lside_ref, frow_ref, hsum_ref,
    dx_ref, *refs,
):
    grads = refs[:-9]
    scaled, delta, dblk, qblk, ds_ref, dqt, dqkv, packed, column = refs[-9:]
    step = pl.program_id(0)
    count = k_ref.shape[0]

    @pl.when(step == 0)
    def _():
        for low in range(0, WIDTH, GROUP):
            turned = da_ref[:, low : low + GROUP].astype(f32).T
            product = turned * o_ref[low : low + GROUP, :]
            pieces = []
            for head in range(4):
                span = slice(head * HEAD, (head + 1) * HEAD)
                index = low // HEAD + head
                linv = linv_ref[8 * index : 8 * index + 1, :]
                delta[8 * index : 8 * index + 8, :] = jnp.broadcast_to(
                    column_sum(product[span, :]) * linv, (8, count)
                )
                pieces.append(turned[span, :] * linv)
            scaled[:, low : low + GROUP] = jnp.concatenate(pieces, axis=0).T.astype(bf16)

    def group(side):
        low = side * GROUP
        for head in range(4):
            index = side * 4 + head
            span = slice(head * count, (head + 1) * count)
            own = slice(head * HEAD, (head + 1) * HEAD)
            dblk[span, :] = head_lanes(scaled[:, low : low + GROUP], head)
            qblk[span, :] = head_lanes(q_ref[...], head)
            slopes = dot(v_ref[...], dblk[span, :], 1, 1)
            ds = (
                e_ref[:, span].astype(f32) * (slopes - delta[8 * index : 8 * index + 1, :])
            ).astype(bf16)
            ds_ref[:, span] = ds
            dqt[own, :] = dot(kt_ref[low + head * HEAD : low + (head + 1) * HEAD, :], ds)
        value_grad = dot(e_ref[...], dblk[...])
        key_grad = dot(ds_ref[...], qblk[...])
        query_grad = dqt[...].T * (1.0 / math.sqrt(HEAD))
        dqkv[:, low : low + GROUP] = query_grad.astype(bf16)
        dqkv[:, WIDTH + low : WIDTH + low + GROUP] = key_grad.astype(bf16)
        dqkv[:, 2 * WIDTH + low : 2 * WIDTH + low + GROUP] = value_grad.astype(bf16)

    for side in (0, 1):
        pl.when(step == side)(functools.partial(group, side))

    @pl.when(step == 1)
    def _():
        rows_grad = dot(dqkv[...], w_ref[...], 1, 1)
        standard, inverse = standardize(x_ref[LONG:, :].astype(f32))
        through = norm_backward(rows_grad, standard, inverse, row_of(vec_ref, V_G1))
        dx_ref[...] = (mid_ref[...] + through).astype(bf16)
        core = place_ref[1]
        column[...] = jnp.zeros_like(column)
        column[0:1, :] = column_sum(dqkv[:, :WIDTH].astype(f32))
        column[1:2, :] = column_sum(dqkv[:, 2 * WIDTH :].astype(f32))
        for other in (0, 1):
            @pl.when(core == other)
            def _():
                span = slice(other * GROUP, (other + 1) * GROUP)
                column[0:2, span] += lside_ref[0:2, :]
        column[2:4, :] = frow_ref[0:2, :]
        column[4:5, :] = lrow_ref[0:1, :] + column_sum(rows_grad * standard)
        column[5:6, :] = lrow_ref[1:2, :] + column_sum(rows_grad)
        column[6:8, :] = frow_ref[2:4, :]
        packed[:, 3 * WIDTH :] = column[...].T
        if layout.pieces:
            shard = 4 * layout.rows
            for index in range(layout.shards):
                low = index * layout.rows
                packed[low : low + 1, FIRST - shard :] = hsum_ref[:, index * shard : (index + 1) * shard]
        packed[:, : 3 * WIDTH] = dot(n1_ref[...], dqkv[...], 0, 0)
        for other in (0, 1):
            @pl.when(core == other)
            def _():
                for third in range(3):
                    low = third * WIDTH + other * GROUP
                    extra = gq_ref[...] if third == 0 else gkv_ref[:, (third - 1) * GROUP : third * GROUP]
                    packed[:, low : low + GROUP] += extra

        layout.store_scattered(
            place_ref, grads, lambda block: packed[pl.ds(pl.multiple_of(block * 16, 16), 16), :].astype(bf16)
        )


def short_backward(
    layout, place, e, k, v, q, kt, da, o, linv, n1, rows, mid, weights, vectors, gq, gkv, lrow, lside, frow, hsum, deps
):
    count = k.shape[0]
    half = pl.BlockSpec((count, GROUP), lambda i, _: (0, i))
    grads = layout.scattered_shapes(FIRST)
    return pl.pallas_call(
        behind(functools.partial(short_backward_kernel, layout), len(deps)),
        grid_spec=pltpu.PrefetchScalarGridSpec(
            num_scalar_prefetch=1,
            grid=(2,),
            in_specs=[ANYWHERE] * len(deps)
            + [
                pl.BlockSpec((count, 4 * count), lambda i, _: (0, i)),
                half,
                half,
                half,
                once((WIDTH, count)),
                once((count, WIDTH)),
                once((WIDTH, count)),
                once((HEADS * 8, count)),
                once((count, WIDTH)),
                once(rows.shape),
                once((count, WIDTH)),
                once((WIDTH, 3 * WIDTH)),
                whole(vectors.shape),
                once((WIDTH, GROUP)),
                once((WIDTH, 2 * GROUP)),
                whole((8, WIDTH)),
                whole((8, GROUP)),
                whole((8, WIDTH)),
                whole((1, FF)),
            ],
            out_specs=[once((count, WIDTH))] + [once(g.shape) for g in grads],
            scratch_shapes=[
                pltpu.VMEM((count, WIDTH), bf16),
                pltpu.VMEM((HEADS * 8, count), f32),
                pltpu.VMEM((4 * count, GROUP), bf16),
                pltpu.VMEM((4 * count, GROUP), bf16),
                pltpu.VMEM((count, 4 * count), bf16),
                pltpu.VMEM((GROUP, count), f32),
                pltpu.VMEM((count, 3 * WIDTH), bf16),
                pltpu.VMEM((WIDTH, FIRST), f32),
                pltpu.VMEM((SIDE, WIDTH), f32),
            ],
        ),
        out_shape=[jax.ShapeDtypeStruct((count, WIDTH), bf16)] + grads,
        compiler_params=pltpu.CompilerParams(**PARAMS),
        cost_estimate=pl.CostEstimate(
            flops=24 * count * count * WIDTH, bytes_accessed=18 << 20, transcendentals=0
        ),
        name="short_backward",
    )(place, *deps, e, k, v, q, kt, da, o, linv, n1, rows, mid, weights, vectors, gq, gkv, lrow, lside, frow, hsum)


def per_device(
    incoming_rows,
    picture_label,
    triple_kernel,
    mixer_kernel,
    widening_kernel,
    narrowing_kernel,
    asker_offset,
    content_offset,
    mixer_offset_vector,
    widening_offset,
    narrowing_offset,
    leading_gain,
    leading_offset,
    second_gain,
    second_offset,
    loss_sensitivity,
):
    layout = Layout(lax.axis_size("band"), lax.axis_size("batch"))
    band = lax.axis_index("band")
    rows = incoming_rows[0]
    ids = picture_label[0]
    upstream = loss_sensitivity[0]
    shard = layout.rows
    place = jnp.stack([band // 2, band % 2, band // 4, (band // 2) % 2, lax.axis_index("batch")]).astype(jnp.int32)

    small = (
        asker_offset,
        content_offset,
        mixer_offset_vector,
        narrowing_offset,
        leading_gain,
        leading_offset,
        second_gain,
        second_offset,
    )
    if layout.pieces:
        first_stack = layout.gather_depth(pack_first(triple_kernel, small, widening_offset))
        first_plane = layout.gather_plane(first_stack)
        near = layout.gather_depth(pack_rows(rows, (first_stack,)), tuple(first_plane[1:]))
        first = layout.gather_core(first_plane)
    else:
        near = layout.gather_depth(rows[:LONG])
        columns = [v.astype(bf16)[:, None] for v in small]
        columns += [jnp.zeros((shard, SIDE - 12), bf16), widening_offset.astype(bf16).reshape(shard, 4)]
        first = layout.gather_whole(jnp.concatenate([triple_kernel.astype(bf16)] + columns, axis=1))
        second_stack = layout.gather_whole(
            jnp.concatenate([mixer_kernel.astype(bf16), widening_kernel.astype(bf16)], axis=1)
        )[0]
        narrow = layout.gather_whole(narrowing_kernel.astype(bf16))[0]
        narrow = narrow.reshape(WIDTH // 16, 4, 16, WIDTH).transpose(0, 2, 1, 3).reshape(WIDTH, FF)
        second = [jnp.concatenate([second_stack, narrow], axis=1)]
    far = layout.flip(near, 2)

    n1, q_s, k_s, v_s, kt_s, vt_s, wqkv, vectors, hidden_shift = short_qkv(layout, place, rows, first)
    if layout.pieces:
        packed = pack_second(mixer_kernel, widening_kernel, narrowing_kernel, (n1,))
    else:
        hidden_shift = first[0][:, FIRST - 4 :].reshape(1, FF).astype(f32)
        packed = second[0]
    e_s, o_s, linv_s, att_s = short_forward(q_s, k_s, vt_s, ids[LONG:], (near, packed))
    if layout.pieces:
        second_stack = layout.gather_depth(packed, (linv_s,))
        second_plane = layout.gather_plane(second_stack)
    (far,) = tie([far], (second_stack,))
    stacks = (near, layout.flip(near, 1), far, layout.flip(far, 1))
    n1_l, q_l, k_l, vt_l = long_prepare(layout, place, stacks, wqkv, vectors, (second_stack,))

    e_l, o_l, linv_l, att_keep, att_send = long_forward(q_l, k_l, vt_l)
    if layout.pieces:
        second = layout.gather_core(second_plane[:1] + list(tie(second_plane[1:], (att_keep,))))
    layer_out, mid_l, mid_s, da_keep, da_send, da_s, feed_rows, hidden_sum, *second_grads = feed(
        layout, place, rows, ids, upstream, att_keep, layout.flip(att_send, 1), att_s, vectors, hidden_shift, second
    )
    da_other = layout.flip(da_send, 1)
    inputs = (place, e_l, k_l, vt_l, n1_l, q_l, da_keep, da_other, o_l, linv_l, wqkv, vectors)

    pairs = layout.scatter_core(second_grads) if layout.pieces else []
    keep_x, send_x, _, *sums = long_backward(layout, False, *inputs, (), tuple(pairs[1:]))
    moved = (keep_x.astype(f32) + layout.flip(send_x, 1).astype(f32)).astype(bf16)
    totals = layout.scatter_plane(pairs) if layout.pieces else []
    keep, send, gq, _, gkv, long_sums, long_side = long_backward(
        layout, True, *inputs, sums, (moved, *totals[1:])
    )
    dx_totals = layout.add_depth([keep, layout.flip(send, 1), layout.flip(moved, 2)])
    dx_s, *first_grads = short_backward(
        layout, place, e_s, k_s, v_s, q_s, kt_s, da_s, o_s, linv_s, n1, rows, mid_s, wqkv, vectors,
        gq, gkv, long_sums, long_side, feed_rows, hidden_sum, tuple(dx_totals[1:]),
    )
    dx_long = layout.scatter_depth(dx_totals, -1)
    if layout.pieces:
        second_grad = layout.scatter_depth(totals)
        narrow_grad = second_grad[:, WIDTH + FF :].reshape(shard, 4, WIDTH).transpose(1, 0, 2)
        narrow_grad = narrow_grad.reshape(4 * shard, WIDTH)
        first_grad = layout.scatter_depth(layout.scatter_plane(layout.scatter_core(first_grads)))
        hidden_grad = first_grad[0, FIRST - 4 * shard :]
    else:
        packed = second_grads[0][:, WIDTH + FF :].reshape(WIDTH // 16, 16, 4, WIDTH).transpose(0, 2, 1, 3)
        narrow_grad = layout.scatter_whole(packed.reshape(FF, WIDTH))
        second_grad = layout.scatter_whole(second_grads[0][:, : WIDTH + FF])
        first_grad = layout.scatter_whole(first_grads[0])
        hidden_grad = layout.scatter_whole(hidden_sum[0])
    small = first_grad[:, 3 * WIDTH :]

    standard, inverse = standardize(rows[:LONG].astype(f32))
    dx_l = (mid_l + norm_backward(dx_long, standard, inverse, vectors[V_G1][None, :])).astype(bf16)
    input_grad = jnp.concatenate([dx_l, dx_s], axis=0)
    return (
        layer_out[None],
        input_grad[None],
        first_grad[:, : 3 * WIDTH],
        second_grad[:, :WIDTH],
        second_grad[:, WIDTH : WIDTH + FF],
        narrow_grad,
        small[:, 0],
        small[:, 1],
        small[:, 2],
        hidden_grad,
        small[:, 3],
        small[:, 4],
        small[:, 5],
        small[:, 6],
        small[:, 7],
    )


def solution(mesh):
    shards = P(("band", "batch"))
    tokens = P("batch", "band", None)
    kernels = P(("band", "batch"), None)
    in_specs = (
        (tokens, P("batch", "band")) + (kernels,) * 4 + (shards,) * 9 + (tokens,)
    )
    out_specs = (tokens, tokens) + (kernels,) * 4 + (shards,) * 9
    return jax.shard_map(
        per_device, mesh=mesh, in_specs=in_specs, out_specs=out_specs, check_vma=False
    )
```

```python
import functools
import math

import jax
import jax.numpy as jnp
from jax import lax
from jax.experimental import pallas as pl
from jax.experimental.pallas import tpu as pltpu
from jax.sharding import PartitionSpec as P

HEADS = 8
HEAD = 64
LONG = 256
WIDTH = 512
FF = 2048
GROUP = 256
TILE = 512
epsilon = 1e-06
gelu_scale = 0.7978845608028654
f32 = jnp.float32
bf16 = jnp.bfloat16
PARAMS = dict(vmem_limit_bytes=58 << 20)


def dot(left, right, cl=1, cr=0):
    return lax.dot_general(left, right, (((cl,), (cr,)), ((), ())), preferred_element_type=f32)


def standardize(rows):
    center = rows - jnp.mean(rows, axis=1, keepdims=True)
    inverse = lax.rsqrt(jnp.mean(center * center, axis=1, keepdims=True) + epsilon)
    return center * inverse, inverse


def norm_backward(incoming, standard, inverse, scaling):
    scaled = incoming * scaling
    return inverse * (
        scaled
        - jnp.mean(scaled, axis=1, keepdims=True)
        - standard * jnp.mean(scaled * standard, axis=1, keepdims=True)
    )


def column_sum(rows):
    return jnp.sum(rows, axis=0, keepdims=True)


def head_lanes(block, head):
    lane = lax.broadcasted_iota(jnp.int32, block.shape, 1) // HEAD
    return jnp.where(lane == head, block.astype(f32), 0.0).astype(bf16)


V_ASK, V_CONTENT, V_MIXER, V_NARROW, V_G1, V_O1, V_G2, V_O2 = range(8)


def row_of(table_ref, index):
    return table_ref[index : index + 1, :]


def whole(shape):
    return pl.BlockSpec(shape, lambda *_: (0,) * len(shape))


def once(shape):
    return pl.BlockSpec(shape, lambda *_: (0,) * len(shape), pipeline_mode=pl.Buffered(1))


ANYWHERE = pl.BlockSpec(memory_space=pl.ANY)


def behind(kernel, count, prefetch=True):
    skip = 1 if prefetch else 0
    return lambda *refs: kernel(*refs[:skip], *refs[skip + count :])


SIDE = 128
FIRST = 3 * WIDTH + SIDE
SECOND = WIDTH + 2 * FF


class Layout:
    def __init__(self, bands, batches):
        self.bands, self.batches = bands, batches
        self.depth = bands // 4
        self.shards = bands * batches
        self.rows = WIDTH // self.shards
        self.pieces = self.rows % 16 == 0
        self.plane = [(kx, ky) for kx in (0, 1) for ky in range(batches)]

    def shard(self, place, kc, kx, ky, kz, sign):
        z = lax.rem(place[2] + (self.depth + sign * kz), self.depth)
        x = lax.rem(place[3] + kx, 2)
        y = lax.rem(place[4] + (self.batches + sign * ky), self.batches)
        core = lax.rem(place[1] + kc, 2)
        return ((z * 2 + x) * 2 + core) * self.batches + y

    def chip(self, place, kx, kz):
        return lax.rem(place[2] + kz, self.depth) * 2 + lax.rem(place[3] + kx, 2)

    def shift_depth(self, block, k):
        pairs = [(i, ((i // 4 + k) % self.depth) * 4 + i % 4) for i in range(self.bands)]
        return lax.ppermute(block, "band", pairs)

    def flip(self, block, bit):
        return lax.ppermute(block, "band", [(i, i ^ bit) for i in range(self.bands)])

    def shift_plane(self, block, kx, ky):
        n = self.batches
        pairs = [
            (b * n + y, (b ^ (2 * kx)) * n + (y + ky) % n) for b in range(self.bands) for y in range(n)
        ]
        return lax.ppermute(block, ("band", "batch"), pairs)

    def gather_depth(self, block, deps=()):
        return stack_blocks([block] + [self.shift_depth(block, k) for k in range(1, self.depth)], deps)

    def gather_plane(self, stack):
        return [stack if k == (0, 0) else self.shift_plane(stack, *k) for k in self.plane]

    def gather_core(self, plane):
        return plane + [self.flip(part, 1) for part in plane]

    def gather_whole(self, block):
        return [lax.all_gather(block, ("band", "batch"), axis=0, tiled=True)]

    def gathered_specs(self, columns):
        if not self.pieces:
            return [once((WIDTH, columns))]
        return [once((self.depth, self.rows, columns))] * (2 * len(self.plane))

    def each_gathered(self, place, refs, visit):
        if not self.pieces:
            for low in range(0, WIDTH, 16):
                visit(low // 16, refs[0][low : low + 16, :])
            return
        index = 0
        for kc in (0, 1):
            for kx, ky in self.plane:
                for kz in range(self.depth):
                    visit(self.shard(place, kc, kx, ky, kz, -1), refs[index][kz])
                index += 1

    def scattered_shapes(self, columns):
        if not self.pieces:
            return [jax.ShapeDtypeStruct((WIDTH, columns), bf16)]
        shape = (len(self.plane), self.depth, self.rows, columns)
        return [jax.ShapeDtypeStruct(shape, bf16)] * 2

    def store_scattered(self, place, refs, take):
        if not self.pieces:
            for low in range(0, WIDTH, 16):
                refs[0][low : low + 16, :] = take(low // 16)
            return
        for kc in (0, 1):
            for n, (kx, ky) in enumerate(self.plane):
                for kz in range(self.depth):
                    refs[kc][n, kz] = take(self.shard(place, kc, kx, ky, kz, 1))

    def scatter_core(self, parts):
        keep, send = parts
        arrived = self.flip(send, 1)
        return [(keep[n].astype(f32) + arrived[n].astype(f32)).astype(bf16) for n in range(len(self.plane))]

    def scatter_plane(self, pairs):
        arrived = [self.shift_plane(pairs[n], *k) for n, k in enumerate(self.plane) if n]
        return self.add_depth(pairs[:1] + arrived)

    def add_depth(self, stacks):
        totals = []
        for k in range(self.depth):
            total = stacks[0][k].astype(f32)
            for stack in stacks[1:]:
                total = total + stack[k].astype(f32)
            totals.append(total if k == 0 else total.astype(bf16))
        return totals

    def scatter_depth(self, totals, sign=1):
        final = totals[0]
        for k in range(1, self.depth):
            final = final + self.shift_depth(totals[k], (sign * k) % self.depth).astype(f32)
        return final

    def scatter_whole(self, part):
        return lax.psum_scatter(part, ("band", "batch"), scatter_dimension=0, tiled=True).astype(f32)


def tie(values, deps):
    count = len(values)
    return pl.pallas_call(
        lambda *refs: None,
        in_specs=[ANYWHERE] * (count + len(deps)),
        out_specs=[ANYWHERE] * count,
        out_shape=[jax.ShapeDtypeStruct(v.shape, v.dtype) for v in values],
        input_output_aliases={i: i for i in range(count)},
        name="tie",
    )(*values, *deps)


def stack_kernel(*refs):
    for index, ref in enumerate(refs[:-1]):
        refs[-1][index] = ref[...]


def stack_blocks(blocks, deps):
    shape = blocks[0].shape
    return pl.pallas_call(
        behind(stack_kernel, len(deps), False),
        in_specs=[ANYWHERE] * len(deps) + [pl.BlockSpec(memory_space=pltpu.VMEM)] * len(blocks),
        out_shape=jax.ShapeDtypeStruct((len(blocks), *shape), blocks[0].dtype),
        name="stack_blocks",
    )(*deps, *blocks)


def pack_first_kernel(triple_ref, *refs):
    vectors, wide, out_ref, table = refs[:8], *refs[8:]
    shard = triple_ref.shape[0]
    table[...] = jnp.zeros_like(table)
    for index, ref in enumerate(vectors):
        table[index : index + 1, :shard] = ref[...]
    out_ref[:, : 3 * WIDTH] = triple_ref[...].astype(bf16)
    turned = table[...].T[:shard, :]
    across = jnp.pad(wide[...], ((0, shard - 1), (SIDE - 4 * shard, 0)))
    out_ref[:, 3 * WIDTH :] = (turned + across).astype(bf16)


def pack_first(triple, vectors, wide):
    shard = triple.shape[0]
    return pl.pallas_call(
        pack_first_kernel,
        out_shape=jax.ShapeDtypeStruct((shard, FIRST), bf16),
        scratch_shapes=[pltpu.VMEM((SIDE, SIDE), f32)],
        compiler_params=pltpu.CompilerParams(**PARAMS),
        name="pack_first",
    )(triple, *[v[None, :] for v in vectors], wide[None, :])


def pack_rows_kernel(rows_ref, out_ref):
    out_ref[...] = rows_ref[...]


def pack_rows(rows, deps):
    block = pl.BlockSpec((LONG, WIDTH), lambda i: (0, 0))
    return pl.pallas_call(
        behind(pack_rows_kernel, len(deps), False),
        grid=(1,),
        in_specs=[ANYWHERE] * len(deps) + [block],
        out_specs=block,
        out_shape=jax.ShapeDtypeStruct((LONG, WIDTH), bf16),
        name="pack_rows",
    )(*deps, rows)


def pack_second_kernel(mixer_ref, widening_ref, narrowing_ref, out_ref):
    shard = mixer_ref.shape[0]
    out_ref[:, :WIDTH] = mixer_ref[...].astype(bf16)
    out_ref[:, WIDTH : WIDTH + FF] = widening_ref[...].astype(bf16)
    for k in range(4):
        low = WIDTH + FF + k * WIDTH
        out_ref[:, low : low + WIDTH] = narrowing_ref[k * shard : (k + 1) * shard, :].astype(bf16)


def pack_second(mixer, widening, narrowing, deps):
    blocks = [pl.BlockSpec(memory_space=pltpu.VMEM)] * 3
    return pl.pallas_call(
        behind(pack_second_kernel, len(deps), False),
        out_shape=jax.ShapeDtypeStruct((mixer.shape[0], SECOND), bf16),
        in_specs=[ANYWHERE] * len(deps) + blocks,
        compiler_params=pltpu.CompilerParams(**PARAMS),
        name="pack_second",
    )(*deps, mixer, widening, narrowing)


def short_qkv_kernel(layout, place_ref, x_ref, *refs):
    count = len(layout.gathered_specs(FIRST))
    pieces = refs[:count]
    n1_ref, q_ref, k_ref, v_ref, kt_ref, vt_ref, w_ref, vec_ref, hid_ref, side, spread = refs[count:]

    @pl.when(pl.program_id(0) == 0)
    def _():
        def visit(block, rows):
            span = pl.ds(pl.multiple_of(block * 16, 16), 16)
            w_ref[span, :] = rows[:, : 3 * WIDTH]
            side[span, :] = rows[:, 3 * WIDTH :].astype(f32)
            if layout.pieces:
                spread[pl.ds(block, 1), :] = rows[0:1, 3 * WIDTH :].astype(f32)

        layout.each_gathered(place_ref, pieces, visit)
        vec_ref[...] = side[...].T[:16, :]
        if layout.pieces:
            shard = 4 * layout.rows
            for index in range(layout.shards):
                hid_ref[:, index * shard : (index + 1) * shard] = spread[index : index + 1, SIDE - shard :]

    standard, _ = standardize(x_ref[...].astype(f32))
    normed = (standard * row_of(vec_ref, V_G1) + row_of(vec_ref, V_O1)).astype(bf16)
    n1_ref[...] = normed
    projected = dot(normed, w_ref[...])
    q = (projected[:, :WIDTH] + row_of(vec_ref, V_ASK)).astype(bf16)
    q_ref[...] = (q.astype(f32) * (1.0 / math.sqrt(HEAD))).astype(bf16)
    k = projected[:, WIDTH : 2 * WIDTH]
    v = projected[:, 2 * WIDTH :] + row_of(vec_ref, V_CONTENT)
    k_ref[...] = k.astype(bf16)
    v_ref[...] = v.astype(bf16)
    kt_ref[...] = k.T.astype(bf16)
    vt_ref[...] = v.T.astype(bf16)


def short_qkv(layout, place, rows, pieces):
    count = rows.shape[0] - LONG
    block = 256
    row_spec = pl.BlockSpec((block, WIDTH), lambda i, _: (i, 0))
    col_spec = pl.BlockSpec((WIDTH, block), lambda i, _: (0, i))
    flat = jax.ShapeDtypeStruct((count, WIDTH), bf16)
    tall = jax.ShapeDtypeStruct((WIDTH, count), bf16)
    return pl.pallas_call(
        functools.partial(short_qkv_kernel, layout),
        grid_spec=pltpu.PrefetchScalarGridSpec(
            num_scalar_prefetch=1,
            grid=(count // block,),
            in_specs=[pl.BlockSpec((block, WIDTH), lambda i, _: (i + LONG // block, 0))]
            + layout.gathered_specs(FIRST),
            out_specs=[row_spec, row_spec, row_spec, row_spec, col_spec, col_spec]
            + [once((WIDTH, 3 * WIDTH)), whole((16, WIDTH)), whole((1, FF))],
            scratch_shapes=[pltpu.VMEM((WIDTH, SIDE), f32), pltpu.VMEM((max(8, layout.shards), SIDE), f32)],
        ),
        out_shape=[flat, flat, flat, flat, tall, tall]
        + [
            jax.ShapeDtypeStruct((WIDTH, 3 * WIDTH), bf16),
            jax.ShapeDtypeStruct((16, WIDTH), f32),
            jax.ShapeDtypeStruct((1, FF), f32),
        ],
        compiler_params=pltpu.CompilerParams(**PARAMS),
        cost_estimate=pl.CostEstimate(
            flops=2 * count * WIDTH * 3 * WIDTH, bytes_accessed=10 << 20, transcendentals=0
        ),
        name="short_qkv",
    )(place, rows, *pieces)


def short_forward_kernel(
    q_ref, k_ref, vt_ref, idc_ref, idr_ref, e_ref, o_ref, linv_ref, att_ref, s_ref, bias_ref, top_ref
):
    step = pl.program_id(0)
    count = k_ref.shape[0]

    @pl.when(step == 0)
    def _():
        same = idc_ref[LONG:, :] == idr_ref[:, LONG:]
        bias_ref[...] = jnp.where(same, 0.0, -1e30)

    tile = 256

    def first(slot, low, masked):
        span = slice(low, low + tile)
        s = dot(k_ref[...], masked[span, :], 1, 1) + bias_ref[:, span]
        s_ref[slot, :, span] = s
        top_ref[slot, :, span] = jnp.broadcast_to(jnp.max(s, axis=0, keepdims=True), (8, tile))

    def second(slot, low):
        span = slice(low, low + tile)
        own = pl.ds(pl.multiple_of((step - 1) * HEAD, HEAD), HEAD)
        e = jnp.exp(s_ref[slot, :, span] - top_ref[slot, 0:1, span])
        linv = 1.0 / column_sum(e)
        low_e = e.astype(bf16)
        e_ref[:, span] = low_e
        linv_ref[:, span] = jnp.broadcast_to(linv, (8, tile))
        o_ref[own, span] = dot(vt_ref[own, :], low_e) * linv

    def masked_queries():
        return head_lanes(q_ref[...], lax.rem(step, 4))

    last = pl.num_programs(0) - 1

    @pl.when(step == 0)
    def _():
        masked = masked_queries()
        for low in range(0, count, tile):
            first(0, low, masked)

    for parity in (0, 1):
        @pl.when((step > 0) & (step < last) & (lax.rem(step, 2) == parity))
        def _():
            masked = masked_queries()
            for low in range(0, count, tile):
                first(parity, low, masked)
                second(1 - parity, low)

    @pl.when(step == last)
    def _():
        for low in range(0, count, tile):
            second((HEADS - 1) % 2, low)
        for low in range(0, WIDTH, 128):
            att_ref[:, low : low + 128] = o_ref[low : low + 128, :].T.astype(bf16)


def short_forward(q, k, vt, id_column, id_row, deps):
    count = q.shape[0]
    now = lambda s: (0, jnp.minimum(s, HEADS - 1) // 4)
    before = lambda s: (0, jnp.maximum(s - 1, 0))
    return pl.pallas_call(
        behind(short_forward_kernel, len(deps), False),
        grid=(HEADS + 1,),
        in_specs=[ANYWHERE] * len(deps)
        + [
            pl.BlockSpec((count, GROUP), now),
            pl.BlockSpec((count, GROUP), now),
            whole((WIDTH, count)),
            whole(id_column.shape),
            whole(id_row.shape),
        ],
        out_specs=[
            pl.BlockSpec((count, count), before),
            whole((WIDTH, count)),
            pl.BlockSpec((8, count), lambda s: (jnp.maximum(s - 1, 0), 0)),
            whole((count, WIDTH)),
        ],
        out_shape=[
            jax.ShapeDtypeStruct((count, HEADS * count), bf16),
            jax.ShapeDtypeStruct((WIDTH, count), f32),
            jax.ShapeDtypeStruct((HEADS * 8, count), f32),
            jax.ShapeDtypeStruct((count, WIDTH), bf16),
        ],
        scratch_shapes=[
            pltpu.VMEM((2, count, count), f32),
            pltpu.VMEM((count, count), f32),
            pltpu.VMEM((2, 8, count), f32),
        ],
        compiler_params=pltpu.CompilerParams(**PARAMS),
        cost_estimate=pl.CostEstimate(
            flops=12 * count * count * WIDTH, bytes_accessed=12 << 20, transcendentals=HEADS * count * count
        ),
        name="short_forward",
    )(*deps, q, k, vt, id_column, id_row)


CHIPS = 2


def long_prepare_kernel(
    depth, place_ref, own0, other0, own1, other1, w_ref, vec_ref, n1_ref, q_ref, k_ref, vt_ref,
    wk, wv,
):
    step = pl.program_id(0)
    core = place_ref[1]
    near = step < depth
    lanes = lambda base: pl.ds(pl.multiple_of(base + core * GROUP, GROUP), GROUP)

    @pl.when(step == 0)
    def _():
        for other in (0, 1):
            @pl.when(core == other)
            def _():
                wk[...] = w_ref[:, WIDTH + other * GROUP : WIDTH + (other + 1) * GROUP]
                wv[...] = w_ref[:, 2 * WIDTH + other * GROUP : 2 * WIDTH + (other + 1) * GROUP]

    chips = own0.shape[0]
    rows = jnp.concatenate(
        [jnp.where(near, a[chip], b[chip]) for chip in range(chips) for a, b in ((own0, own1), (other0, other1))],
        axis=0,
    )
    standard, _ = standardize(rows.astype(f32))
    normed = (standard * row_of(vec_ref, V_G1) + row_of(vec_ref, V_O1)).astype(bf16)
    n1_ref[...] = normed
    k = dot(normed, wk[...])
    v = dot(normed, wv[...]) + vec_ref[V_CONTENT : V_CONTENT + 1, lanes(0)]
    k_ref[...] = k.astype(bf16)
    vt_ref[...] = v.astype(bf16).T

    @pl.when(step == 0)
    def _():
        q = (dot(normed[:TILE, :], w_ref[:, lanes(0)]) + vec_ref[V_ASK : V_ASK + 1, lanes(0)]).astype(bf16)
        q_ref[...] = (q.astype(f32) * (1.0 / math.sqrt(HEAD))).astype(bf16)


def long_prepare(layout, place, stacks, weights, vectors, deps):
    depth = layout.depth
    total = 2 * depth * TILE
    steps = depth // CHIPS
    tile = CHIPS * TILE
    row_spec = pl.BlockSpec((tile, GROUP), lambda i, _: (i, 0))
    col_spec = pl.BlockSpec((GROUP, tile), lambda i, _: (0, i))
    near = pl.BlockSpec((CHIPS, LONG, WIDTH), lambda i, _: (jnp.minimum(i, steps - 1), 0, 0))
    far = pl.BlockSpec((CHIPS, LONG, WIDTH), lambda i, _: (jnp.maximum(i - steps, 0), 0, 0))
    flat = jax.ShapeDtypeStruct((total, GROUP), bf16)
    tall = jax.ShapeDtypeStruct((GROUP, total), bf16)
    return pl.pallas_call(
        behind(functools.partial(long_prepare_kernel, depth // CHIPS), len(deps)),
        grid_spec=pltpu.PrefetchScalarGridSpec(
            num_scalar_prefetch=1,
            grid=(2 * steps,),
            in_specs=[ANYWHERE] * len(deps)
            + [near, near, far, far, whole((WIDTH, 3 * WIDTH)), whole(vectors.shape)],
            out_specs=[
                pl.BlockSpec((tile, WIDTH), lambda i, _: (i, 0)),
                whole((TILE, GROUP)),
                row_spec,
                col_spec,
            ],
            scratch_shapes=[pltpu.VMEM((WIDTH, GROUP), bf16)] * 2,
        ),
        out_shape=[
            jax.ShapeDtypeStruct((total, WIDTH), bf16),
            jax.ShapeDtypeStruct((TILE, GROUP), bf16),
            flat,
            tall,
        ],
        compiler_params=pltpu.CompilerParams(**PARAMS),
        cost_estimate=pl.CostEstimate(
            flops=4 * total * WIDTH * GROUP, bytes_accessed=18 << 20, transcendentals=0
        ),
        name="long_prepare",
    )(place, *deps, *stacks, weights, vectors)


CHUNK = 256
BACK = 2 * TILE
PARTS = TILE // CHUNK
LOCAL_HEADS = GROUP // HEAD
STEPS = LOCAL_HEADS * PARTS


def long_forward_kernel(
    q_ref, k_ref, vt_ref, e_ref, o_ref, linv_ref, keep_ref, send_ref, s_ref, top_ref
):
    step = pl.program_id(0)
    total = k_ref.shape[0]
    tile = min(total, 4096)
    last = pl.num_programs(0) - 1

    def masked_queries():
        rows = pl.ds(pl.multiple_of(lax.rem(step, PARTS) * CHUNK, CHUNK), CHUNK)
        return head_lanes(q_ref[rows, :], step // PARTS)

    def first_tile(slot, low, masked, top):
        s = dot(k_ref[pl.ds(low, tile), :], masked, 1, 1)
        s_ref[slot, pl.ds(low, tile), :] = s
        return jnp.maximum(top, jnp.max(s.reshape(tile // 8, 8, CHUNK), axis=0))

    def second_tile(slot, low, top, head, carry):
        summed, mixed = carry
        e = jnp.exp(s_ref[slot, pl.ds(low, tile), :] - top)
        summed = summed + jnp.sum(e.reshape(tile // 8, 8, CHUNK), axis=0)
        low_e = e.astype(bf16)
        e_ref[pl.ds(low, tile), :] = low_e
        values = vt_ref[pl.ds(pl.multiple_of(head * HEAD, HEAD), HEAD), pl.ds(low, tile)]
        return summed, mixed + dot(values, low_e)

    start_top = jnp.full((8, CHUNK), -1e30, f32)
    start_sum = (jnp.zeros((8, CHUNK), f32), jnp.zeros((HEAD, CHUNK), f32))

    def finish(head, part, carry):
        summed, mixed = carry
        linv = 1.0 / column_sum(summed)
        linv_ref[...] = jnp.broadcast_to(linv, (8, CHUNK))
        o_ref[part, pl.ds(pl.multiple_of(head * HEAD, HEAD), HEAD), :] = mixed * linv

    def place(turn):
        return pl.multiple_of(turn * tile, tile)

    @pl.when(step == 0)
    def _():
        masked = masked_queries()
        top_ref[0] = lax.fori_loop(
            0, total // tile, lambda t, top: first_tile(0, place(t), masked, top), start_top
        )

    for parity in (0, 1):
        @pl.when((step > 0) & (step < last) & (lax.rem(step, 2) == parity))
        def _():
            masked = masked_queries()
            before = step - 1
            head = before // PARTS
            top_row = jnp.max(top_ref[1 - parity], axis=0, keepdims=True)

            def body(turn, carry):
                top, kept = carry
                low = place(turn)
                top = first_tile(parity, low, masked, top)
                kept = second_tile(1 - parity, low, top_row, head, kept)
                return top, kept

            top, kept = lax.fori_loop(0, total // tile, body, (start_top, start_sum))
            top_ref[parity] = top
            finish(head, lax.rem(before, PARTS), kept)

    @pl.when(step == last)
    def _():
        slot = (STEPS - 1) % 2
        top_row = jnp.max(top_ref[slot], axis=0, keepdims=True)
        head = LOCAL_HEADS - 1
        kept = lax.fori_loop(
            0,
            total // tile,
            lambda t, carry: second_tile(slot, place(t), top_row, head, carry),
            start_sum,
        )
        finish(head, PARTS - 1, kept)
        keep_ref[...] = o_ref[0].T.astype(bf16)
        send_ref[...] = o_ref[1].T.astype(bf16)


def long_forward(q, k, vt):
    total = k.shape[0]
    before = lambda s: jnp.maximum(s - 1, 0)
    half = jax.ShapeDtypeStruct((CHUNK, GROUP), bf16)
    return pl.pallas_call(
        long_forward_kernel,
        grid=(STEPS + 1,),
        in_specs=[once((TILE, GROUP)), once((total, GROUP)), once((GROUP, total))],
        out_specs=[
            pl.BlockSpec((total, CHUNK), lambda s: (0, before(s))),
            whole((PARTS, GROUP, CHUNK)),
            pl.BlockSpec((8, CHUNK), lambda s: (before(s), 0)),
            whole((CHUNK, GROUP)),
            whole((CHUNK, GROUP)),
        ],
        scratch_shapes=[pltpu.VMEM((2, total, CHUNK), f32), pltpu.VMEM((2, 8, CHUNK), f32)],
        out_shape=[
            jax.ShapeDtypeStruct((total, STEPS * CHUNK), bf16),
            jax.ShapeDtypeStruct((PARTS, GROUP, CHUNK), f32),
            jax.ShapeDtypeStruct((STEPS * 8, CHUNK), f32),
            half,
            half,
        ],
        compiler_params=pltpu.CompilerParams(**PARAMS),
        cost_estimate=pl.CostEstimate(
            flops=16 * TILE * total * GROUP, bytes_accessed=24 << 20, transcendentals=4 * TILE * total
        ),
        name="long_forward",
    )(q, k, vt)


def feed_kernel(layout, place_ref, x_ref, ids_ref, g_ref, mine_ref, other_ref, short_ref, vec_ref, hid_ref, *refs):
    count = len(layout.gathered_specs(SECOND))
    pieces, refs = refs[:count], refs[count:]
    out_ref, midl_ref, mids_ref, keep_ref, send_ref, das_ref, row_ref, hsum_ref = refs[:8]
    grads = refs[8:-8]
    wp_ref, we_ref, wr_ref, gp_ref, ge_ref, gr_ref, act_ref, dh_ref = refs[-8:]
    swapped = place_ref[1] == 1

    def visit(block, rows):
        span = pl.ds(pl.multiple_of(block * 16, 16), 16)
        wp_ref[span, :] = rows[:, :WIDTH]
        we_ref[span, :] = rows[:, WIDTH : WIDTH + FF]
        for k in range(4):
            low = WIDTH + FF + k * WIDTH
            wr_ref[pl.ds(pl.multiple_of(block * 64 + 16 * k, 16), 16), :] = rows[:, low : low + WIDTH]

    layout.each_gathered(place_ref, pieces, visit)

    x = x_ref[...].astype(f32)
    live = (ids_ref[...] >= 0).astype(f32)
    upstream = g_ref[...].astype(f32)
    mine, other = mine_ref[...], other_ref[...]
    long = jnp.concatenate([jnp.where(swapped, other, mine), jnp.where(swapped, mine, other)], axis=1)
    attended = jnp.concatenate([long, short_ref[...]], axis=0)
    branch = dot(attended, wp_ref[...]) + row_of(vec_ref, V_MIXER)
    middle = x + live * branch
    standard, inverse = standardize(middle)
    gain = row_of(vec_ref, V_G2)
    normed = (standard * gain + row_of(vec_ref, V_O2)).astype(bf16)
    branch_low = (live * upstream).astype(bf16)

    part = 256

    def products(low):
        return (
            dot(normed, we_ref[:, low : low + part]) + hid_ref[:, low : low + part],
            dot(branch_low, wr_ref[low : low + part, :], 1, 1),
        )

    following = products(0)
    for low in range(0, FF, part):
        hidden, into = following
        if low + part < FF:
            following = products(low + part)
        square = hidden * hidden
        tangent = jnp.tanh(hidden * (gelu_scale + (gelu_scale * 0.044715) * square))
        half = 0.5 + 0.5 * tangent
        active = (hidden * half).astype(bf16)
        slope = half + (0.5 * hidden) * (1.0 - tangent * tangent) * (
            gelu_scale + (gelu_scale * 3.0 * 0.044715) * square
        )
        hidden_low = (into * slope).astype(bf16)
        hsum_ref[:, low : low + part] = column_sum(hidden_low.astype(f32))
        act_ref[:, low : low + part] = active
        dh_ref[:, low : low + part] = hidden_low
        gr_ref[low : low + part, :] = dot(active, branch_low, 0, 0).astype(bf16)
        ge_ref[:, low : low + part] = dot(normed, hidden_low, 0, 0).astype(bf16)

    branch_two = dot(act_ref[...], wr_ref[...]) + row_of(vec_ref, V_NARROW)
    out_ref[...] = (middle + live * branch_two).astype(bf16)
    normed_grad = dot(dh_ref[...], we_ref[...], 1, 1)
    middle_grad = upstream + norm_backward(normed_grad, standard, inverse, gain)
    midl_ref[...] = middle_grad[:LONG, :]
    mids_ref[...] = middle_grad[LONG:, :]
    attn_low = (live * middle_grad).astype(bf16)
    attended_grad = dot(attn_low, wp_ref[...], 1, 1).astype(bf16)
    das_ref[...] = attended_grad[LONG:, :]
    left, right = attended_grad[:LONG, :GROUP], attended_grad[:LONG, GROUP:]
    keep_ref[...] = jnp.where(swapped, right, left)
    send_ref[...] = jnp.where(swapped, left, right)
    gp_ref[...] = dot(attended, attn_low, 0, 0).astype(bf16)
    row_ref[...] = jnp.zeros_like(row_ref)
    row_ref[0:1, :] = column_sum(attn_low.astype(f32))
    row_ref[1:2, :] = column_sum(branch_low.astype(f32))
    row_ref[2:3, :] = column_sum(normed_grad * standard)
    row_ref[3:4, :] = column_sum(normed_grad)

    def take(block):
        span = pl.ds(pl.multiple_of(block * 16, 16), 16)
        parts = [gp_ref[span, :], ge_ref[span, :]] + [
            gr_ref[pl.ds(pl.multiple_of(block * 64 + 16 * k, 16), 16), :] for k in range(4)
        ]
        return jnp.concatenate(parts, axis=1)

    layout.store_scattered(place_ref, grads, take)


def feed(layout, place, rows, id_column, upstream, mine, other, short, vectors, hidden_shift, pieces):
    count = rows.shape[0]
    grads = layout.scattered_shapes(SECOND)
    operands = [rows, id_column, upstream, mine, other, short, vectors, hidden_shift]
    shapes = [
        jax.ShapeDtypeStruct((count, WIDTH), bf16),
        jax.ShapeDtypeStruct((LONG, WIDTH), f32),
        jax.ShapeDtypeStruct((count - LONG, WIDTH), f32),
        jax.ShapeDtypeStruct((LONG, GROUP), bf16),
        jax.ShapeDtypeStruct((LONG, GROUP), bf16),
        jax.ShapeDtypeStruct((count - LONG, WIDTH), bf16),
        jax.ShapeDtypeStruct((8, WIDTH), f32),
        jax.ShapeDtypeStruct((1, FF), f32),
    ] + grads
    return pl.pallas_call(
        functools.partial(feed_kernel, layout),
        grid_spec=pltpu.PrefetchScalarGridSpec(
            num_scalar_prefetch=1,
            grid=(1,),
            in_specs=[once(x.shape) for x in operands] + layout.gathered_specs(SECOND),
            out_specs=[once(x.shape) for x in shapes],
            scratch_shapes=[
                pltpu.VMEM((WIDTH, WIDTH), bf16),
                pltpu.VMEM((WIDTH, FF), bf16),
                pltpu.VMEM((FF, WIDTH), bf16),
                pltpu.VMEM((WIDTH, WIDTH), bf16),
                pltpu.VMEM((WIDTH, FF), bf16),
                pltpu.VMEM((FF, WIDTH), bf16),
                pltpu.VMEM((count, FF), bf16),
                pltpu.VMEM((count, FF), bf16),
            ],
        ),
        out_shape=shapes,
        compiler_params=pltpu.CompilerParams(**PARAMS),
        cost_estimate=pl.CostEstimate(
            flops=6 * count * WIDTH * (WIDTH + 2 * FF), bytes_accessed=18 << 20, transcendentals=count * FF
        ),
        name="feed",
    )(place, *operands, *pieces)


def long_backward_kernel(
    final, place_ref, e_ref, k_ref, vt_ref, n1_ref, q_ref, mine_ref, other_ref, o_ref, linv_ref, w_ref, vec_ref,
    *refs,
):
    if final:
        dq_in, gkv_in, row_in, side_in, *refs = refs
    (
    keep_ref, send_ref, gq_ref, dq_acc, gkv_ref, row_ref, side_ref,
    qblk, dblk, delta, ds_ref, wq, wkv,
    ) = refs
    step = pl.program_id(0)
    core = place_ref[1]

    @pl.when(step == 0)
    def _():
        lanes = lambda base: pl.ds(pl.multiple_of(base + core * GROUP, GROUP), GROUP)
        wq[...] = w_ref[:, lanes(0)]
        wkv[:, :GROUP] = w_ref[:, lanes(WIDTH)]
        wkv[:, GROUP:] = w_ref[:, lanes(2 * WIDTH)]
        if final:
            dq_acc[...] = dq_in[...]
            gkv_ref[...] = gkv_in[...]
            row_ref[...] = row_in[...]
            side_ref[...] = side_in[...]
        else:
            for ref in (dq_acc, gkv_ref, row_ref, side_ref):
                ref[...] = jnp.zeros_like(ref)
        for part in range(PARTS):
            rows = slice(part * CHUNK, (part + 1) * CHUNK)
            turned = (mine_ref, other_ref)[part][...].astype(f32).T
            product = turned * o_ref[part]
            pieces = []
            for head in range(LOCAL_HEADS):
                index = head * PARTS + part
                span = slice(head * HEAD, (head + 1) * HEAD)
                linv = linv_ref[8 * index : 8 * index + 1, :]
                delta[8 * index : 8 * index + 8, :] = jnp.broadcast_to(
                    column_sum(product[span, :]) * linv, (8, CHUNK)
                )
                pieces.append(turned[span, :] * linv)
            scaled = jnp.concatenate(pieces, axis=0).T
            for head in range(LOCAL_HEADS):
                index = head * PARTS + part
                span = slice(index * CHUNK, (index + 1) * CHUNK)
                dblk[span, :] = head_lanes(scaled, head)
                qblk[span, :] = head_lanes(q_ref[rows, :], head)

    def span_of(index):
        return slice(index * CHUNK, (index + 1) * CHUNK)

    v = vt_ref[...].T
    kt = k_ref[...].T
    slopes = dot(v, dblk[span_of(0), :], 1, 1)
    for index in range(STEPS):
        head, part = index // PARTS, index % PARTS
        span = span_of(index)
        following = dot(v, dblk[span_of(index + 1), :], 1, 1) if index + 1 < STEPS else None
        ds = (
            e_ref[:, span].astype(f32) * (slopes - delta[8 * index : 8 * index + 1, :])
        ).astype(bf16)
        ds_ref[:, span] = ds
        own = slice(head * HEAD, (head + 1) * HEAD)
        dq_acc[part, own, :] += dot(kt[own, :], ds)
        slopes = following

    value_grad = dot(e_ref[...], dblk[...]).astype(bf16)
    key_grad = dot(ds_ref[...], qblk[...]).astype(bf16)
    both = jnp.concatenate([key_grad, value_grad], axis=1)
    normed = n1_ref[...]
    through = dot(both, wkv[...], 1, 1)
    gkv_ref[...] += dot(normed, both, 0, 0)
    side_ref[1:2, :] += column_sum(value_grad.astype(f32))

    def put(entire):
        low = entire.astype(bf16)
        for chip in range(BACK // TILE):
            base = chip * TILE
            keep_ref[chip] = low[base : base + LONG, :]
            send_ref[chip] = low[base + LONG : base + TILE, :]
        shifts = column_sum(entire)
        scales = column_sum(entire * normed.astype(f32)) - shifts * row_of(vec_ref, V_O1)
        row_ref[0:1, :] += scales / row_of(vec_ref, V_G1)
        row_ref[1:2, :] += shifts

    if not final:
        put(through)
        return
    last = pl.num_programs(0) - 1

    @pl.when(step < last)
    def _():
        put(through)

    @pl.when(step == last)
    def _():
        query_grad = jnp.concatenate(
            [dq_acc[part].T for part in range(PARTS)], axis=0
        ) * (1.0 / math.sqrt(HEAD))
        low = query_grad.astype(bf16)
        put(jnp.concatenate([through[:TILE, :] + dot(low, wq[...], 1, 1), through[TILE:, :]], axis=0))
        gq_ref[...] = dot(normed[:TILE, :], low, 0, 0)
        side_ref[0:1, :] += column_sum(low.astype(f32))


def long_backward(layout, final, place, e, k, vt, normed, q, mine, other, o, linv, weights, vectors, sums, deps):
    tiles = layout.depth * TILE // BACK
    away = (lambda i: i) if not final else (lambda i: lax.rem(i + 1, tiles))
    turn = lambda i: away(i) if final else tiles + i
    out = jax.ShapeDtypeStruct((layout.depth, LONG, WIDTH), bf16)
    out_spec = pl.BlockSpec((BACK // TILE, LONG, WIDTH), lambda i, p: (away(i), 0, 0))
    sum_shapes = [
        jax.ShapeDtypeStruct((PARTS, GROUP, CHUNK), f32),
        jax.ShapeDtypeStruct((WIDTH, 2 * GROUP), f32),
        jax.ShapeDtypeStruct((8, WIDTH), f32),
        jax.ShapeDtypeStruct((8, GROUP), f32),
    ]
    sum_specs = [whole(x.shape) for x in sum_shapes]
    return pl.pallas_call(
        behind(functools.partial(long_backward_kernel, final), len(deps)),
        grid_spec=pltpu.PrefetchScalarGridSpec(
            num_scalar_prefetch=1,
            grid=(tiles,),
            in_specs=[ANYWHERE] * len(deps)
            + [
                pl.BlockSpec((BACK, STEPS * CHUNK), lambda i, p: (turn(i), 0)),
                pl.BlockSpec((BACK, GROUP), lambda i, p: (turn(i), 0)),
                pl.BlockSpec((GROUP, BACK), lambda i, p: (0, turn(i))),
                pl.BlockSpec((BACK, WIDTH), lambda i, p: (turn(i), 0)),
                whole((TILE, GROUP)),
                whole((CHUNK, GROUP)),
                whole((CHUNK, GROUP)),
                whole((PARTS, GROUP, CHUNK)),
                whole((STEPS * 8, CHUNK)),
                once((WIDTH, 3 * WIDTH)),
                whole(vectors.shape),
            ]
            + sum_specs[: len(sums)],
            out_specs=[out_spec, out_spec, whole((WIDTH, GROUP))] + sum_specs,
            scratch_shapes=[
                pltpu.VMEM((STEPS * CHUNK, GROUP), bf16),
                pltpu.VMEM((STEPS * CHUNK, GROUP), bf16),
                pltpu.VMEM((STEPS * 8, CHUNK), f32),
                pltpu.VMEM((BACK, STEPS * CHUNK), bf16),
                pltpu.VMEM((WIDTH, GROUP), bf16),
                pltpu.VMEM((WIDTH, 2 * GROUP), bf16),
            ],
        ),
        out_shape=[out, out, jax.ShapeDtypeStruct((WIDTH, GROUP), f32)] + sum_shapes,
        compiler_params=pltpu.CompilerParams(**PARAMS),
        cost_estimate=pl.CostEstimate(
            flops=20 * TILE * k.shape[0] * GROUP, bytes_accessed=16 << 20, transcendentals=0
        ),
        name="long_backward_final" if final else "long_backward",
    )(place, *deps, e, k, vt, normed, q, mine, other, o, linv, weights, vectors, *sums)


def short_backward_kernel(
    layout, place_ref, e_ref, k_ref, v_ref, q_ref, kt_ref, da_ref, o_ref, linv_ref, n1_ref, x_ref, mid_ref, w_ref,
    vec_ref, gq_ref, gkv_ref, lrow_ref, lside_ref, frow_ref, hsum_ref,
    dx_ref, *refs,
):
    grads = refs[:-9]
    scaled, delta, dblk, qblk, ds_ref, dqt, dqkv, packed, column = refs[-9:]
    step = pl.program_id(0)
    count = k_ref.shape[0]

    @pl.when(step == 0)
    def _():
        for low in range(0, WIDTH, GROUP):
            turned = da_ref[:, low : low + GROUP].astype(f32).T
            product = turned * o_ref[low : low + GROUP, :]
            pieces = []
            for head in range(4):
                span = slice(head * HEAD, (head + 1) * HEAD)
                index = low // HEAD + head
                linv = linv_ref[8 * index : 8 * index + 1, :]
                delta[8 * index : 8 * index + 8, :] = jnp.broadcast_to(
                    column_sum(product[span, :]) * linv, (8, count)
                )
                pieces.append(turned[span, :] * linv)
            scaled[:, low : low + GROUP] = jnp.concatenate(pieces, axis=0).T.astype(bf16)

    def group(side):
        low = side * GROUP
        for head in range(4):
            index = side * 4 + head
            span = slice(head * count, (head + 1) * count)
            own = slice(head * HEAD, (head + 1) * HEAD)
            dblk[span, :] = head_lanes(scaled[:, low : low + GROUP], head)
            qblk[span, :] = head_lanes(q_ref[...], head)
            slopes = dot(v_ref[...], dblk[span, :], 1, 1)
            ds = (
                e_ref[:, span].astype(f32) * (slopes - delta[8 * index : 8 * index + 1, :])
            ).astype(bf16)
            ds_ref[:, span] = ds
            dqt[own, :] = dot(kt_ref[low + head * HEAD : low + (head + 1) * HEAD, :], ds)
        value_grad = dot(e_ref[...], dblk[...])
        key_grad = dot(ds_ref[...], qblk[...])
        query_grad = dqt[...].T * (1.0 / math.sqrt(HEAD))
        dqkv[:, low : low + GROUP] = query_grad.astype(bf16)
        dqkv[:, WIDTH + low : WIDTH + low + GROUP] = key_grad.astype(bf16)
        dqkv[:, 2 * WIDTH + low : 2 * WIDTH + low + GROUP] = value_grad.astype(bf16)

    for side in (0, 1):
        pl.when(step == side)(functools.partial(group, side))

    @pl.when(step == 1)
    def _():
        rows_grad = dot(dqkv[...], w_ref[...], 1, 1)
        standard, inverse = standardize(x_ref[LONG:, :].astype(f32))
        through = norm_backward(rows_grad, standard, inverse, row_of(vec_ref, V_G1))
        dx_ref[...] = (mid_ref[...] + through).astype(bf16)
        core = place_ref[1]
        column[...] = jnp.zeros_like(column)
        column[0:1, :] = column_sum(dqkv[:, :WIDTH].astype(f32))
        column[1:2, :] = column_sum(dqkv[:, 2 * WIDTH :].astype(f32))
        for other in (0, 1):
            @pl.when(core == other)
            def _():
                span = slice(other * GROUP, (other + 1) * GROUP)
                column[0:2, span] += lside_ref[0:2, :]
        column[2:4, :] = frow_ref[0:2, :]
        column[4:5, :] = lrow_ref[0:1, :] + column_sum(rows_grad * standard)
        column[5:6, :] = lrow_ref[1:2, :] + column_sum(rows_grad)
        column[6:8, :] = frow_ref[2:4, :]
        packed[:, 3 * WIDTH :] = column[...].T
        if layout.pieces:
            shard = 4 * layout.rows
            for index in range(layout.shards):
                low = index * layout.rows
                packed[low : low + 1, FIRST - shard :] = hsum_ref[:, index * shard : (index + 1) * shard]
        packed[:, : 3 * WIDTH] = dot(n1_ref[...], dqkv[...], 0, 0)
        for other in (0, 1):
            @pl.when(core == other)
            def _():
                for third in range(3):
                    low = third * WIDTH + other * GROUP
                    extra = gq_ref[...] if third == 0 else gkv_ref[:, (third - 1) * GROUP : third * GROUP]
                    packed[:, low : low + GROUP] += extra

        layout.store_scattered(
            place_ref, grads, lambda block: packed[pl.ds(pl.multiple_of(block * 16, 16), 16), :].astype(bf16)
        )


def short_backward(
    layout, place, e, k, v, q, kt, da, o, linv, n1, rows, mid, weights, vectors, gq, gkv, lrow, lside, frow, hsum, deps
):
    count = k.shape[0]
    half = pl.BlockSpec((count, GROUP), lambda i, _: (0, i))
    grads = layout.scattered_shapes(FIRST)
    return pl.pallas_call(
        behind(functools.partial(short_backward_kernel, layout), len(deps)),
        grid_spec=pltpu.PrefetchScalarGridSpec(
            num_scalar_prefetch=1,
            grid=(2,),
            in_specs=[ANYWHERE] * len(deps)
            + [
                pl.BlockSpec((count, 4 * count), lambda i, _: (0, i)),
                half,
                half,
                half,
                once((WIDTH, count)),
                once((count, WIDTH)),
                once((WIDTH, count)),
                once((HEADS * 8, count)),
                once((count, WIDTH)),
                once(rows.shape),
                once((count, WIDTH)),
                once((WIDTH, 3 * WIDTH)),
                whole(vectors.shape),
                once((WIDTH, GROUP)),
                once((WIDTH, 2 * GROUP)),
                whole((8, WIDTH)),
                whole((8, GROUP)),
                whole((8, WIDTH)),
                whole((1, FF)),
            ],
            out_specs=[once((count, WIDTH))] + [once(g.shape) for g in grads],
            scratch_shapes=[
                pltpu.VMEM((count, WIDTH), bf16),
                pltpu.VMEM((HEADS * 8, count), f32),
                pltpu.VMEM((4 * count, GROUP), bf16),
                pltpu.VMEM((4 * count, GROUP), bf16),
                pltpu.VMEM((count, 4 * count), bf16),
                pltpu.VMEM((GROUP, count), f32),
                pltpu.VMEM((count, 3 * WIDTH), bf16),
                pltpu.VMEM((WIDTH, FIRST), f32),
                pltpu.VMEM((SIDE, WIDTH), f32),
            ],
        ),
        out_shape=[jax.ShapeDtypeStruct((count, WIDTH), bf16)] + grads,
        compiler_params=pltpu.CompilerParams(**PARAMS),
        cost_estimate=pl.CostEstimate(
            flops=24 * count * count * WIDTH, bytes_accessed=18 << 20, transcendentals=0
        ),
        name="short_backward",
    )(place, *deps, e, k, v, q, kt, da, o, linv, n1, rows, mid, weights, vectors, gq, gkv, lrow, lside, frow, hsum)


def per_device(
    incoming_rows,
    picture_label,
    triple_kernel,
    mixer_kernel,
    widening_kernel,
    narrowing_kernel,
    asker_offset,
    content_offset,
    mixer_offset_vector,
    widening_offset,
    narrowing_offset,
    leading_gain,
    leading_offset,
    second_gain,
    second_offset,
    loss_sensitivity,
):
    layout = Layout(lax.axis_size("band"), lax.axis_size("batch"))
    band = lax.axis_index("band")
    rows = incoming_rows[0]
    id_column = picture_label[0][:, None]
    upstream = loss_sensitivity[0]
    shard = layout.rows
    place = jnp.stack([band // 2, band % 2, band // 4, (band // 2) % 2, lax.axis_index("batch")]).astype(jnp.int32)

    small = (
        asker_offset,
        content_offset,
        mixer_offset_vector,
        narrowing_offset,
        leading_gain,
        leading_offset,
        second_gain,
        second_offset,
    )
    if layout.pieces:
        first_stack = layout.gather_depth(
            pack_first(triple_kernel, small, widening_offset), (place, id_column)
        )
        first_plane = layout.gather_plane(first_stack)
        near = layout.gather_depth(pack_rows(rows, (first_stack,)), tuple(first_plane[1:]))
        packed = pack_second(mixer_kernel, widening_kernel, narrowing_kernel, (first_stack,))
        first = layout.gather_core(first_plane[:1] + list(tie(first_plane[1:], (packed,))))
    else:
        near = layout.gather_depth(rows[:LONG])
        columns = [v.astype(bf16)[:, None] for v in small]
        columns += [jnp.zeros((shard, SIDE - 12), bf16), widening_offset.astype(bf16).reshape(shard, 4)]
        first = layout.gather_whole(jnp.concatenate([triple_kernel.astype(bf16)] + columns, axis=1))
        second_stack = layout.gather_whole(
            jnp.concatenate([mixer_kernel.astype(bf16), widening_kernel.astype(bf16)], axis=1)
        )[0]
        narrow = layout.gather_whole(narrowing_kernel.astype(bf16))[0]
        narrow = narrow.reshape(WIDTH // 16, 4, 16, WIDTH).transpose(0, 2, 1, 3).reshape(WIDTH, FF)
        second = [jnp.concatenate([second_stack, narrow], axis=1)]
    far = layout.flip(near, 2)
    n1, q_s, k_s, v_s, kt_s, vt_s, wqkv, vectors, hidden_shift = short_qkv(layout, place, rows, first)
    if not layout.pieces:
        hidden_shift = first[0][:, FIRST - 4 :].reshape(1, FF).astype(f32)
        packed = second[0]
    e_s, o_s, linv_s, att_s = short_forward(q_s, k_s, vt_s, id_column, picture_label, (near, packed))
    if layout.pieces:
        second_stack = layout.gather_depth(packed, (linv_s,))
        second_plane = layout.gather_plane(second_stack)
    (far,) = tie([far], (second_stack,))
    stacks = (near, layout.flip(near, 1), far, layout.flip(far, 1))
    n1_l, q_l, k_l, vt_l = long_prepare(layout, place, stacks, wqkv, vectors, (second_stack,))

    e_l, o_l, linv_l, att_keep, att_send = long_forward(q_l, k_l, vt_l)
    if layout.pieces:
        second = layout.gather_core(second_plane[:1] + list(tie(second_plane[1:], (att_keep,))))
    layer_out, mid_l, mid_s, da_keep, da_send, da_s, feed_rows, hidden_sum, *second_grads = feed(
        layout, place, rows, id_column, upstream, att_keep, layout.flip(att_send, 1), att_s, vectors, hidden_shift, second
    )
    da_other = layout.flip(da_send, 1)
    inputs = (place, e_l, k_l, vt_l, n1_l, q_l, da_keep, da_other, o_l, linv_l, wqkv, vectors)

    pairs = layout.scatter_core(second_grads) if layout.pieces else []
    keep_x, send_x, _, *sums = long_backward(layout, False, *inputs, (), tuple(pairs[1:]))
    moved = (keep_x.astype(f32) + layout.flip(send_x, 1).astype(f32)).astype(bf16)
    totals = layout.scatter_plane(pairs) if layout.pieces else []
    keep, send, gq, _, gkv, long_sums, long_side = long_backward(
        layout, True, *inputs, sums, (moved, *totals[1:])
    )
    dx_totals = layout.add_depth([keep, layout.flip(send, 1), layout.flip(moved, 2)])
    dx_s, *first_grads = short_backward(
        layout, place, e_s, k_s, v_s, q_s, kt_s, da_s, o_s, linv_s, n1, rows, mid_s, wqkv, vectors,
        gq, gkv, long_sums, long_side, feed_rows, hidden_sum, tuple(dx_totals[1:]),
    )
    dx_long = layout.scatter_depth(dx_totals, -1)
    if layout.pieces:
        second_grad = layout.scatter_depth(totals)
        narrow_grad = second_grad[:, WIDTH + FF :].reshape(shard, 4, WIDTH).transpose(1, 0, 2)
        narrow_grad = narrow_grad.reshape(4 * shard, WIDTH)
        first_grad = layout.scatter_depth(layout.scatter_plane(layout.scatter_core(first_grads)))
        hidden_grad = first_grad[0, FIRST - 4 * shard :]
    else:
        packed = second_grads[0][:, WIDTH + FF :].reshape(WIDTH // 16, 16, 4, WIDTH).transpose(0, 2, 1, 3)
        narrow_grad = layout.scatter_whole(packed.reshape(FF, WIDTH))
        second_grad = layout.scatter_whole(second_grads[0][:, : WIDTH + FF])
        first_grad = layout.scatter_whole(first_grads[0])
        hidden_grad = layout.scatter_whole(hidden_sum[0])
    small = first_grad[:, 3 * WIDTH :]

    standard, inverse = standardize(rows[:LONG].astype(f32))
    dx_l = (mid_l + norm_backward(dx_long, standard, inverse, vectors[V_G1][None, :])).astype(bf16)
    input_grad = jnp.concatenate([dx_l, dx_s], axis=0)
    return (
        layer_out[None],
        input_grad[None],
        first_grad[:, : 3 * WIDTH],
        second_grad[:, :WIDTH],
        second_grad[:, WIDTH : WIDTH + FF],
        narrow_grad,
        small[:, 0],
        small[:, 1],
        small[:, 2],
        hidden_grad,
        small[:, 3],
        small[:, 4],
        small[:, 5],
        small[:, 6],
        small[:, 7],
    )


def solution(mesh):
    shards = P(("band", "batch"))
    tokens = P("batch", "band", None)
    kernels = P(("band", "batch"), None)
    in_specs = (
        (tokens, P("batch", "band")) + (kernels,) * 4 + (shards,) * 9 + (tokens,)
    )
    out_specs = (tokens, tokens) + (kernels,) * 4 + (shards,) * 9
    return jax.shard_map(
        per_device, mesh=mesh, in_specs=in_specs, out_specs=out_specs, check_vma=False
    )
```

```python
import functools
import math

import jax
import jax.numpy as jnp
from jax import lax
from jax.experimental import pallas as pl
from jax.experimental.pallas import tpu as pltpu
from jax.sharding import PartitionSpec as P

HEADS = 8
HEAD = 64
LONG = 256
WIDTH = 512
FF = 2048
GROUP = 256
TILE = 512
epsilon = 1e-06
gelu_scale = 0.7978845608028654
f32 = jnp.float32
bf16 = jnp.bfloat16
PARAMS = dict(vmem_limit_bytes=58 << 20)


def dot(left, right, cl=1, cr=0):
    return lax.dot_general(left, right, (((cl,), (cr,)), ((), ())), preferred_element_type=f32)


def standardize(rows):
    center = rows - jnp.mean(rows, axis=1, keepdims=True)
    inverse = lax.rsqrt(jnp.mean(center * center, axis=1, keepdims=True) + epsilon)
    return center * inverse, inverse


def norm_backward(incoming, standard, inverse, scaling):
    scaled = incoming * scaling
    return inverse * (
        scaled
        - jnp.mean(scaled, axis=1, keepdims=True)
        - standard * jnp.mean(scaled * standard, axis=1, keepdims=True)
    )


def column_sum(rows):
    return jnp.sum(rows, axis=0, keepdims=True)


def head_lanes(block, head):
    lane = lax.broadcasted_iota(jnp.int32, block.shape, 1) // HEAD
    return jnp.where(lane == head, block.astype(f32), 0.0).astype(bf16)


V_ASK, V_CONTENT, V_MIXER, V_NARROW, V_G1, V_O1, V_G2, V_O2 = range(8)


def row_of(table_ref, index):
    return table_ref[index : index + 1, :]


def whole(shape):
    return pl.BlockSpec(shape, lambda *_: (0,) * len(shape))


def once(shape):
    return pl.BlockSpec(shape, lambda *_: (0,) * len(shape), pipeline_mode=pl.Buffered(1))


ANYWHERE = pl.BlockSpec(memory_space=pl.ANY)


def behind(kernel, count, prefetch=True):
    skip = 1 if prefetch else 0
    return lambda *refs: kernel(*refs[:skip], *refs[skip + count :])


SIDE = 128
FIRST = 3 * WIDTH + SIDE
SECOND = WIDTH + 2 * FF


class Layout:
    def __init__(self, bands, batches):
        self.bands, self.batches = bands, batches
        self.depth = bands // 4
        self.shards = bands * batches
        self.rows = WIDTH // self.shards
        self.pieces = self.rows % 16 == 0
        self.plane = [(kx, ky) for kx in (0, 1) for ky in range(batches)]

    def shard(self, place, kc, kx, ky, kz, sign):
        z = lax.rem(place[2] + (self.depth + sign * kz), self.depth)
        x = lax.rem(place[3] + kx, 2)
        y = lax.rem(place[4] + (self.batches + sign * ky), self.batches)
        core = lax.rem(place[1] + kc, 2)
        return ((z * 2 + x) * 2 + core) * self.batches + y

    def chip(self, place, kx, kz):
        return lax.rem(place[2] + kz, self.depth) * 2 + lax.rem(place[3] + kx, 2)

    def shift_depth(self, block, k):
        pairs = [(i, ((i // 4 + k) % self.depth) * 4 + i % 4) for i in range(self.bands)]
        return lax.ppermute(block, "band", pairs)

    def flip(self, block, bit):
        return lax.ppermute(block, "band", [(i, i ^ bit) for i in range(self.bands)])

    def shift_plane(self, block, kx, ky):
        n = self.batches
        pairs = [
            (b * n + y, (b ^ (2 * kx)) * n + (y + ky) % n) for b in range(self.bands) for y in range(n)
        ]
        return lax.ppermute(block, ("band", "batch"), pairs)

    def gather_depth(self, block, deps=()):
        return stack_blocks([block] + [self.shift_depth(block, k) for k in range(1, self.depth)], deps)

    def gather_plane(self, stack):
        return [stack if k == (0, 0) else self.shift_plane(stack, *k) for k in self.plane]

    def gather_core(self, plane):
        return plane + [self.flip(part, 1) for part in plane]

    def gather_whole(self, block):
        return [lax.all_gather(block, ("band", "batch"), axis=0, tiled=True)]

    def gathered_specs(self, columns):
        if not self.pieces:
            return [once((WIDTH, columns))]
        return [once((self.depth, self.rows, columns))] * (2 * len(self.plane))

    def each_gathered(self, place, refs, visit):
        if not self.pieces:
            for low in range(0, WIDTH, 16):
                visit(low // 16, refs[0][low : low + 16, :])
            return
        index = 0
        for kc in (0, 1):
            for kx, ky in self.plane:
                for kz in range(self.depth):
                    visit(self.shard(place, kc, kx, ky, kz, -1), refs[index][kz])
                index += 1

    def scattered_shapes(self, columns):
        if not self.pieces:
            return [jax.ShapeDtypeStruct((WIDTH, columns), bf16)]
        shape = (len(self.plane), self.depth, self.rows, columns)
        return [jax.ShapeDtypeStruct(shape, bf16)] * 2

    def store_scattered(self, place, refs, take):
        if not self.pieces:
            for low in range(0, WIDTH, 16):
                refs[0][low : low + 16, :] = take(low // 16)
            return
        for kc in (0, 1):
            for n, (kx, ky) in enumerate(self.plane):
                for kz in range(self.depth):
                    refs[kc][n, kz] = take(self.shard(place, kc, kx, ky, kz, 1))

    def scatter_core(self, parts):
        keep, send = parts
        arrived = self.flip(send, 1)
        return [(keep[n].astype(f32) + arrived[n].astype(f32)).astype(bf16) for n in range(len(self.plane))]

    def scatter_plane(self, pairs):
        arrived = [self.shift_plane(pairs[n], *k) for n, k in enumerate(self.plane) if n]
        return self.add_depth(pairs[:1] + arrived)

    def add_depth(self, stacks):
        totals = []
        for k in range(self.depth):
            total = stacks[0][k].astype(f32)
            for stack in stacks[1:]:
                total = total + stack[k].astype(f32)
            totals.append(total if k == 0 else total.astype(bf16))
        return totals

    def scatter_depth(self, totals, sign=1):
        final = totals[0]
        for k in range(1, self.depth):
            final = final + self.shift_depth(totals[k], (sign * k) % self.depth).astype(f32)
        return final

    def scatter_whole(self, part):
        return lax.psum_scatter(part, ("band", "batch"), scatter_dimension=0, tiled=True).astype(f32)


def tie(values, deps):
    count = len(values)
    return pl.pallas_call(
        lambda *refs: None,
        in_specs=[ANYWHERE] * (count + len(deps)),
        out_specs=[ANYWHERE] * count,
        out_shape=[jax.ShapeDtypeStruct(v.shape, v.dtype) for v in values],
        input_output_aliases={i: i for i in range(count)},
        name="tie",
    )(*values, *deps)


def stack_kernel(*refs):
    for index, ref in enumerate(refs[:-1]):
        refs[-1][index] = ref[...]


def stack_blocks(blocks, deps):
    shape = blocks[0].shape
    return pl.pallas_call(
        behind(stack_kernel, len(deps), False),
        in_specs=[ANYWHERE] * len(deps) + [pl.BlockSpec(memory_space=pltpu.VMEM)] * len(blocks),
        out_shape=jax.ShapeDtypeStruct((len(blocks), *shape), blocks[0].dtype),
        name="stack_blocks",
    )(*deps, *blocks)


def pack_first_kernel(triple_ref, *refs):
    vectors, wide, out_ref, table = refs[:8], *refs[8:]
    shard = triple_ref.shape[0]
    table[...] = jnp.zeros_like(table)
    for index, ref in enumerate(vectors):
        table[index : index + 1, :shard] = ref[...]
    out_ref[:, : 3 * WIDTH] = triple_ref[...].astype(bf16)
    turned = table[...].T[:shard, :]
    across = jnp.pad(wide[...], ((0, shard - 1), (SIDE - 4 * shard, 0)))
    out_ref[:, 3 * WIDTH :] = (turned + across).astype(bf16)


def pack_first(triple, vectors, wide):
    shard = triple.shape[0]
    return pl.pallas_call(
        pack_first_kernel,
        out_shape=jax.ShapeDtypeStruct((shard, FIRST), bf16),
        scratch_shapes=[pltpu.VMEM((SIDE, SIDE), f32)],
        compiler_params=pltpu.CompilerParams(**PARAMS),
        name="pack_first",
    )(triple, *[v[None, :] for v in vectors], wide[None, :])


def pack_rows_kernel(rows_ref, out_ref):
    out_ref[...] = rows_ref[...]


def pack_rows(rows, deps):
    block = pl.BlockSpec((LONG, WIDTH), lambda i: (0, 0))
    return pl.pallas_call(
        behind(pack_rows_kernel, len(deps), False),
        grid=(1,),
        in_specs=[ANYWHERE] * len(deps) + [block],
        out_specs=block,
        out_shape=jax.ShapeDtypeStruct((LONG, WIDTH), bf16),
        name="pack_rows",
    )(*deps, rows)


def pack_second_kernel(mixer_ref, widening_ref, narrowing_ref, out_ref):
    shard = mixer_ref.shape[0]
    out_ref[:, :WIDTH] = mixer_ref[...].astype(bf16)
    out_ref[:, WIDTH : WIDTH + FF] = widening_ref[...].astype(bf16)
    for k in range(4):
        low = WIDTH + FF + k * WIDTH
        out_ref[:, low : low + WIDTH] = narrowing_ref[k * shard : (k + 1) * shard, :].astype(bf16)


def pack_second(mixer, widening, narrowing, deps):
    blocks = [pl.BlockSpec(memory_space=pltpu.VMEM)] * 3
    return pl.pallas_call(
        behind(pack_second_kernel, len(deps), False),
        out_shape=jax.ShapeDtypeStruct((mixer.shape[0], SECOND), bf16),
        in_specs=[ANYWHERE] * len(deps) + blocks,
        compiler_params=pltpu.CompilerParams(**PARAMS),
        name="pack_second",
    )(*deps, mixer, widening, narrowing)


def short_qkv_kernel(layout, place_ref, x_ref, *refs):
    count = len(layout.gathered_specs(FIRST))
    pieces = refs[:count]
    n1_ref, q_ref, k_ref, v_ref, kt_ref, vt_ref, w_ref, vec_ref, hid_ref, side, spread = refs[count:]

    @pl.when(pl.program_id(0) == 0)
    def _():
        def visit(block, rows):
            span = pl.ds(pl.multiple_of(block * 16, 16), 16)
            w_ref[span, :] = rows[:, : 3 * WIDTH]
            side[span, :] = rows[:, 3 * WIDTH :].astype(f32)
            if layout.pieces:
                spread[pl.ds(block, 1), :] = rows[0:1, 3 * WIDTH :].astype(f32)

        layout.each_gathered(place_ref, pieces, visit)
        vec_ref[...] = side[...].T[:16, :]
        if layout.pieces:
            shard = 4 * layout.rows
            for index in range(layout.shards):
                hid_ref[:, index * shard : (index + 1) * shard] = spread[index : index + 1, SIDE - shard :]

    standard, _ = standardize(x_ref[...].astype(f32))
    normed = (standard * row_of(vec_ref, V_G1) + row_of(vec_ref, V_O1)).astype(bf16)
    n1_ref[...] = normed
    projected = dot(normed, w_ref[...])
    q = (projected[:, :WIDTH] + row_of(vec_ref, V_ASK)).astype(bf16)
    q_ref[...] = (q.astype(f32) * (1.0 / math.sqrt(HEAD))).astype(bf16)
    k = projected[:, WIDTH : 2 * WIDTH]
    v = projected[:, 2 * WIDTH :] + row_of(vec_ref, V_CONTENT)
    k_ref[...] = k.astype(bf16)
    v_ref[...] = v.astype(bf16)
    kt_ref[...] = k.T.astype(bf16)
    vt_ref[...] = v.T.astype(bf16)


def short_qkv(layout, place, rows, pieces):
    count = rows.shape[0] - LONG
    block = 256
    row_spec = pl.BlockSpec((block, WIDTH), lambda i, _: (i, 0))
    col_spec = pl.BlockSpec((WIDTH, block), lambda i, _: (0, i))
    flat = jax.ShapeDtypeStruct((count, WIDTH), bf16)
    tall = jax.ShapeDtypeStruct((WIDTH, count), bf16)
    return pl.pallas_call(
        functools.partial(short_qkv_kernel, layout),
        grid_spec=pltpu.PrefetchScalarGridSpec(
            num_scalar_prefetch=1,
            grid=(count // block,),
            in_specs=[pl.BlockSpec((block, WIDTH), lambda i, _: (i + LONG // block, 0))]
            + layout.gathered_specs(FIRST),
            out_specs=[row_spec, row_spec, row_spec, row_spec, col_spec, col_spec]
            + [once((WIDTH, 3 * WIDTH)), whole((16, WIDTH)), whole((1, FF))],
            scratch_shapes=[pltpu.VMEM((WIDTH, SIDE), f32), pltpu.VMEM((max(8, layout.shards), SIDE), f32)],
        ),
        out_shape=[flat, flat, flat, flat, tall, tall]
        + [
            jax.ShapeDtypeStruct((WIDTH, 3 * WIDTH), bf16),
            jax.ShapeDtypeStruct((16, WIDTH), f32),
            jax.ShapeDtypeStruct((1, FF), f32),
        ],
        compiler_params=pltpu.CompilerParams(**PARAMS),
        cost_estimate=pl.CostEstimate(
            flops=2 * count * WIDTH * 3 * WIDTH, bytes_accessed=10 << 20, transcendentals=0
        ),
        name="short_qkv",
    )(place, rows, *pieces)


def short_forward_kernel(
    q_ref, k_ref, vt_ref, idc_ref, idr_ref, e_ref, o_ref, linv_ref, att_ref, s_ref, bias_ref, top_ref
):
    step = pl.program_id(0)
    count = k_ref.shape[0]

    @pl.when(step == 0)
    def _():
        same = idc_ref[...] == idr_ref[...]
        bias_ref[...] = jnp.where(same, 0.0, -1e30)

    tile = 256

    def first(slot, low, masked):
        span = slice(low, low + tile)
        s = dot(k_ref[...], masked[span, :], 1, 1) + bias_ref[:, span]
        s_ref[slot, :, span] = s
        top_ref[slot, :, span] = jnp.broadcast_to(jnp.max(s, axis=0, keepdims=True), (8, tile))

    def second(slot, low):
        span = slice(low, low + tile)
        own = pl.ds(pl.multiple_of((step - 1) * HEAD, HEAD), HEAD)
        e = jnp.exp(s_ref[slot, :, span] - top_ref[slot, 0:1, span])
        linv = 1.0 / column_sum(e)
        low_e = e.astype(bf16)
        e_ref[:, span] = low_e
        linv_ref[:, span] = jnp.broadcast_to(linv, (8, tile))
        o_ref[own, span] = dot(vt_ref[own, :], low_e) * linv

    def masked_queries():
        return head_lanes(q_ref[...], lax.rem(step, 4))

    last = pl.num_programs(0) - 1

    @pl.when(step == 0)
    def _():
        masked = masked_queries()
        for low in range(0, count, tile):
            first(0, low, masked)

    for parity in (0, 1):
        @pl.when((step > 0) & (step < last) & (lax.rem(step, 2) == parity))
        def _():
            masked = masked_queries()
            for low in range(0, count, tile):
                first(parity, low, masked)
                second(1 - parity, low)

    @pl.when(step == last)
    def _():
        for low in range(0, count, tile):
            second((HEADS - 1) % 2, low)
        for low in range(0, WIDTH, 128):
            att_ref[:, low : low + 128] = o_ref[low : low + 128, :].T.astype(bf16)


def short_forward(q, k, vt, ids, deps):
    count = q.shape[0]
    now = lambda s: (0, jnp.minimum(s, HEADS - 1) // 4)
    before = lambda s: (0, jnp.maximum(s - 1, 0))
    return pl.pallas_call(
        behind(short_forward_kernel, len(deps), False),
        grid=(HEADS + 1,),
        in_specs=[ANYWHERE] * len(deps)
        + [
            pl.BlockSpec((count, GROUP), now),
            pl.BlockSpec((count, GROUP), now),
            whole((WIDTH, count)),
            whole((count, 1)),
            whole((1, count)),
        ],
        out_specs=[
            pl.BlockSpec((count, count), before),
            whole((WIDTH, count)),
            pl.BlockSpec((8, count), lambda s: (jnp.maximum(s - 1, 0), 0)),
            whole((count, WIDTH)),
        ],
        out_shape=[
            jax.ShapeDtypeStruct((count, HEADS * count), bf16),
            jax.ShapeDtypeStruct((WIDTH, count), f32),
            jax.ShapeDtypeStruct((HEADS * 8, count), f32),
            jax.ShapeDtypeStruct((count, WIDTH), bf16),
        ],
        scratch_shapes=[
            pltpu.VMEM((2, count, count), f32),
            pltpu.VMEM((count, count), f32),
            pltpu.VMEM((2, 8, count), f32),
        ],
        compiler_params=pltpu.CompilerParams(**PARAMS),
        cost_estimate=pl.CostEstimate(
            flops=12 * count * count * WIDTH, bytes_accessed=12 << 20, transcendentals=HEADS * count * count
        ),
        name="short_forward",
    )(*deps, q, k, vt, ids[:, None], ids[None, :])


CHIPS = 2


def long_prepare_kernel(
    depth, place_ref, own0, other0, own1, other1, w_ref, vec_ref, n1_ref, q_ref, k_ref, vt_ref,
    wk, wv,
):
    step = pl.program_id(0)
    core = place_ref[1]
    near = step < depth
    lanes = lambda base: pl.ds(pl.multiple_of(base + core * GROUP, GROUP), GROUP)

    @pl.when(step == 0)
    def _():
        for other in (0, 1):
            @pl.when(core == other)
            def _():
                wk[...] = w_ref[:, WIDTH + other * GROUP : WIDTH + (other + 1) * GROUP]
                wv[...] = w_ref[:, 2 * WIDTH + other * GROUP : 2 * WIDTH + (other + 1) * GROUP]

    chips = own0.shape[0]
    rows = jnp.concatenate(
        [jnp.where(near, a[chip], b[chip]) for chip in range(chips) for a, b in ((own0, own1), (other0, other1))],
        axis=0,
    )
    standard, _ = standardize(rows.astype(f32))
    normed = (standard * row_of(vec_ref, V_G1) + row_of(vec_ref, V_O1)).astype(bf16)
    n1_ref[...] = normed
    k = dot(normed, wk[...])
    v = dot(normed, wv[...]) + vec_ref[V_CONTENT : V_CONTENT + 1, lanes(0)]
    k_ref[...] = k.astype(bf16)
    vt_ref[...] = v.astype(bf16).T

    @pl.when(step == 0)
    def _():
        q = (dot(normed[:TILE, :], w_ref[:, lanes(0)]) + vec_ref[V_ASK : V_ASK + 1, lanes(0)]).astype(bf16)
        q_ref[...] = (q.astype(f32) * (1.0 / math.sqrt(HEAD))).astype(bf16)


def long_prepare(layout, place, stacks, weights, vectors, deps):
    depth = layout.depth
    total = 2 * depth * TILE
    steps = depth // CHIPS
    tile = CHIPS * TILE
    row_spec = pl.BlockSpec((tile, GROUP), lambda i, _: (i, 0))
    col_spec = pl.BlockSpec((GROUP, tile), lambda i, _: (0, i))
    near = pl.BlockSpec((CHIPS, LONG, WIDTH), lambda i, _: (jnp.minimum(i, steps - 1), 0, 0))
    far = pl.BlockSpec((CHIPS, LONG, WIDTH), lambda i, _: (jnp.maximum(i - steps, 0), 0, 0))
    flat = jax.ShapeDtypeStruct((total, GROUP), bf16)
    tall = jax.ShapeDtypeStruct((GROUP, total), bf16)
    return pl.pallas_call(
        behind(functools.partial(long_prepare_kernel, depth // CHIPS), len(deps)),
        grid_spec=pltpu.PrefetchScalarGridSpec(
            num_scalar_prefetch=1,
            grid=(2 * steps,),
            in_specs=[ANYWHERE] * len(deps)
            + [near, near, far, far, whole((WIDTH, 3 * WIDTH)), whole(vectors.shape)],
            out_specs=[
                pl.BlockSpec((tile, WIDTH), lambda i, _: (i, 0)),
                whole((TILE, GROUP)),
                row_spec,
                col_spec,
            ],
            scratch_shapes=[pltpu.VMEM((WIDTH, GROUP), bf16)] * 2,
        ),
        out_shape=[
            jax.ShapeDtypeStruct((total, WIDTH), bf16),
            jax.ShapeDtypeStruct((TILE, GROUP), bf16),
            flat,
            tall,
        ],
        compiler_params=pltpu.CompilerParams(**PARAMS),
        cost_estimate=pl.CostEstimate(
            flops=4 * total * WIDTH * GROUP, bytes_accessed=18 << 20, transcendentals=0
        ),
        name="long_prepare",
    )(place, *deps, *stacks, weights, vectors)


CHUNK = 256
BACK = 2 * TILE
PARTS = TILE // CHUNK
LOCAL_HEADS = GROUP // HEAD
STEPS = LOCAL_HEADS * PARTS


def long_forward_kernel(
    q_ref, k_ref, vt_ref, e_ref, o_ref, linv_ref, keep_ref, send_ref, s_ref, top_ref
):
    step = pl.program_id(0)
    total = k_ref.shape[0]
    tile = min(total, 4096)
    last = pl.num_programs(0) - 1

    def masked_queries():
        rows = pl.ds(pl.multiple_of(lax.rem(step, PARTS) * CHUNK, CHUNK), CHUNK)
        return head_lanes(q_ref[rows, :], step // PARTS)

    def first_tile(slot, low, masked, top):
        s = dot(k_ref[pl.ds(low, tile), :], masked, 1, 1)
        s_ref[slot, pl.ds(low, tile), :] = s
        return jnp.maximum(top, jnp.max(s.reshape(tile // 8, 8, CHUNK), axis=0))

    def second_tile(slot, low, top, head, carry):
        summed, mixed = carry
        e = jnp.exp(s_ref[slot, pl.ds(low, tile), :] - top)
        summed = summed + jnp.sum(e.reshape(tile // 8, 8, CHUNK), axis=0)
        low_e = e.astype(bf16)
        e_ref[pl.ds(low, tile), :] = low_e
        values = vt_ref[pl.ds(pl.multiple_of(head * HEAD, HEAD), HEAD), pl.ds(low, tile)]
        return summed, mixed + dot(values, low_e)

    start_top = jnp.full((8, CHUNK), -1e30, f32)
    start_sum = (jnp.zeros((8, CHUNK), f32), jnp.zeros((HEAD, CHUNK), f32))

    def finish(head, part, carry):
        summed, mixed = carry
        linv = 1.0 / column_sum(summed)
        linv_ref[...] = jnp.broadcast_to(linv, (8, CHUNK))
        o_ref[part, pl.ds(pl.multiple_of(head * HEAD, HEAD), HEAD), :] = mixed * linv

    def place(turn):
        return pl.multiple_of(turn * tile, tile)

    @pl.when(step == 0)
    def _():
        masked = masked_queries()
        top_ref[0] = lax.fori_loop(
            0, total // tile, lambda t, top: first_tile(0, place(t), masked, top), start_top
        )

    for parity in (0, 1):
        @pl.when((step > 0) & (step < last) & (lax.rem(step, 2) == parity))
        def _():
            masked = masked_queries()
            before = step - 1
            head = before // PARTS
            top_row = jnp.max(top_ref[1 - parity], axis=0, keepdims=True)

            def body(turn, carry):
                top, kept = carry
                low = place(turn)
                top = first_tile(parity, low, masked, top)
                kept = second_tile(1 - parity, low, top_row, head, kept)
                return top, kept

            top, kept = lax.fori_loop(0, total // tile, body, (start_top, start_sum))
            top_ref[parity] = top
            finish(head, lax.rem(before, PARTS), kept)

    @pl.when(step == last)
    def _():
        slot = (STEPS - 1) % 2
        top_row = jnp.max(top_ref[slot], axis=0, keepdims=True)
        head = LOCAL_HEADS - 1
        kept = lax.fori_loop(
            0,
            total // tile,
            lambda t, carry: second_tile(slot, place(t), top_row, head, carry),
            start_sum,
        )
        finish(head, PARTS - 1, kept)
        keep_ref[...] = o_ref[0].T.astype(bf16)
        send_ref[...] = o_ref[1].T.astype(bf16)


def long_forward(q, k, vt):
    total = k.shape[0]
    before = lambda s: jnp.maximum(s - 1, 0)
    half = jax.ShapeDtypeStruct((CHUNK, GROUP), bf16)
    return pl.pallas_call(
        long_forward_kernel,
        grid=(STEPS + 1,),
        in_specs=[once((TILE, GROUP)), once((total, GROUP)), once((GROUP, total))],
        out_specs=[
            pl.BlockSpec((total, CHUNK), lambda s: (0, before(s))),
            whole((PARTS, GROUP, CHUNK)),
            pl.BlockSpec((8, CHUNK), lambda s: (before(s), 0)),
            whole((CHUNK, GROUP)),
            whole((CHUNK, GROUP)),
        ],
        scratch_shapes=[pltpu.VMEM((2, total, CHUNK), f32), pltpu.VMEM((2, 8, CHUNK), f32)],
        out_shape=[
            jax.ShapeDtypeStruct((total, STEPS * CHUNK), bf16),
            jax.ShapeDtypeStruct((PARTS, GROUP, CHUNK), f32),
            jax.ShapeDtypeStruct((STEPS * 8, CHUNK), f32),
            half,
            half,
        ],
        compiler_params=pltpu.CompilerParams(**PARAMS),
        cost_estimate=pl.CostEstimate(
            flops=16 * TILE * total * GROUP, bytes_accessed=24 << 20, transcendentals=4 * TILE * total
        ),
        name="long_forward",
    )(q, k, vt)


def feed_kernel(layout, place_ref, x_ref, ids_ref, g_ref, mine_ref, other_ref, short_ref, vec_ref, hid_ref, *refs):
    count = len(layout.gathered_specs(SECOND))
    pieces, refs = refs[:count], refs[count:]
    out_ref, midl_ref, mids_ref, keep_ref, send_ref, das_ref, row_ref, hsum_ref = refs[:8]
    grads = refs[8:-8]
    wp_ref, we_ref, wr_ref, gp_ref, ge_ref, gr_ref, act_ref, dh_ref = refs[-8:]
    swapped = place_ref[1] == 1

    def visit(block, rows):
        span = pl.ds(pl.multiple_of(block * 16, 16), 16)
        wp_ref[span, :] = rows[:, :WIDTH]
        we_ref[span, :] = rows[:, WIDTH : WIDTH + FF]
        for k in range(4):
            low = WIDTH + FF + k * WIDTH
            wr_ref[pl.ds(pl.multiple_of(block * 64 + 16 * k, 16), 16), :] = rows[:, low : low + WIDTH]

    layout.each_gathered(place_ref, pieces, visit)

    x = x_ref[...].astype(f32)
    live = (ids_ref[...] >= 0).astype(f32)
    upstream = g_ref[...].astype(f32)
    mine, other = mine_ref[...], other_ref[...]
    long = jnp.concatenate([jnp.where(swapped, other, mine), jnp.where(swapped, mine, other)], axis=1)
    attended = jnp.concatenate([long, short_ref[...]], axis=0)
    branch = dot(attended, wp_ref[...]) + row_of(vec_ref, V_MIXER)
    middle = x + live * branch
    standard, inverse = standardize(middle)
    gain = row_of(vec_ref, V_G2)
    normed = (standard * gain + row_of(vec_ref, V_O2)).astype(bf16)
    branch_low = (live * upstream).astype(bf16)

    part = 256

    def products(low):
        return (
            dot(normed, we_ref[:, low : low + part]) + hid_ref[:, low : low + part],
            dot(branch_low, wr_ref[low : low + part, :], 1, 1),
        )

    following = products(0)
    for low in range(0, FF, part):
        hidden, into = following
        if low + part < FF:
            following = products(low + part)
        square = hidden * hidden
        tangent = jnp.tanh(hidden * (gelu_scale + (gelu_scale * 0.044715) * square))
        half = 0.5 + 0.5 * tangent
        active = (hidden * half).astype(bf16)
        slope = half + (0.5 * hidden) * (1.0 - tangent * tangent) * (
            gelu_scale + (gelu_scale * 3.0 * 0.044715) * square
        )
        hidden_low = (into * slope).astype(bf16)
        hsum_ref[:, low : low + part] = column_sum(hidden_low.astype(f32))
        act_ref[:, low : low + part] = active
        dh_ref[:, low : low + part] = hidden_low
        gr_ref[low : low + part, :] = dot(active, branch_low, 0, 0).astype(bf16)
        ge_ref[:, low : low + part] = dot(normed, hidden_low, 0, 0).astype(bf16)

    branch_two = dot(act_ref[...], wr_ref[...]) + row_of(vec_ref, V_NARROW)
    out_ref[...] = (middle + live * branch_two).astype(bf16)
    normed_grad = dot(dh_ref[...], we_ref[...], 1, 1)
    middle_grad = upstream + norm_backward(normed_grad, standard, inverse, gain)
    midl_ref[...] = middle_grad[:LONG, :]
    mids_ref[...] = middle_grad[LONG:, :]
    attn_low = (live * middle_grad).astype(bf16)
    attended_grad = dot(attn_low, wp_ref[...], 1, 1).astype(bf16)
    das_ref[...] = attended_grad[LONG:, :]
    left, right = attended_grad[:LONG, :GROUP], attended_grad[:LONG, GROUP:]
    keep_ref[...] = jnp.where(swapped, right, left)
    send_ref[...] = jnp.where(swapped, left, right)
    gp_ref[...] = dot(attended, attn_low, 0, 0).astype(bf16)
    row_ref[...] = jnp.zeros_like(row_ref)
    row_ref[0:1, :] = column_sum(attn_low.astype(f32))
    row_ref[1:2, :] = column_sum(branch_low.astype(f32))
    row_ref[2:3, :] = column_sum(normed_grad * standard)
    row_ref[3:4, :] = column_sum(normed_grad)

    def take(block):
        span = pl.ds(pl.multiple_of(block * 16, 16), 16)
        parts = [gp_ref[span, :], ge_ref[span, :]] + [
            gr_ref[pl.ds(pl.multiple_of(block * 64 + 16 * k, 16), 16), :] for k in range(4)
        ]
        return jnp.concatenate(parts, axis=1)

    layout.store_scattered(place_ref, grads, take)


def feed(layout, place, rows, ids, upstream, mine, other, short, vectors, hidden_shift, pieces):
    count = rows.shape[0]
    grads = layout.scattered_shapes(SECOND)
    operands = [rows, ids[:, None], upstream, mine, other, short, vectors, hidden_shift]
    shapes = [
        jax.ShapeDtypeStruct((count, WIDTH), bf16),
        jax.ShapeDtypeStruct((LONG, WIDTH), f32),
        jax.ShapeDtypeStruct((count - LONG, WIDTH), f32),
        jax.ShapeDtypeStruct((LONG, GROUP), bf16),
        jax.ShapeDtypeStruct((LONG, GROUP), bf16),
        jax.ShapeDtypeStruct((count - LONG, WIDTH), bf16),
        jax.ShapeDtypeStruct((8, WIDTH), f32),
        jax.ShapeDtypeStruct((1, FF), f32),
    ] + grads
    return pl.pallas_call(
        functools.partial(feed_kernel, layout),
        grid_spec=pltpu.PrefetchScalarGridSpec(
            num_scalar_prefetch=1,
            grid=(1,),
            in_specs=[once(x.shape) for x in operands] + layout.gathered_specs(SECOND),
            out_specs=[once(x.shape) for x in shapes],
            scratch_shapes=[
                pltpu.VMEM((WIDTH, WIDTH), bf16),
                pltpu.VMEM((WIDTH, FF), bf16),
                pltpu.VMEM((FF, WIDTH), bf16),
                pltpu.VMEM((WIDTH, WIDTH), bf16),
                pltpu.VMEM((WIDTH, FF), bf16),
                pltpu.VMEM((FF, WIDTH), bf16),
                pltpu.VMEM((count, FF), bf16),
                pltpu.VMEM((count, FF), bf16),
            ],
        ),
        out_shape=shapes,
        compiler_params=pltpu.CompilerParams(**PARAMS),
        cost_estimate=pl.CostEstimate(
            flops=6 * count * WIDTH * (WIDTH + 2 * FF), bytes_accessed=18 << 20, transcendentals=count * FF
        ),
        name="feed",
    )(place, *operands, *pieces)


def long_backward_kernel(
    final, place_ref, e_ref, k_ref, vt_ref, n1_ref, q_ref, mine_ref, other_ref, o_ref, linv_ref, w_ref, vec_ref,
    *refs,
):
    if final:
        dq_in, gkv_in, row_in, side_in, *refs = refs
    (
    keep_ref, send_ref, gq_ref, dq_acc, gkv_ref, row_ref, side_ref,
    qblk, dblk, delta, ds_ref, wq, wkv,
    ) = refs
    step = pl.program_id(0)
    core = place_ref[1]

    @pl.when(step == 0)
    def _():
        lanes = lambda base: pl.ds(pl.multiple_of(base + core * GROUP, GROUP), GROUP)
        wq[...] = w_ref[:, lanes(0)]
        wkv[:, :GROUP] = w_ref[:, lanes(WIDTH)]
        wkv[:, GROUP:] = w_ref[:, lanes(2 * WIDTH)]
        if final:
            dq_acc[...] = dq_in[...]
            gkv_ref[...] = gkv_in[...]
            row_ref[...] = row_in[...]
            side_ref[...] = side_in[...]
        else:
            for ref in (dq_acc, gkv_ref, row_ref, side_ref):
                ref[...] = jnp.zeros_like(ref)
        for part in range(PARTS):
            rows = slice(part * CHUNK, (part + 1) * CHUNK)
            turned = (mine_ref, other_ref)[part][...].astype(f32).T
            product = turned * o_ref[part]
            pieces = []
            for head in range(LOCAL_HEADS):
                index = head * PARTS + part
                span = slice(head * HEAD, (head + 1) * HEAD)
                linv = linv_ref[8 * index : 8 * index + 1, :]
                delta[8 * index : 8 * index + 8, :] = jnp.broadcast_to(
                    column_sum(product[span, :]) * linv, (8, CHUNK)
                )
                pieces.append(turned[span, :] * linv)
            scaled = jnp.concatenate(pieces, axis=0).T
            for head in range(LOCAL_HEADS):
                index = head * PARTS + part
                span = slice(index * CHUNK, (index + 1) * CHUNK)
                dblk[span, :] = head_lanes(scaled, head)
                qblk[span, :] = head_lanes(q_ref[rows, :], head)

    def span_of(index):
        return slice(index * CHUNK, (index + 1) * CHUNK)

    v = vt_ref[...].T
    kt = k_ref[...].T
    slopes = dot(v, dblk[span_of(0), :], 1, 1)
    for index in range(STEPS):
        head, part = index // PARTS, index % PARTS
        span = span_of(index)
        following = dot(v, dblk[span_of(index + 1), :], 1, 1) if index + 1 < STEPS else None
        ds = (
            e_ref[:, span].astype(f32) * (slopes - delta[8 * index : 8 * index + 1, :])
        ).astype(bf16)
        ds_ref[:, span] = ds
        own = slice(head * HEAD, (head + 1) * HEAD)
        dq_acc[part, own, :] += dot(kt[own, :], ds)
        slopes = following

    value_grad = dot(e_ref[...], dblk[...]).astype(bf16)
    key_grad = dot(ds_ref[...], qblk[...]).astype(bf16)
    both = jnp.concatenate([key_grad, value_grad], axis=1)
    normed = n1_ref[...]
    through = dot(both, wkv[...], 1, 1)
    gkv_ref[...] += dot(normed, both, 0, 0)
    side_ref[1:2, :] += column_sum(value_grad.astype(f32))

    def put(entire):
        low = entire.astype(bf16)
        for chip in range(BACK // TILE):
            base = chip * TILE
            keep_ref[chip] = low[base : base + LONG, :]
            send_ref[chip] = low[base + LONG : base + TILE, :]
        shifts = column_sum(entire)
        scales = column_sum(entire * normed.astype(f32)) - shifts * row_of(vec_ref, V_O1)
        row_ref[0:1, :] += scales / row_of(vec_ref, V_G1)
        row_ref[1:2, :] += shifts

    if not final:
        put(through)
        return
    last = pl.num_programs(0) - 1

    @pl.when(step < last)
    def _():
        put(through)

    @pl.when(step == last)
    def _():
        query_grad = jnp.concatenate(
            [dq_acc[part].T for part in range(PARTS)], axis=0
        ) * (1.0 / math.sqrt(HEAD))
        low = query_grad.astype(bf16)
        put(jnp.concatenate([through[:TILE, :] + dot(low, wq[...], 1, 1), through[TILE:, :]], axis=0))
        gq_ref[...] = dot(normed[:TILE, :], low, 0, 0)
        side_ref[0:1, :] += column_sum(low.astype(f32))


def long_backward(layout, final, place, e, k, vt, normed, q, mine, other, o, linv, weights, vectors, sums, deps):
    tiles = layout.depth * TILE // BACK
    away = (lambda i: i) if not final else (lambda i: lax.rem(i + 1, tiles))
    turn = lambda i: away(i) if final else tiles + i
    out = jax.ShapeDtypeStruct((layout.depth, LONG, WIDTH), bf16)
    out_spec = pl.BlockSpec((BACK // TILE, LONG, WIDTH), lambda i, p: (away(i), 0, 0))
    sum_shapes = [
        jax.ShapeDtypeStruct((PARTS, GROUP, CHUNK), f32),
        jax.ShapeDtypeStruct((WIDTH, 2 * GROUP), f32),
        jax.ShapeDtypeStruct((8, WIDTH), f32),
        jax.ShapeDtypeStruct((8, GROUP), f32),
    ]
    sum_specs = [whole(x.shape) for x in sum_shapes]
    return pl.pallas_call(
        behind(functools.partial(long_backward_kernel, final), len(deps)),
        grid_spec=pltpu.PrefetchScalarGridSpec(
            num_scalar_prefetch=1,
            grid=(tiles,),
            in_specs=[ANYWHERE] * len(deps)
            + [
                pl.BlockSpec((BACK, STEPS * CHUNK), lambda i, p: (turn(i), 0)),
                pl.BlockSpec((BACK, GROUP), lambda i, p: (turn(i), 0)),
                pl.BlockSpec((GROUP, BACK), lambda i, p: (0, turn(i))),
                pl.BlockSpec((BACK, WIDTH), lambda i, p: (turn(i), 0)),
                whole((TILE, GROUP)),
                whole((CHUNK, GROUP)),
                whole((CHUNK, GROUP)),
                whole((PARTS, GROUP, CHUNK)),
                whole((STEPS * 8, CHUNK)),
                once((WIDTH, 3 * WIDTH)),
                whole(vectors.shape),
            ]
            + sum_specs[: len(sums)],
            out_specs=[out_spec, out_spec, whole((WIDTH, GROUP))] + sum_specs,
            scratch_shapes=[
                pltpu.VMEM((STEPS * CHUNK, GROUP), bf16),
                pltpu.VMEM((STEPS * CHUNK, GROUP), bf16),
                pltpu.VMEM((STEPS * 8, CHUNK), f32),
                pltpu.VMEM((BACK, STEPS * CHUNK), bf16),
                pltpu.VMEM((WIDTH, GROUP), bf16),
                pltpu.VMEM((WIDTH, 2 * GROUP), bf16),
            ],
        ),
        out_shape=[out, out, jax.ShapeDtypeStruct((WIDTH, GROUP), f32)] + sum_shapes,
        compiler_params=pltpu.CompilerParams(**PARAMS),
        cost_estimate=pl.CostEstimate(
            flops=20 * TILE * k.shape[0] * GROUP, bytes_accessed=16 << 20, transcendentals=0
        ),
        name="long_backward_final" if final else "long_backward",
    )(place, *deps, e, k, vt, normed, q, mine, other, o, linv, weights, vectors, *sums)


def short_backward_kernel(
    layout, place_ref, e_ref, k_ref, v_ref, q_ref, kt_ref, da_ref, o_ref, linv_ref, n1_ref, x_ref, mid_ref, w_ref,
    vec_ref, gq_ref, gkv_ref, lrow_ref, lside_ref, frow_ref, hsum_ref,
    dx_ref, *refs,
):
    grads = refs[:-9]
    scaled, delta, dblk, qblk, ds_ref, dqt, dqkv, packed, column = refs[-9:]
    step = pl.program_id(0)
    count = k_ref.shape[0]

    @pl.when(step == 0)
    def _():
        for low in range(0, WIDTH, GROUP):
            turned = da_ref[:, low : low + GROUP].astype(f32).T
            product = turned * o_ref[low : low + GROUP, :]
            pieces = []
            for head in range(4):
                span = slice(head * HEAD, (head + 1) * HEAD)
                index = low // HEAD + head
                linv = linv_ref[8 * index : 8 * index + 1, :]
                delta[8 * index : 8 * index + 8, :] = jnp.broadcast_to(
                    column_sum(product[span, :]) * linv, (8, count)
                )
                pieces.append(turned[span, :] * linv)
            scaled[:, low : low + GROUP] = jnp.concatenate(pieces, axis=0).T.astype(bf16)

    def group(side):
        low = side * GROUP
        for head in range(4):
            index = side * 4 + head
            span = slice(head * count, (head + 1) * count)
            own = slice(head * HEAD, (head + 1) * HEAD)
            dblk[span, :] = head_lanes(scaled[:, low : low + GROUP], head)
            qblk[span, :] = head_lanes(q_ref[...], head)
            slopes = dot(v_ref[...], dblk[span, :], 1, 1)
            ds = (
                e_ref[:, span].astype(f32) * (slopes - delta[8 * index : 8 * index + 1, :])
            ).astype(bf16)
            ds_ref[:, span] = ds
            dqt[own, :] = dot(kt_ref[low + head * HEAD : low + (head + 1) * HEAD, :], ds)
        value_grad = dot(e_ref[...], dblk[...])
        key_grad = dot(ds_ref[...], qblk[...])
        query_grad = dqt[...].T * (1.0 / math.sqrt(HEAD))
        dqkv[:, low : low + GROUP] = query_grad.astype(bf16)
        dqkv[:, WIDTH + low : WIDTH + low + GROUP] = key_grad.astype(bf16)
        dqkv[:, 2 * WIDTH + low : 2 * WIDTH + low + GROUP] = value_grad.astype(bf16)

    for side in (0, 1):
        pl.when(step == side)(functools.partial(group, side))

    @pl.when(step == 1)
    def _():
        rows_grad = dot(dqkv[...], w_ref[...], 1, 1)
        standard, inverse = standardize(x_ref[LONG:, :].astype(f32))
        through = norm_backward(rows_grad, standard, inverse, row_of(vec_ref, V_G1))
        dx_ref[...] = (mid_ref[...] + through).astype(bf16)
        core = place_ref[1]
        column[...] = jnp.zeros_like(column)
        column[0:1, :] = column_sum(dqkv[:, :WIDTH].astype(f32))
        column[1:2, :] = column_sum(dqkv[:, 2 * WIDTH :].astype(f32))
        for other in (0, 1):
            @pl.when(core == other)
            def _():
                span = slice(other * GROUP, (other + 1) * GROUP)
                column[0:2, span] += lside_ref[0:2, :]
        column[2:4, :] = frow_ref[0:2, :]
        column[4:5, :] = lrow_ref[0:1, :] + column_sum(rows_grad * standard)
        column[5:6, :] = lrow_ref[1:2, :] + column_sum(rows_grad)
        column[6:8, :] = frow_ref[2:4, :]
        packed[:, 3 * WIDTH :] = column[...].T
        if layout.pieces:
            shard = 4 * layout.rows
            for index in range(layout.shards):
                low = index * layout.rows
                packed[low : low + 1, FIRST - shard :] = hsum_ref[:, index * shard : (index + 1) * shard]
        packed[:, : 3 * WIDTH] = dot(n1_ref[...], dqkv[...], 0, 0)
        for other in (0, 1):
            @pl.when(core == other)
            def _():
                for third in range(3):
                    low = third * WIDTH + other * GROUP
                    extra = gq_ref[...] if third == 0 else gkv_ref[:, (third - 1) * GROUP : third * GROUP]
                    packed[:, low : low + GROUP] += extra

        layout.store_scattered(
            place_ref, grads, lambda block: packed[pl.ds(pl.multiple_of(block * 16, 16), 16), :].astype(bf16)
        )


def short_backward(
    layout, place, e, k, v, q, kt, da, o, linv, n1, rows, mid, weights, vectors, gq, gkv, lrow, lside, frow, hsum, deps
):
    count = k.shape[0]
    half = pl.BlockSpec((count, GROUP), lambda i, _: (0, i))
    grads = layout.scattered_shapes(FIRST)
    return pl.pallas_call(
        behind(functools.partial(short_backward_kernel, layout), len(deps)),
        grid_spec=pltpu.PrefetchScalarGridSpec(
            num_scalar_prefetch=1,
            grid=(2,),
            in_specs=[ANYWHERE] * len(deps)
            + [
                pl.BlockSpec((count, 4 * count), lambda i, _: (0, i)),
                half,
                half,
                half,
                once((WIDTH, count)),
                once((count, WIDTH)),
                once((WIDTH, count)),
                once((HEADS * 8, count)),
                once((count, WIDTH)),
                once(rows.shape),
                once((count, WIDTH)),
                once((WIDTH, 3 * WIDTH)),
                whole(vectors.shape),
                once((WIDTH, GROUP)),
                once((WIDTH, 2 * GROUP)),
                whole((8, WIDTH)),
                whole((8, GROUP)),
                whole((8, WIDTH)),
                whole((1, FF)),
            ],
            out_specs=[once((count, WIDTH))] + [once(g.shape) for g in grads],
            scratch_shapes=[
                pltpu.VMEM((count, WIDTH), bf16),
                pltpu.VMEM((HEADS * 8, count), f32),
                pltpu.VMEM((4 * count, GROUP), bf16),
                pltpu.VMEM((4 * count, GROUP), bf16),
                pltpu.VMEM((count, 4 * count), bf16),
                pltpu.VMEM((GROUP, count), f32),
                pltpu.VMEM((count, 3 * WIDTH), bf16),
                pltpu.VMEM((WIDTH, FIRST), f32),
                pltpu.VMEM((SIDE, WIDTH), f32),
            ],
        ),
        out_shape=[jax.ShapeDtypeStruct((count, WIDTH), bf16)] + grads,
        compiler_params=pltpu.CompilerParams(**PARAMS),
        cost_estimate=pl.CostEstimate(
            flops=24 * count * count * WIDTH, bytes_accessed=18 << 20, transcendentals=0
        ),
        name="short_backward",
    )(place, *deps, e, k, v, q, kt, da, o, linv, n1, rows, mid, weights, vectors, gq, gkv, lrow, lside, frow, hsum)


def per_device(
    incoming_rows,
    picture_label,
    triple_kernel,
    mixer_kernel,
    widening_kernel,
    narrowing_kernel,
    asker_offset,
    content_offset,
    mixer_offset_vector,
    widening_offset,
    narrowing_offset,
    leading_gain,
    leading_offset,
    second_gain,
    second_offset,
    loss_sensitivity,
):
    layout = Layout(lax.axis_size("band"), lax.axis_size("batch"))
    band = lax.axis_index("band")
    rows = incoming_rows[0]
    ids = picture_label[0]
    upstream = loss_sensitivity[0]
    shard = layout.rows
    place = jnp.stack([band // 2, band % 2, band // 4, (band // 2) % 2, lax.axis_index("batch")]).astype(jnp.int32)

    small = (
        asker_offset,
        content_offset,
        mixer_offset_vector,
        narrowing_offset,
        leading_gain,
        leading_offset,
        second_gain,
        second_offset,
    )
    if layout.pieces:
        first_stack = layout.gather_depth(pack_first(triple_kernel, small, widening_offset))
        first_plane = layout.gather_plane(first_stack)
        near = layout.gather_depth(pack_rows(rows, (first_stack,)), tuple(first_plane[1:]))
        packed = pack_second(mixer_kernel, widening_kernel, narrowing_kernel, (first_stack,))
        first = layout.gather_core(first_plane[:1] + list(tie(first_plane[1:], (packed,))))
    else:
        near = layout.gather_depth(rows[:LONG])
        columns = [v.astype(bf16)[:, None] for v in small]
        columns += [jnp.zeros((shard, SIDE - 12), bf16), widening_offset.astype(bf16).reshape(shard, 4)]
        first = layout.gather_whole(jnp.concatenate([triple_kernel.astype(bf16)] + columns, axis=1))
        second_stack = layout.gather_whole(
            jnp.concatenate([mixer_kernel.astype(bf16), widening_kernel.astype(bf16)], axis=1)
        )[0]
        narrow = layout.gather_whole(narrowing_kernel.astype(bf16))[0]
        narrow = narrow.reshape(WIDTH // 16, 4, 16, WIDTH).transpose(0, 2, 1, 3).reshape(WIDTH, FF)
        second = [jnp.concatenate([second_stack, narrow], axis=1)]
    far = layout.flip(near, 2)

    n1, q_s, k_s, v_s, kt_s, vt_s, wqkv, vectors, hidden_shift = short_qkv(layout, place, rows, first)
    if not layout.pieces:
        hidden_shift = first[0][:, FIRST - 4 :].reshape(1, FF).astype(f32)
        packed = second[0]
    e_s, o_s, linv_s, att_s = short_forward(q_s, k_s, vt_s, ids[LONG:], (near, packed))
    if layout.pieces:
        second_stack = layout.gather_depth(packed, (linv_s,))
        second_plane = layout.gather_plane(second_stack)
    (far,) = tie([far], (second_stack,))
    stacks = (near, layout.flip(near, 1), far, layout.flip(far, 1))
    n1_l, q_l, k_l, vt_l = long_prepare(layout, place, stacks, wqkv, vectors, (second_stack,))

    e_l, o_l, linv_l, att_keep, att_send = long_forward(q_l, k_l, vt_l)
    if layout.pieces:
        second = layout.gather_core(second_plane[:1] + list(tie(second_plane[1:], (att_keep,))))
    layer_out, mid_l, mid_s, da_keep, da_send, da_s, feed_rows, hidden_sum, *second_grads = feed(
        layout, place, rows, ids, upstream, att_keep, layout.flip(att_send, 1), att_s, vectors, hidden_shift, second
    )
    da_other = layout.flip(da_send, 1)
    inputs = (place, e_l, k_l, vt_l, n1_l, q_l, da_keep, da_other, o_l, linv_l, wqkv, vectors)

    pairs = layout.scatter_core(second_grads) if layout.pieces else []
    keep_x, send_x, _, *sums = long_backward(layout, False, *inputs, (), tuple(pairs[1:]))
    moved = (keep_x.astype(f32) + layout.flip(send_x, 1).astype(f32)).astype(bf16)
    totals = layout.scatter_plane(pairs) if layout.pieces else []
    keep, send, gq, _, gkv, long_sums, long_side = long_backward(
        layout, True, *inputs, sums, (moved, *totals[1:])
    )
    dx_totals = layout.add_depth([keep, layout.flip(send, 1), layout.flip(moved, 2)])
    dx_s, *first_grads = short_backward(
        layout, place, e_s, k_s, v_s, q_s, kt_s, da_s, o_s, linv_s, n1, rows, mid_s, wqkv, vectors,
        gq, gkv, long_sums, long_side, feed_rows, hidden_sum, tuple(dx_totals[1:]),
    )
    dx_long = layout.scatter_depth(dx_totals, -1)
    if layout.pieces:
        second_grad = layout.scatter_depth(totals)
        narrow_grad = second_grad[:, WIDTH + FF :].reshape(shard, 4, WIDTH).transpose(1, 0, 2)
        narrow_grad = narrow_grad.reshape(4 * shard, WIDTH)
        first_grad = layout.scatter_depth(layout.scatter_plane(layout.scatter_core(first_grads)))
        hidden_grad = first_grad[0, FIRST - 4 * shard :]
    else:
        packed = second_grads[0][:, WIDTH + FF :].reshape(WIDTH // 16, 16, 4, WIDTH).transpose(0, 2, 1, 3)
        narrow_grad = layout.scatter_whole(packed.reshape(FF, WIDTH))
        second_grad = layout.scatter_whole(second_grads[0][:, : WIDTH + FF])
        first_grad = layout.scatter_whole(first_grads[0])
        hidden_grad = layout.scatter_whole(hidden_sum[0])
    small = first_grad[:, 3 * WIDTH :]

    standard, inverse = standardize(rows[:LONG].astype(f32))
    dx_l = (mid_l + norm_backward(dx_long, standard, inverse, vectors[V_G1][None, :])).astype(bf16)
    input_grad = jnp.concatenate([dx_l, dx_s], axis=0)
    return (
        layer_out[None],
        input_grad[None],
        first_grad[:, : 3 * WIDTH],
        second_grad[:, :WIDTH],
        second_grad[:, WIDTH : WIDTH + FF],
        narrow_grad,
        small[:, 0],
        small[:, 1],
        small[:, 2],
        hidden_grad,
        small[:, 3],
        small[:, 4],
        small[:, 5],
        small[:, 6],
        small[:, 7],
    )


def solution(mesh):
    shards = P(("band", "batch"))
    tokens = P("batch", "band", None)
    kernels = P(("band", "batch"), None)
    in_specs = (
        (tokens, P("batch", "band")) + (kernels,) * 4 + (shards,) * 9 + (tokens,)
    )
    out_specs = (tokens, tokens) + (kernels,) * 4 + (shards,) * 9
    return jax.shard_map(
        per_device, mesh=mesh, in_specs=in_specs, out_specs=out_specs, check_vma=False
    )
```

```python
import functools
import math

import jax
import jax.numpy as jnp
from jax import lax
from jax.experimental import pallas as pl
from jax.experimental.pallas import tpu as pltpu
from jax.sharding import PartitionSpec as P

HEADS = 8
HEAD = 64
LONG = 256
WIDTH = 512
FF = 2048
GROUP = 256
TILE = 512
epsilon = 1e-06
gelu_scale = 0.7978845608028654
f32 = jnp.float32
bf16 = jnp.bfloat16
PARAMS = dict(vmem_limit_bytes=58 << 20)


def dot(left, right, cl=1, cr=0):
    return lax.dot_general(left, right, (((cl,), (cr,)), ((), ())), preferred_element_type=f32)


def standardize(rows):
    center = rows - jnp.mean(rows, axis=1, keepdims=True)
    inverse = lax.rsqrt(jnp.mean(center * center, axis=1, keepdims=True) + epsilon)
    return center * inverse, inverse


def norm_backward(incoming, standard, inverse, scaling):
    scaled = incoming * scaling
    return inverse * (
        scaled
        - jnp.mean(scaled, axis=1, keepdims=True)
        - standard * jnp.mean(scaled * standard, axis=1, keepdims=True)
    )


def column_sum(rows):
    return jnp.sum(rows, axis=0, keepdims=True)


def head_lanes(block, head):
    lane = lax.broadcasted_iota(jnp.int32, block.shape, 1) // HEAD
    return jnp.where(lane == head, block.astype(f32), 0.0).astype(bf16)


V_ASK, V_CONTENT, V_MIXER, V_NARROW, V_G1, V_O1, V_G2, V_O2 = range(8)


def row_of(table_ref, index):
    return table_ref[index : index + 1, :]


def whole(shape):
    return pl.BlockSpec(shape, lambda *_: (0,) * len(shape))


def once(shape):
    return pl.BlockSpec(shape, lambda *_: (0,) * len(shape), pipeline_mode=pl.Buffered(1))


ANYWHERE = pl.BlockSpec(memory_space=pl.ANY)


def behind(kernel, count, prefetch=True):
    skip = 1 if prefetch else 0
    return lambda *refs: kernel(*refs[:skip], *refs[skip + count :])


SIDE = 128
FIRST = 3 * WIDTH + SIDE
SECOND = WIDTH + 2 * FF


class Layout:
    def __init__(self, bands, batches):
        self.bands, self.batches = bands, batches
        self.depth = bands // 4
        self.shards = bands * batches
        self.rows = WIDTH // self.shards
        self.pieces = self.rows % 16 == 0
        self.plane = [(kx, ky) for kx in (0, 1) for ky in range(batches)]

    def shard(self, place, kc, kx, ky, kz, sign):
        z = lax.rem(place[2] + (self.depth + sign * kz), self.depth)
        x = lax.rem(place[3] + kx, 2)
        y = lax.rem(place[4] + (self.batches + sign * ky), self.batches)
        core = lax.rem(place[1] + kc, 2)
        return ((z * 2 + x) * 2 + core) * self.batches + y

    def chip(self, place, kx, kz):
        return lax.rem(place[2] + kz, self.depth) * 2 + lax.rem(place[3] + kx, 2)

    def shift_depth(self, block, k):
        pairs = [(i, ((i // 4 + k) % self.depth) * 4 + i % 4) for i in range(self.bands)]
        return lax.ppermute(block, "band", pairs)

    def flip(self, block, bit):
        return lax.ppermute(block, "band", [(i, i ^ bit) for i in range(self.bands)])

    def shift_plane(self, block, kx, ky):
        n = self.batches
        pairs = [
            (b * n + y, (b ^ (2 * kx)) * n + (y + ky) % n) for b in range(self.bands) for y in range(n)
        ]
        return lax.ppermute(block, ("band", "batch"), pairs)

    def gather_depth(self, block, deps=()):
        return stack_blocks([block] + [self.shift_depth(block, k) for k in range(1, self.depth)], deps)

    def gather_plane(self, stack):
        return [stack if k == (0, 0) else self.shift_plane(stack, *k) for k in self.plane]

    def gather_core(self, plane):
        return plane + [self.flip(part, 1) for part in plane]

    def gather_whole(self, block):
        return [lax.all_gather(block, ("band", "batch"), axis=0, tiled=True)]

    def gathered_specs(self, columns):
        if not self.pieces:
            return [once((WIDTH, columns))]
        return [once((self.depth, self.rows, columns))] * (2 * len(self.plane))

    def each_gathered(self, place, refs, visit):
        if not self.pieces:
            for low in range(0, WIDTH, 16):
                visit(low // 16, refs[0][low : low + 16, :])
            return
        index = 0
        for kc in (0, 1):
            for kx, ky in self.plane:
                for kz in range(self.depth):
                    visit(self.shard(place, kc, kx, ky, kz, -1), refs[index][kz])
                index += 1

    def scattered_shapes(self, columns):
        if not self.pieces:
            return [jax.ShapeDtypeStruct((WIDTH, columns), bf16)]
        shape = (len(self.plane), self.depth, self.rows, columns)
        return [jax.ShapeDtypeStruct(shape, bf16)] * 2

    def store_scattered(self, place, refs, take):
        if not self.pieces:
            for low in range(0, WIDTH, 16):
                refs[0][low : low + 16, :] = take(low // 16)
            return
        for kc in (0, 1):
            for n, (kx, ky) in enumerate(self.plane):
                for kz in range(self.depth):
                    refs[kc][n, kz] = take(self.shard(place, kc, kx, ky, kz, 1))

    def scatter_core(self, parts, deps=()):
        keep, send = parts
        arrived = self.flip(send, 1)
        if deps:
            (arrived,) = tie([arrived], deps)
        return [(keep[n].astype(f32) + arrived[n].astype(f32)).astype(bf16) for n in range(len(self.plane))]

    def scatter_plane(self, pairs):
        arrived = [self.shift_plane(pairs[n], *k) for n, k in enumerate(self.plane) if n]
        return self.add_depth(pairs[:1] + arrived)

    def add_depth(self, stacks):
        totals = []
        for k in range(self.depth):
            total = stacks[0][k].astype(f32)
            for stack in stacks[1:]:
                total = total + stack[k].astype(f32)
            totals.append(total if k == 0 else total.astype(bf16))
        return totals

    def scatter_depth(self, totals, sign=1):
        final = totals[0]
        for k in range(1, self.depth):
            final = final + self.shift_depth(totals[k], (sign * k) % self.depth).astype(f32)
        return final

    def scatter_whole(self, part):
        return lax.psum_scatter(part, ("band", "batch"), scatter_dimension=0, tiled=True).astype(f32)


def tie(values, deps):
    count = len(values)
    return pl.pallas_call(
        lambda *refs: None,
        in_specs=[ANYWHERE] * (count + len(deps)),
        out_specs=[ANYWHERE] * count,
        out_shape=[jax.ShapeDtypeStruct(v.shape, v.dtype) for v in values],
        input_output_aliases={i: i for i in range(count)},
        name="tie",
    )(*values, *deps)


def stack_kernel(*refs):
    for index, ref in enumerate(refs[:-1]):
        refs[-1][index] = ref[...]


def stack_blocks(blocks, deps):
    shape = blocks[0].shape
    return pl.pallas_call(
        behind(stack_kernel, len(deps), False),
        in_specs=[ANYWHERE] * len(deps) + [pl.BlockSpec(memory_space=pltpu.VMEM)] * len(blocks),
        out_shape=jax.ShapeDtypeStruct((len(blocks), *shape), blocks[0].dtype),
        name="stack_blocks",
    )(*deps, *blocks)


def pack_first_kernel(triple_ref, *refs):
    vectors, wide, out_ref, table = refs[:8], *refs[8:]
    shard = triple_ref.shape[0]
    table[...] = jnp.zeros_like(table)
    for index, ref in enumerate(vectors):
        table[index : index + 1, :shard] = ref[...]
    out_ref[:, : 3 * WIDTH] = triple_ref[...].astype(bf16)
    turned = table[...].T[:shard, :]
    across = jnp.pad(wide[...], ((0, shard - 1), (SIDE - 4 * shard, 0)))
    out_ref[:, 3 * WIDTH :] = (turned + across).astype(bf16)


def pack_first(triple, vectors, wide):
    shard = triple.shape[0]
    return pl.pallas_call(
        pack_first_kernel,
        out_shape=jax.ShapeDtypeStruct((shard, FIRST), bf16),
        scratch_shapes=[pltpu.VMEM((SIDE, SIDE), f32)],
        compiler_params=pltpu.CompilerParams(**PARAMS),
        name="pack_first",
    )(triple, *[v[None, :] for v in vectors], wide[None, :])


def pack_rows_kernel(rows_ref, out_ref):
    out_ref[...] = rows_ref[...]


def pack_rows(rows, deps):
    block = pl.BlockSpec((LONG, WIDTH), lambda i: (0, 0))
    return pl.pallas_call(
        behind(pack_rows_kernel, len(deps), False),
        grid=(1,),
        in_specs=[ANYWHERE] * len(deps) + [block],
        out_specs=block,
        out_shape=jax.ShapeDtypeStruct((LONG, WIDTH), bf16),
        name="pack_rows",
    )(*deps, rows)


def pack_second_kernel(mixer_ref, widening_ref, narrowing_ref, out_ref):
    shard = mixer_ref.shape[0]
    out_ref[:, :WIDTH] = mixer_ref[...].astype(bf16)
    out_ref[:, WIDTH : WIDTH + FF] = widening_ref[...].astype(bf16)
    for k in range(4):
        low = WIDTH + FF + k * WIDTH
        out_ref[:, low : low + WIDTH] = narrowing_ref[k * shard : (k + 1) * shard, :].astype(bf16)


def pack_second(mixer, widening, narrowing, deps):
    blocks = [pl.BlockSpec(memory_space=pltpu.VMEM)] * 3
    return pl.pallas_call(
        behind(pack_second_kernel, len(deps), False),
        out_shape=jax.ShapeDtypeStruct((mixer.shape[0], SECOND), bf16),
        in_specs=[ANYWHERE] * len(deps) + blocks,
        compiler_params=pltpu.CompilerParams(**PARAMS),
        name="pack_second",
    )(*deps, mixer, widening, narrowing)


def short_qkv_kernel(layout, place_ref, x_ref, *refs):
    count = len(layout.gathered_specs(FIRST))
    pieces = refs[:count]
    n1_ref, q_ref, k_ref, v_ref, kt_ref, vt_ref, w_ref, vec_ref, hid_ref, side, spread = refs[count:]

    @pl.when(pl.program_id(0) == 0)
    def _():
        def visit(block, rows):
            span = pl.ds(pl.multiple_of(block * 16, 16), 16)
            w_ref[span, :] = rows[:, : 3 * WIDTH]
            side[span, :] = rows[:, 3 * WIDTH :].astype(f32)
            if layout.pieces:
                spread[pl.ds(block, 1), :] = rows[0:1, 3 * WIDTH :].astype(f32)

        layout.each_gathered(place_ref, pieces, visit)
        vec_ref[...] = side[...].T[:16, :]
        if layout.pieces:
            shard = 4 * layout.rows
            for index in range(layout.shards):
                hid_ref[:, index * shard : (index + 1) * shard] = spread[index : index + 1, SIDE - shard :]

    standard, _ = standardize(x_ref[...].astype(f32))
    normed = (standard * row_of(vec_ref, V_G1) + row_of(vec_ref, V_O1)).astype(bf16)
    n1_ref[...] = normed
    projected = dot(normed, w_ref[...])
    q = (projected[:, :WIDTH] + row_of(vec_ref, V_ASK)).astype(bf16)
    q_ref[...] = (q.astype(f32) * (1.0 / math.sqrt(HEAD))).astype(bf16)
    k = projected[:, WIDTH : 2 * WIDTH]
    v = projected[:, 2 * WIDTH :] + row_of(vec_ref, V_CONTENT)
    k_ref[...] = k.astype(bf16)
    v_ref[...] = v.astype(bf16)
    kt_ref[...] = k.T.astype(bf16)
    vt_ref[...] = v.T.astype(bf16)


def short_qkv(layout, place, rows, pieces):
    count = rows.shape[0] - LONG
    block = 256
    row_spec = pl.BlockSpec((block, WIDTH), lambda i, _: (i, 0))
    col_spec = pl.BlockSpec((WIDTH, block), lambda i, _: (0, i))
    flat = jax.ShapeDtypeStruct((count, WIDTH), bf16)
    tall = jax.ShapeDtypeStruct((WIDTH, count), bf16)
    return pl.pallas_call(
        functools.partial(short_qkv_kernel, layout),
        grid_spec=pltpu.PrefetchScalarGridSpec(
            num_scalar_prefetch=1,
            grid=(count // block,),
            in_specs=[pl.BlockSpec((block, WIDTH), lambda i, _: (i + LONG // block, 0))]
            + layout.gathered_specs(FIRST),
            out_specs=[row_spec, row_spec, row_spec, row_spec, col_spec, col_spec]
            + [once((WIDTH, 3 * WIDTH)), whole((16, WIDTH)), whole((1, FF))],
            scratch_shapes=[pltpu.VMEM((WIDTH, SIDE), f32), pltpu.VMEM((max(8, layout.shards), SIDE), f32)],
        ),
        out_shape=[flat, flat, flat, flat, tall, tall]
        + [
            jax.ShapeDtypeStruct((WIDTH, 3 * WIDTH), bf16),
            jax.ShapeDtypeStruct((16, WIDTH), f32),
            jax.ShapeDtypeStruct((1, FF), f32),
        ],
        compiler_params=pltpu.CompilerParams(**PARAMS),
        cost_estimate=pl.CostEstimate(
            flops=2 * count * WIDTH * 3 * WIDTH, bytes_accessed=10 << 20, transcendentals=0
        ),
        name="short_qkv",
    )(place, rows, *pieces)


def short_forward_kernel(
    q_ref, k_ref, vt_ref, idc_ref, idr_ref, e_ref, o_ref, linv_ref, att_ref, s_ref, bias_ref, top_ref
):
    step = pl.program_id(0)
    count = k_ref.shape[0]
    tile = count

    @pl.when(step == 0)
    def _():
        same = idc_ref[LONG:, :] == idr_ref[:, LONG:]
        bias_ref[...] = jnp.where(same, 0.0, -1e30)

    def first(slot):
        masked = head_lanes(q_ref[...], lax.rem(step, 4))
        top = None
        for low in range(0, count, tile):
            s = dot(k_ref[low : low + tile, :], masked, 1, 1) + bias_ref[low : low + tile, :]
            s_ref[slot, low : low + tile, :] = s
            part = jnp.max(s, axis=0, keepdims=True)
            top = part if top is None else jnp.maximum(top, part)
        top_ref[slot] = jnp.broadcast_to(top, (8, count))

    def second(slot):
        head = step - 1
        top = top_ref[slot, 0:1, :]
        mixed = jnp.zeros((HEAD, count), f32)
        total = jnp.zeros((1, count), f32)
        for low in range(0, count, tile):
            e = jnp.exp(s_ref[slot, low : low + tile, :] - top)
            total += column_sum(e)
            low_e = e.astype(bf16)
            e_ref[low : low + tile, :] = low_e
            mixed += dot(vt_ref[pl.ds(pl.multiple_of(head * HEAD, HEAD), HEAD), low : low + tile], low_e)
        linv = 1.0 / total
        linv_ref[...] = jnp.broadcast_to(linv, (8, count))
        o_ref[pl.ds(pl.multiple_of(head * HEAD, HEAD), HEAD), :] = mixed * linv

    last = pl.num_programs(0) - 1

    @pl.when(step == 0)
    def _():
        first(0)

    for parity in (0, 1):
        @pl.when((step > 0) & (step < last) & (lax.rem(step, 2) == parity))
        def _():
            first(parity)
            second(1 - parity)

    @pl.when(step == last)
    def _():
        second((HEADS - 1) % 2)
        for low in range(0, WIDTH, 128):
            att_ref[:, low : low + 128] = o_ref[low : low + 128, :].T.astype(bf16)


def short_forward(q, k, vt, id_column, id_row, deps):
    count = q.shape[0]
    now = lambda s: (0, jnp.minimum(s, HEADS - 1) // 4)
    before = lambda s: (0, jnp.maximum(s - 1, 0))
    return pl.pallas_call(
        behind(short_forward_kernel, len(deps), False),
        grid=(HEADS + 1,),
        in_specs=[ANYWHERE] * len(deps)
        + [
            pl.BlockSpec((count, GROUP), now),
            pl.BlockSpec((count, GROUP), now),
            whole((WIDTH, count)),
            whole(id_column.shape),
            whole(id_row.shape),
        ],
        out_specs=[
            pl.BlockSpec((count, count), before),
            whole((WIDTH, count)),
            pl.BlockSpec((8, count), lambda s: (jnp.maximum(s - 1, 0), 0)),
            whole((count, WIDTH)),
        ],
        out_shape=[
            jax.ShapeDtypeStruct((count, HEADS * count), bf16),
            jax.ShapeDtypeStruct((WIDTH, count), f32),
            jax.ShapeDtypeStruct((HEADS * 8, count), f32),
            jax.ShapeDtypeStruct((count, WIDTH), bf16),
        ],
        scratch_shapes=[
            pltpu.VMEM((2, count, count), f32),
            pltpu.VMEM((count, count), f32),
            pltpu.VMEM((2, 8, count), f32),
        ],
        compiler_params=pltpu.CompilerParams(**PARAMS),
        cost_estimate=pl.CostEstimate(
            flops=12 * count * count * WIDTH, bytes_accessed=12 << 20, transcendentals=HEADS * count * count
        ),
        name="short_forward",
    )(*deps, q, k, vt, id_column, id_row)


CHIPS = 2


def long_prepare_kernel(
    depth, place_ref, own0, other0, own1, other1, w_ref, vec_ref, n1_ref, q_ref, k_ref, vt_ref,
    wk, wv,
):
    step = pl.program_id(0)
    core = place_ref[1]
    near = step < depth
    lanes = lambda base: pl.ds(pl.multiple_of(base + core * GROUP, GROUP), GROUP)

    @pl.when(step == 0)
    def _():
        for other in (0, 1):
            @pl.when(core == other)
            def _():
                wk[...] = w_ref[:, WIDTH + other * GROUP : WIDTH + (other + 1) * GROUP]
                wv[...] = w_ref[:, 2 * WIDTH + other * GROUP : 2 * WIDTH + (other + 1) * GROUP]

    chips = own0.shape[0]
    rows = jnp.concatenate(
        [jnp.where(near, a[chip], b[chip]) for chip in range(chips) for a, b in ((own0, own1), (other0, other1))],
        axis=0,
    )
    standard, _ = standardize(rows.astype(f32))
    normed = (standard * row_of(vec_ref, V_G1) + row_of(vec_ref, V_O1)).astype(bf16)
    n1_ref[...] = normed
    k = dot(normed, wk[...])
    v = dot(normed, wv[...]) + vec_ref[V_CONTENT : V_CONTENT + 1, lanes(0)]
    k_ref[...] = k.astype(bf16)
    vt_ref[...] = v.astype(bf16).T

    @pl.when(step == 0)
    def _():
        q = (dot(normed[:TILE, :], w_ref[:, lanes(0)]) + vec_ref[V_ASK : V_ASK + 1, lanes(0)]).astype(bf16)
        q_ref[...] = (q.astype(f32) * (1.0 / math.sqrt(HEAD))).astype(bf16)


def long_prepare(layout, place, stacks, weights, vectors, deps):
    depth = layout.depth
    total = 2 * depth * TILE
    steps = depth // CHIPS
    tile = CHIPS * TILE
    row_spec = pl.BlockSpec((tile, GROUP), lambda i, _: (i, 0))
    col_spec = pl.BlockSpec((GROUP, tile), lambda i, _: (0, i))
    near = pl.BlockSpec((CHIPS, LONG, WIDTH), lambda i, _: (jnp.minimum(i, steps - 1), 0, 0))
    far = pl.BlockSpec((CHIPS, LONG, WIDTH), lambda i, _: (jnp.maximum(i - steps, 0), 0, 0))
    flat = jax.ShapeDtypeStruct((total, GROUP), bf16)
    tall = jax.ShapeDtypeStruct((GROUP, total), bf16)
    return pl.pallas_call(
        behind(functools.partial(long_prepare_kernel, depth // CHIPS), len(deps)),
        grid_spec=pltpu.PrefetchScalarGridSpec(
            num_scalar_prefetch=1,
            grid=(2 * steps,),
            in_specs=[ANYWHERE] * len(deps)
            + [near, near, far, far, whole((WIDTH, 3 * WIDTH)), whole(vectors.shape)],
            out_specs=[
                pl.BlockSpec((tile, WIDTH), lambda i, _: (i, 0)),
                whole((TILE, GROUP)),
                row_spec,
                col_spec,
            ],
            scratch_shapes=[pltpu.VMEM((WIDTH, GROUP), bf16)] * 2,
        ),
        out_shape=[
            jax.ShapeDtypeStruct((total, WIDTH), bf16),
            jax.ShapeDtypeStruct((TILE, GROUP), bf16),
            flat,
            tall,
        ],
        compiler_params=pltpu.CompilerParams(**PARAMS),
        cost_estimate=pl.CostEstimate(
            flops=4 * total * WIDTH * GROUP, bytes_accessed=18 << 20, transcendentals=0
        ),
        name="long_prepare",
    )(place, *deps, *stacks, weights, vectors)


CHUNK = 256
BACK = 2 * TILE
PARTS = TILE // CHUNK
LOCAL_HEADS = GROUP // HEAD
STEPS = LOCAL_HEADS * PARTS


def long_forward_kernel(
    q_ref, k_ref, vt_ref, e_ref, o_ref, linv_ref, keep_ref, send_ref, s_ref, top_ref
):
    step = pl.program_id(0)
    total = k_ref.shape[0]
    tile = min(total, 4096)
    last = pl.num_programs(0) - 1

    def masked_queries():
        rows = pl.ds(pl.multiple_of(lax.rem(step, PARTS) * CHUNK, CHUNK), CHUNK)
        return head_lanes(q_ref[rows, :], step // PARTS)

    def first_tile(slot, low, masked, top):
        s = dot(k_ref[pl.ds(low, tile), :], masked, 1, 1)
        s_ref[slot, pl.ds(low, tile), :] = s
        return jnp.maximum(top, jnp.max(s.reshape(tile // 8, 8, CHUNK), axis=0))

    def second_tile(slot, low, top, head, carry):
        summed, mixed = carry
        e = jnp.exp(s_ref[slot, pl.ds(low, tile), :] - top)
        summed = summed + jnp.sum(e.reshape(tile // 8, 8, CHUNK), axis=0)
        low_e = e.astype(bf16)
        e_ref[pl.ds(low, tile), :] = low_e
        values = vt_ref[pl.ds(pl.multiple_of(head * HEAD, HEAD), HEAD), pl.ds(low, tile)]
        return summed, mixed + dot(values, low_e)

    start_top = jnp.full((8, CHUNK), -1e30, f32)
    start_sum = (jnp.zeros((8, CHUNK), f32), jnp.zeros((HEAD, CHUNK), f32))

    def finish(head, part, carry):
        summed, mixed = carry
        linv = 1.0 / column_sum(summed)
        linv_ref[...] = jnp.broadcast_to(linv, (8, CHUNK))
        o_ref[part, pl.ds(pl.multiple_of(head * HEAD, HEAD), HEAD), :] = mixed * linv

    def place(turn):
        return pl.multiple_of(turn * tile, tile)

    @pl.when(step == 0)
    def _():
        masked = masked_queries()
        top_ref[0] = lax.fori_loop(
            0, total // tile, lambda t, top: first_tile(0, place(t), masked, top), start_top
        )

    for parity in (0, 1):
        @pl.when((step > 0) & (step < last) & (lax.rem(step, 2) == parity))
        def _():
            masked = masked_queries()
            before = step - 1
            head = before // PARTS
            top_row = jnp.max(top_ref[1 - parity], axis=0, keepdims=True)

            def body(turn, carry):
                top, kept = carry
                low = place(turn)
                top = first_tile(parity, low, masked, top)
                kept = second_tile(1 - parity, low, top_row, head, kept)
                return top, kept

            top, kept = lax.fori_loop(0, total // tile, body, (start_top, start_sum))
            top_ref[parity] = top
            finish(head, lax.rem(before, PARTS), kept)

    @pl.when(step == last)
    def _():
        slot = (STEPS - 1) % 2
        top_row = jnp.max(top_ref[slot], axis=0, keepdims=True)
        head = LOCAL_HEADS - 1
        kept = lax.fori_loop(
            0,
            total // tile,
            lambda t, carry: second_tile(slot, place(t), top_row, head, carry),
            start_sum,
        )
        finish(head, PARTS - 1, kept)
        keep_ref[...] = o_ref[0].T.astype(bf16)
        send_ref[...] = o_ref[1].T.astype(bf16)


def long_forward(q, k, vt):
    total = k.shape[0]
    before = lambda s: jnp.maximum(s - 1, 0)
    half = jax.ShapeDtypeStruct((CHUNK, GROUP), bf16)
    return pl.pallas_call(
        long_forward_kernel,
        grid=(STEPS + 1,),
        in_specs=[once((TILE, GROUP)), once((total, GROUP)), once((GROUP, total))],
        out_specs=[
            pl.BlockSpec((total, CHUNK), lambda s: (0, before(s))),
            whole((PARTS, GROUP, CHUNK)),
            pl.BlockSpec((8, CHUNK), lambda s: (before(s), 0)),
            whole((CHUNK, GROUP)),
            whole((CHUNK, GROUP)),
        ],
        scratch_shapes=[pltpu.VMEM((2, total, CHUNK), f32), pltpu.VMEM((2, 8, CHUNK), f32)],
        out_shape=[
            jax.ShapeDtypeStruct((total, STEPS * CHUNK), bf16),
            jax.ShapeDtypeStruct((PARTS, GROUP, CHUNK), f32),
            jax.ShapeDtypeStruct((STEPS * 8, CHUNK), f32),
            half,
            half,
        ],
        compiler_params=pltpu.CompilerParams(**PARAMS),
        cost_estimate=pl.CostEstimate(
            flops=16 * TILE * total * GROUP, bytes_accessed=24 << 20, transcendentals=4 * TILE * total
        ),
        name="long_forward",
    )(q, k, vt)


def feed_kernel(layout, place_ref, x_ref, ids_ref, g_ref, mine_ref, other_ref, short_ref, vec_ref, hid_ref, *refs):
    count = len(layout.gathered_specs(SECOND))
    pieces, refs = refs[:count], refs[count:]
    out_ref, midl_ref, mids_ref, keep_ref, send_ref, das_ref, row_ref, hsum_ref = refs[:8]
    grads = refs[8:-8]
    wp_ref, we_ref, wr_ref, gp_ref, ge_ref, gr_ref, act_ref, dh_ref = refs[-8:]
    swapped = place_ref[1] == 1

    def visit(block, rows):
        span = pl.ds(pl.multiple_of(block * 16, 16), 16)
        wp_ref[span, :] = rows[:, :WIDTH]
        we_ref[span, :] = rows[:, WIDTH : WIDTH + FF]
        for k in range(4):
            low = WIDTH + FF + k * WIDTH
            wr_ref[pl.ds(pl.multiple_of(block * 64 + 16 * k, 16), 16), :] = rows[:, low : low + WIDTH]

    layout.each_gathered(place_ref, pieces, visit)

    x = x_ref[...].astype(f32)
    live = (ids_ref[...] >= 0).astype(f32)
    upstream = g_ref[...].astype(f32)
    mine, other = mine_ref[...], other_ref[...]
    long = jnp.concatenate([jnp.where(swapped, other, mine), jnp.where(swapped, mine, other)], axis=1)
    attended = jnp.concatenate([long, short_ref[...]], axis=0)
    branch = dot(attended, wp_ref[...]) + row_of(vec_ref, V_MIXER)
    middle = x + live * branch
    standard, inverse = standardize(middle)
    gain = row_of(vec_ref, V_G2)
    normed = (standard * gain + row_of(vec_ref, V_O2)).astype(bf16)
    branch_low = (live * upstream).astype(bf16)

    part = 256

    def products(low):
        return (
            dot(normed, we_ref[:, low : low + part]) + hid_ref[:, low : low + part],
            dot(branch_low, wr_ref[low : low + part, :], 1, 1),
        )

    following = products(0)
    for low in range(0, FF, part):
        hidden, into = following
        if low + part < FF:
            following = products(low + part)
        square = hidden * hidden
        tangent = jnp.tanh(hidden * (gelu_scale + (gelu_scale * 0.044715) * square))
        half = 0.5 + 0.5 * tangent
        active = (hidden * half).astype(bf16)
        slope = half + (0.5 * hidden) * (1.0 - tangent * tangent) * (
            gelu_scale + (gelu_scale * 3.0 * 0.044715) * square
        )
        hidden_low = (into * slope).astype(bf16)
        hsum_ref[:, low : low + part] = column_sum(hidden_low.astype(f32))
        act_ref[:, low : low + part] = active
        dh_ref[:, low : low + part] = hidden_low
        gr_ref[low : low + part, :] = dot(active, branch_low, 0, 0).astype(bf16)
        ge_ref[:, low : low + part] = dot(normed, hidden_low, 0, 0).astype(bf16)

    branch_two = dot(act_ref[...], wr_ref[...]) + row_of(vec_ref, V_NARROW)
    out_ref[...] = (middle + live * branch_two).astype(bf16)
    normed_grad = dot(dh_ref[...], we_ref[...], 1, 1)
    middle_grad = upstream + norm_backward(normed_grad, standard, inverse, gain)
    midl_ref[...] = middle_grad[:LONG, :]
    mids_ref[...] = middle_grad[LONG:, :]
    attn_low = (live * middle_grad).astype(bf16)
    attended_grad = dot(attn_low, wp_ref[...], 1, 1).astype(bf16)
    das_ref[...] = attended_grad[LONG:, :]
    left, right = attended_grad[:LONG, :GROUP], attended_grad[:LONG, GROUP:]
    keep_ref[...] = jnp.where(swapped, right, left)
    send_ref[...] = jnp.where(swapped, left, right)
    gp_ref[...] = dot(attended, attn_low, 0, 0).astype(bf16)
    row_ref[...] = jnp.zeros_like(row_ref)
    row_ref[0:1, :] = column_sum(attn_low.astype(f32))
    row_ref[1:2, :] = column_sum(branch_low.astype(f32))
    row_ref[2:3, :] = column_sum(normed_grad * standard)
    row_ref[3:4, :] = column_sum(normed_grad)

    def take(block):
        span = pl.ds(pl.multiple_of(block * 16, 16), 16)
        parts = [gp_ref[span, :], ge_ref[span, :]] + [
            gr_ref[pl.ds(pl.multiple_of(block * 64 + 16 * k, 16), 16), :] for k in range(4)
        ]
        return jnp.concatenate(parts, axis=1)

    layout.store_scattered(place_ref, grads, take)


def feed(layout, place, rows, id_column, upstream, mine, other, short, vectors, hidden_shift, pieces):
    count = rows.shape[0]
    grads = layout.scattered_shapes(SECOND)
    operands = [rows, id_column, upstream, mine, other, short, vectors, hidden_shift]
    shapes = [
        jax.ShapeDtypeStruct((count, WIDTH), bf16),
        jax.ShapeDtypeStruct((LONG, WIDTH), f32),
        jax.ShapeDtypeStruct((count - LONG, WIDTH), f32),
        jax.ShapeDtypeStruct((LONG, GROUP), bf16),
        jax.ShapeDtypeStruct((LONG, GROUP), bf16),
        jax.ShapeDtypeStruct((count - LONG, WIDTH), bf16),
        jax.ShapeDtypeStruct((8, WIDTH), f32),
        jax.ShapeDtypeStruct((1, FF), f32),
    ] + grads
    return pl.pallas_call(
        functools.partial(feed_kernel, layout),
        grid_spec=pltpu.PrefetchScalarGridSpec(
            num_scalar_prefetch=1,
            grid=(1,),
            in_specs=[once(x.shape) for x in operands] + layout.gathered_specs(SECOND),
            out_specs=[once(x.shape) for x in shapes],
            scratch_shapes=[
                pltpu.VMEM((WIDTH, WIDTH), bf16),
                pltpu.VMEM((WIDTH, FF), bf16),
                pltpu.VMEM((FF, WIDTH), bf16),
                pltpu.VMEM((WIDTH, WIDTH), bf16),
                pltpu.VMEM((WIDTH, FF), bf16),
                pltpu.VMEM((FF, WIDTH), bf16),
                pltpu.VMEM((count, FF), bf16),
                pltpu.VMEM((count, FF), bf16),
            ],
        ),
        out_shape=shapes,
        compiler_params=pltpu.CompilerParams(**PARAMS),
        cost_estimate=pl.CostEstimate(
            flops=6 * count * WIDTH * (WIDTH + 2 * FF), bytes_accessed=18 << 20, transcendentals=count * FF
        ),
        name="feed",
    )(place, *operands, *pieces)


def long_backward_kernel(
    place_ref, e_ref, k_ref, vt_ref, n1_ref, q_ref, mine_ref, other_ref, o_ref, linv_ref, w_ref, vec_ref,
    keep0, send0, keep1, send1, gq_ref, gkv_ref, row_ref, side_ref,
    dq_acc, qblk, dblk, delta, ds_ref, wq, wkv,
):
    step = pl.program_id(0)
    core = place_ref[1]

    @pl.when(step == 0)
    def _():
        lanes = lambda base: pl.ds(pl.multiple_of(base + core * GROUP, GROUP), GROUP)
        wq[...] = w_ref[:, lanes(0)]
        wkv[:, :GROUP] = w_ref[:, lanes(WIDTH)]
        wkv[:, GROUP:] = w_ref[:, lanes(2 * WIDTH)]
        for ref in (dq_acc, gkv_ref, row_ref, side_ref):
            ref[...] = jnp.zeros_like(ref)
        for part in range(PARTS):
            rows = slice(part * CHUNK, (part + 1) * CHUNK)
            turned = (mine_ref, other_ref)[part][...].astype(f32).T
            product = turned * o_ref[part]
            pieces = []
            for head in range(LOCAL_HEADS):
                index = head * PARTS + part
                span = slice(head * HEAD, (head + 1) * HEAD)
                linv = linv_ref[8 * index : 8 * index + 1, :]
                delta[8 * index : 8 * index + 8, :] = jnp.broadcast_to(
                    column_sum(product[span, :]) * linv, (8, CHUNK)
                )
                pieces.append(turned[span, :] * linv)
            scaled = jnp.concatenate(pieces, axis=0).T
            for head in range(LOCAL_HEADS):
                index = head * PARTS + part
                span = slice(index * CHUNK, (index + 1) * CHUNK)
                dblk[span, :] = head_lanes(scaled, head)
                qblk[span, :] = head_lanes(q_ref[rows, :], head)

    def span_of(index):
        return slice(index * CHUNK, (index + 1) * CHUNK)

    v = vt_ref[...].T
    kt = k_ref[...].T
    slopes = dot(v, dblk[span_of(0), :], 1, 1)
    for index in range(STEPS):
        head, part = index // PARTS, index % PARTS
        span = span_of(index)
        following = dot(v, dblk[span_of(index + 1), :], 1, 1) if index + 1 < STEPS else None
        ds = (
            e_ref[:, span].astype(f32) * (slopes - delta[8 * index : 8 * index + 1, :])
        ).astype(bf16)
        ds_ref[:, span] = ds
        own = slice(head * HEAD, (head + 1) * HEAD)
        dq_acc[part, own, :] += dot(kt[own, :], ds)
        slopes = following

    value_grad = dot(e_ref[...], dblk[...]).astype(bf16)
    key_grad = dot(ds_ref[...], qblk[...]).astype(bf16)
    both = jnp.concatenate([key_grad, value_grad], axis=1)
    normed = n1_ref[...]
    through = dot(both, wkv[...], 1, 1)
    gkv_ref[...] += dot(normed, both, 0, 0)
    side_ref[1:2, :] += column_sum(value_grad.astype(f32))

    def put(entire, keep_ref, send_ref):
        low = entire.astype(bf16)
        for chip in range(BACK // TILE):
            base = chip * TILE
            keep_ref[chip] = low[base : base + LONG, :]
            send_ref[chip] = low[base + LONG : base + TILE, :]
        shifts = column_sum(entire)
        scales = column_sum(entire * normed.astype(f32)) - shifts * row_of(vec_ref, V_O1)
        row_ref[0:1, :] += scales / row_of(vec_ref, V_G1)
        row_ref[1:2, :] += shifts

    last = pl.num_programs(0) - 1
    half = pl.num_programs(0) // 2

    @pl.when(step < half)
    def _():
        put(through, keep1, send1)

    @pl.when((step >= half) & (step < last))
    def _():
        put(through, keep0, send0)

    @pl.when(step == last)
    def _():
        query_grad = jnp.concatenate(
            [dq_acc[part].T for part in range(PARTS)], axis=0
        ) * (1.0 / math.sqrt(HEAD))
        low = query_grad.astype(bf16)
        own = through[:TILE, :] + dot(low, wq[...], 1, 1)
        put(jnp.concatenate([own, through[TILE:, :]], axis=0), keep0, send0)
        gq_ref[...] = dot(normed[:TILE, :], low, 0, 0)
        side_ref[0:1, :] += column_sum(low.astype(f32))


def long_backward(layout, place, e, k, vt, normed, q, mine, other, o, linv, weights, vectors, deps):
    tiles = layout.depth * TILE // BACK
    near = lambda i: lax.rem(jnp.maximum(i - tiles, 0) + 1, tiles)
    far = lambda i: jnp.minimum(i, tiles - 1)
    turn = lambda i: jnp.where(i < tiles, tiles + i, near(i))
    chips = BACK // TILE
    out = jax.ShapeDtypeStruct((layout.depth, LONG, WIDTH), bf16)
    near_spec = pl.BlockSpec((chips, LONG, WIDTH), lambda i, p: (near(i), 0, 0))
    far_spec = pl.BlockSpec((chips, LONG, WIDTH), lambda i, p: (far(i), 0, 0))
    sums = [
        jax.ShapeDtypeStruct((WIDTH, GROUP), f32),
        jax.ShapeDtypeStruct((WIDTH, 2 * GROUP), f32),
        jax.ShapeDtypeStruct((8, WIDTH), f32),
        jax.ShapeDtypeStruct((8, GROUP), f32),
    ]
    return pl.pallas_call(
        behind(long_backward_kernel, len(deps)),
        grid_spec=pltpu.PrefetchScalarGridSpec(
            num_scalar_prefetch=1,
            grid=(2 * tiles,),
            in_specs=[ANYWHERE] * len(deps)
            + [
                pl.BlockSpec((BACK, STEPS * CHUNK), lambda i, p: (turn(i), 0)),
                pl.BlockSpec((BACK, GROUP), lambda i, p: (turn(i), 0)),
                pl.BlockSpec((GROUP, BACK), lambda i, p: (0, turn(i))),
                pl.BlockSpec((BACK, WIDTH), lambda i, p: (turn(i), 0)),
                whole((TILE, GROUP)),
                whole((CHUNK, GROUP)),
                whole((CHUNK, GROUP)),
                whole((PARTS, GROUP, CHUNK)),
                whole((STEPS * 8, CHUNK)),
                once((WIDTH, 3 * WIDTH)),
                whole(vectors.shape),
            ],
            out_specs=[near_spec, near_spec, far_spec, far_spec] + [whole(x.shape) for x in sums],
            scratch_shapes=[
                pltpu.VMEM((PARTS, GROUP, CHUNK), f32),
                pltpu.VMEM((STEPS * CHUNK, GROUP), bf16),
                pltpu.VMEM((STEPS * CHUNK, GROUP), bf16),
                pltpu.VMEM((STEPS * 8, CHUNK), f32),
                pltpu.VMEM((BACK, STEPS * CHUNK), bf16),
                pltpu.VMEM((WIDTH, GROUP), bf16),
                pltpu.VMEM((WIDTH, 2 * GROUP), bf16),
            ],
        ),
        out_shape=[out] * 4 + sums,
        compiler_params=pltpu.CompilerParams(**PARAMS),
        cost_estimate=pl.CostEstimate(
            flops=40 * TILE * k.shape[0] * GROUP, bytes_accessed=32 << 20, transcendentals=0
        ),
        name="long_backward",
    )(place, *deps, e, k, vt, normed, q, mine, other, o, linv, weights, vectors)


def short_backward_kernel(
    layout, place_ref, e_ref, k_ref, v_ref, q_ref, kt_ref, da_ref, o_ref, linv_ref, n1_ref, x_ref, mid_ref, w_ref,
    vec_ref, gq_ref, gkv_ref, lrow_ref, lside_ref, frow_ref, hsum_ref,
    dx_ref, *refs,
):
    grads = refs[:-9]
    scaled, delta, dblk, qblk, ds_ref, dqt, dqkv, packed, column = refs[-9:]
    step = pl.program_id(0)
    count = k_ref.shape[0]

    @pl.when(step == 0)
    def _():
        for low in range(0, WIDTH, GROUP):
            turned = da_ref[:, low : low + GROUP].astype(f32).T
            product = turned * o_ref[low : low + GROUP, :]
            pieces = []
            for head in range(4):
                span = slice(head * HEAD, (head + 1) * HEAD)
                index = low // HEAD + head
                linv = linv_ref[8 * index : 8 * index + 1, :]
                delta[8 * index : 8 * index + 8, :] = jnp.broadcast_to(
                    column_sum(product[span, :]) * linv, (8, count)
                )
                pieces.append(turned[span, :] * linv)
            scaled[:, low : low + GROUP] = jnp.concatenate(pieces, axis=0).T.astype(bf16)

    def group(side):
        low = side * GROUP
        for head in range(4):
            index = side * 4 + head
            span = slice(head * count, (head + 1) * count)
            own = slice(head * HEAD, (head + 1) * HEAD)
            dblk[span, :] = head_lanes(scaled[:, low : low + GROUP], head)
            qblk[span, :] = head_lanes(q_ref[...], head)
            slopes = dot(v_ref[...], dblk[span, :], 1, 1)
            ds = (
                e_ref[:, span].astype(f32) * (slopes - delta[8 * index : 8 * index + 1, :])
            ).astype(bf16)
            ds_ref[:, span] = ds
            dqt[own, :] = dot(kt_ref[low + head * HEAD : low + (head + 1) * HEAD, :], ds)
        value_grad = dot(e_ref[...], dblk[...])
        key_grad = dot(ds_ref[...], qblk[...])
        query_grad = dqt[...].T * (1.0 / math.sqrt(HEAD))
        dqkv[:, low : low + GROUP] = query_grad.astype(bf16)
        dqkv[:, WIDTH + low : WIDTH + low + GROUP] = key_grad.astype(bf16)
        dqkv[:, 2 * WIDTH + low : 2 * WIDTH + low + GROUP] = value_grad.astype(bf16)

    for side in (0, 1):
        pl.when(step == side)(functools.partial(group, side))

    @pl.when(step == 1)
    def _():
        rows_grad = dot(dqkv[...], w_ref[...], 1, 1)
        standard, inverse = standardize(x_ref[LONG:, :].astype(f32))
        through = norm_backward(rows_grad, standard, inverse, row_of(vec_ref, V_G1))
        dx_ref[...] = (mid_ref[...] + through).astype(bf16)
        core = place_ref[1]
        column[...] = jnp.zeros_like(column)
        column[0:1, :] = column_sum(dqkv[:, :WIDTH].astype(f32))
        column[1:2, :] = column_sum(dqkv[:, 2 * WIDTH :].astype(f32))
        for other in (0, 1):
            @pl.when(core == other)
            def _():
                span = slice(other * GROUP, (other + 1) * GROUP)
                column[0:2, span] += lside_ref[0:2, :]
        column[2:4, :] = frow_ref[0:2, :]
        column[4:5, :] = lrow_ref[0:1, :] + column_sum(rows_grad * standard)
        column[5:6, :] = lrow_ref[1:2, :] + column_sum(rows_grad)
        column[6:8, :] = frow_ref[2:4, :]
        packed[:, 3 * WIDTH :] = column[...].T
        if layout.pieces:
            shard = 4 * layout.rows
            for index in range(layout.shards):
                low = index * layout.rows
                packed[low : low + 1, FIRST - shard :] = hsum_ref[:, index * shard : (index + 1) * shard]
        packed[:, : 3 * WIDTH] = dot(n1_ref[...], dqkv[...], 0, 0)
        for other in (0, 1):
            @pl.when(core == other)
            def _():
                for third in range(3):
                    low = third * WIDTH + other * GROUP
                    extra = gq_ref[...] if third == 0 else gkv_ref[:, (third - 1) * GROUP : third * GROUP]
                    packed[:, low : low + GROUP] += extra

        layout.store_scattered(
            place_ref, grads, lambda block: packed[pl.ds(pl.multiple_of(block * 16, 16), 16), :].astype(bf16)
        )


def short_backward(
    layout, place, e, k, v, q, kt, da, o, linv, n1, rows, mid, weights, vectors, gq, gkv, lrow, lside, frow, hsum, deps
):
    count = k.shape[0]
    half = pl.BlockSpec((count, GROUP), lambda i, _: (0, i))
    grads = layout.scattered_shapes(FIRST)
    return pl.pallas_call(
        behind(functools.partial(short_backward_kernel, layout), len(deps)),
        grid_spec=pltpu.PrefetchScalarGridSpec(
            num_scalar_prefetch=1,
            grid=(2,),
            in_specs=[ANYWHERE] * len(deps)
            + [
                pl.BlockSpec((count, 4 * count), lambda i, _: (0, i)),
                half,
                half,
                half,
                once((WIDTH, count)),
                once((count, WIDTH)),
                once((WIDTH, count)),
                once((HEADS * 8, count)),
                once((count, WIDTH)),
                once(rows.shape),
                once((count, WIDTH)),
                once((WIDTH, 3 * WIDTH)),
                whole(vectors.shape),
                once((WIDTH, GROUP)),
                once((WIDTH, 2 * GROUP)),
                whole((8, WIDTH)),
                whole((8, GROUP)),
                whole((8, WIDTH)),
                whole((1, FF)),
            ],
            out_specs=[once((count, WIDTH))] + [once(g.shape) for g in grads],
            scratch_shapes=[
                pltpu.VMEM((count, WIDTH), bf16),
                pltpu.VMEM((HEADS * 8, count), f32),
                pltpu.VMEM((4 * count, GROUP), bf16),
                pltpu.VMEM((4 * count, GROUP), bf16),
                pltpu.VMEM((count, 4 * count), bf16),
                pltpu.VMEM((GROUP, count), f32),
                pltpu.VMEM((count, 3 * WIDTH), bf16),
                pltpu.VMEM((WIDTH, FIRST), f32),
                pltpu.VMEM((SIDE, WIDTH), f32),
            ],
        ),
        out_shape=[jax.ShapeDtypeStruct((count, WIDTH), bf16)] + grads,
        compiler_params=pltpu.CompilerParams(**PARAMS),
        cost_estimate=pl.CostEstimate(
            flops=24 * count * count * WIDTH, bytes_accessed=18 << 20, transcendentals=0
        ),
        name="short_backward",
    )(place, *deps, e, k, v, q, kt, da, o, linv, n1, rows, mid, weights, vectors, gq, gkv, lrow, lside, frow, hsum)


def per_device(
    incoming_rows,
    picture_label,
    triple_kernel,
    mixer_kernel,
    widening_kernel,
    narrowing_kernel,
    asker_offset,
    content_offset,
    mixer_offset_vector,
    widening_offset,
    narrowing_offset,
    leading_gain,
    leading_offset,
    second_gain,
    second_offset,
    loss_sensitivity,
):
    layout = Layout(lax.axis_size("band"), lax.axis_size("batch"))
    band = lax.axis_index("band")
    rows = incoming_rows[0]
    id_column = picture_label[0][:, None]
    upstream = loss_sensitivity[0]
    shard = layout.rows
    place = jnp.stack([band // 2, band % 2, band // 4, (band // 2) % 2, lax.axis_index("batch")]).astype(jnp.int32)

    small = (
        asker_offset,
        content_offset,
        mixer_offset_vector,
        narrowing_offset,
        leading_gain,
        leading_offset,
        second_gain,
        second_offset,
    )
    if layout.pieces:
        first_stack = layout.gather_depth(
            pack_first(triple_kernel, small, widening_offset), (place, id_column)
        )
        first_plane = layout.gather_plane(first_stack)
        near = layout.gather_depth(pack_rows(rows, (first_stack,)), tuple(first_plane[1:]))
        first = layout.gather_core(first_plane)
    else:
        near = layout.gather_depth(rows[:LONG])
        columns = [v.astype(bf16)[:, None] for v in small]
        columns += [jnp.zeros((shard, SIDE - 12), bf16), widening_offset.astype(bf16).reshape(shard, 4)]
        first = layout.gather_whole(jnp.concatenate([triple_kernel.astype(bf16)] + columns, axis=1))
        second_stack = layout.gather_whole(
            jnp.concatenate([mixer_kernel.astype(bf16), widening_kernel.astype(bf16)], axis=1)
        )[0]
        narrow = layout.gather_whole(narrowing_kernel.astype(bf16))[0]
        narrow = narrow.reshape(WIDTH // 16, 4, 16, WIDTH).transpose(0, 2, 1, 3).reshape(WIDTH, FF)
        second = [jnp.concatenate([second_stack, narrow], axis=1)]
    far = layout.flip(near, 2)
    n1, q_s, k_s, v_s, kt_s, vt_s, wqkv, vectors, hidden_shift = short_qkv(layout, place, rows, first)
    if layout.pieces:
        packed = pack_second(mixer_kernel, widening_kernel, narrowing_kernel, (n1,))
    else:
        hidden_shift = first[0][:, FIRST - 4 :].reshape(1, FF).astype(f32)
        packed = second[0]
    e_s, o_s, linv_s, att_s = short_forward(q_s, k_s, vt_s, id_column, picture_label, (near, packed))
    if layout.pieces:
        second_stack = layout.gather_depth(packed, (linv_s,))
        second_plane = layout.gather_plane(second_stack)
    (far,) = tie([far], (second_stack,))
    stacks = (near, layout.flip(near, 1), far, layout.flip(far, 1))
    n1_l, q_l, k_l, vt_l = long_prepare(layout, place, stacks, wqkv, vectors, (second_stack,))

    e_l, o_l, linv_l, att_keep, att_send = long_forward(q_l, k_l, vt_l)
    if layout.pieces:
        second = layout.gather_core(second_plane[:1] + list(tie(second_plane[1:], (att_keep,))))
    layer_out, mid_l, mid_s, da_keep, da_send, da_s, feed_rows, hidden_sum, *second_grads = feed(
        layout, place, rows, id_column, upstream, att_keep, layout.flip(att_send, 1), att_s, vectors, hidden_shift, second
    )
    da_other = layout.flip(da_send, 1)
    inputs = (place, e_l, k_l, vt_l, n1_l, q_l, da_keep, da_other, o_l, linv_l, wqkv, vectors)

    pairs = layout.scatter_core(second_grads) if layout.pieces else []
    keep0, send0, keep1, send1, gq, gkv, long_sums, long_side = long_backward(layout, *inputs, tuple(pairs[1:]))
    moved = (keep1.astype(f32) + layout.flip(send1, 1).astype(f32)).astype(bf16)
    totals = layout.scatter_plane(pairs) if layout.pieces else []
    dx_s, *first_grads = short_backward(
        layout, place, e_s, k_s, v_s, q_s, kt_s, da_s, o_s, linv_s, n1, rows, mid_s, wqkv, vectors,
        gq, gkv, long_sums, long_side, feed_rows, hidden_sum, (moved, *totals[1:]),
    )
    dx_totals = layout.add_depth([keep0, layout.flip(send0, 1), layout.flip(moved, 2)])
    dx_long = layout.scatter_depth(dx_totals, -1)
    if layout.pieces:
        second_grad = layout.scatter_depth(totals)
        narrow_grad = second_grad[:, WIDTH + FF :].reshape(shard, 4, WIDTH).transpose(1, 0, 2)
        narrow_grad = narrow_grad.reshape(4 * shard, WIDTH)
        first_grad = layout.scatter_depth(
            layout.scatter_plane(layout.scatter_core(first_grads, tuple(dx_totals[1:])))
        )
        hidden_grad = first_grad[0, FIRST - 4 * shard :]
    else:
        packed = second_grads[0][:, WIDTH + FF :].reshape(WIDTH // 16, 16, 4, WIDTH).transpose(0, 2, 1, 3)
        narrow_grad = layout.scatter_whole(packed.reshape(FF, WIDTH))
        second_grad = layout.scatter_whole(second_grads[0][:, : WIDTH + FF])
        first_grad = layout.scatter_whole(first_grads[0])
        hidden_grad = layout.scatter_whole(hidden_sum[0])
    small = first_grad[:, 3 * WIDTH :]

    standard, inverse = standardize(rows[:LONG].astype(f32))
    dx_l = (mid_l + norm_backward(dx_long, standard, inverse, vectors[V_G1][None, :])).astype(bf16)
    input_grad = jnp.concatenate([dx_l, dx_s], axis=0)
    return (
        layer_out[None],
        input_grad[None],
        first_grad[:, : 3 * WIDTH],
        second_grad[:, :WIDTH],
        second_grad[:, WIDTH : WIDTH + FF],
        narrow_grad,
        small[:, 0],
        small[:, 1],
        small[:, 2],
        hidden_grad,
        small[:, 3],
        small[:, 4],
        small[:, 5],
        small[:, 6],
        small[:, 7],
    )


def solution(mesh):
    shards = P(("band", "batch"))
    tokens = P("batch", "band", None)
    kernels = P(("band", "batch"), None)
    in_specs = (
        (tokens, P("batch", "band")) + (kernels,) * 4 + (shards,) * 9 + (tokens,)
    )
    out_specs = (tokens, tokens) + (kernels,) * 4 + (shards,) * 9
    return jax.shard_map(
        per_device, mesh=mesh, in_specs=in_specs, out_specs=out_specs, check_vma=False
    )
```
